128 devices in a mesh: cx: 16 (over z, x), cy: 8 (over y, core).
Axes of the slice: x: 4, y: 4, z: 4, core: 2. Of those that a mesh axis runs over, the one named last changes fastest.
Arguments:
- cell_pos: float32 [64, 32, 3, 1024], P('cx', 'cy'), may hold values from -6 to 6
- cell_drag: float32 [64, 32], P('cx', 'cy'), may hold values from 0.2 to 2
- cell_near: int32 [64, 32, 2], P('cx', 'cy'), may hold values from 0 to 2047, as said below
- analysis: bfloat16 [1024, 1024], replicated, may hold values from -0.1875 to 0.1875
- stiffness: float32 [1024], replicated, may hold values from 0.1 to 1
- synthesis: bfloat16 [1024, 1024], replicated, may hold values from -0.1875 to 0.1875
- wall_pos: float32 [1024, 3, 256], P(('cx', 'cy')), may hold values from -9 to 9
- wall_normal: float32 [1024, 3, 256], P(('cx', 'cy')), may hold values from -6 to 6
- wall_weight: float32 [1024, 256], P(('cx', 'cy')), may hold values from 0.02 to 0.2
- density: float32 [1024, 3, 256], P(('cx', 'cy')), may hold values from -6 to 6
- patch_near: int32 [1024, 4], P(('cx', 'cy')), may hold values from 0 to 1023, as said below
- cell_to_patch: int32 [1024, 2], P(('cx', 'cy')), may hold values from 0 to 2047, as said below
Outputs:
- moved_cells: float32 [64, 32, 3, 1024], P('cx', 'cy')
- density_next: float32 [1024, 3, 256], P(('cx', 'cy'))
The draws below stay inside these ranges and needn't reach their ends.
Inputs may be any that keep to these rules, and one draw needn't show every extreme that they name: `cell_near`: each entry is the row-major index (row times 32 plus column) of a cell whose grid row and column differ from the listing cell's by at most 3 each, cyclically, and never the listing cell itself. `cell_to_patch`: for the patches of block b (patches b * 8 to b * 8 + 7), with b = i * 8 + j, each entry is the row-major index of a cell whose row lies within 3 of the rows i * 4 to i * 4 + 3 and whose column lies within 3 of the columns j * 4 to j * 4 + 3, cyclically. `patch_near`: each entry is a patch of the listing patch's block of 8 or of the two blocks beside it, cyclically, and never the listing patch itself.
All inputs are finite; a program needn't handle non-finite values.
Results may differ from the reference program's by a relative error of at most 0.0041.
Values sent between devices are 32-bit elements; how exact they have to be, the bound alone decides.
No kernel may reach another device: no remote copies, remote signals or barrier semaphores. Data moves between devices by JAX's collectives and lax.ppermute only.
A program may use at most 64 MiB of HBM per device.

```python
import math
import jax
import jax.numpy as jnp
from jax import lax

P_SIZE = 1024
Q = 1024
PP = 256
HALO = 3
NEAR = 2
CPNEAR = 2
PNEAR = 4
CXD = 4
CYD = 4
PATCH_DEV = 8
NXC = 64
NYC = 32
PATCHES = 1024
N_CY = 8


def draw_cell_near(key, part):
    window = 2 * HALO + 1
    centre = HALO * window + HALO
    picked = jax.random.randint(key, (NXC, NYC, NEAR), 0, window * window - 1)
    picked = picked + (picked >= centre).astype(jnp.int32)
    shift_row = picked // window - HALO
    shift_col = picked % window - HALO
    grid_row = jnp.arange(NXC, dtype=jnp.int32)[:, None, None]
    grid_col = jnp.arange(NYC, dtype=jnp.int32)[None, :, None]
    return ((grid_row + shift_row) % NXC * NYC + (grid_col + shift_col) % NYC).astype(jnp.int32)


def draw_cell_to_patch(key, part):
    first_key, second_key = jax.random.split(jax.random.fold_in(key, 7))
    patch_ids = jnp.arange(PATCHES, dtype=jnp.int32)[:, None]
    block = patch_ids // PATCH_DEV
    block_row = block // N_CY
    block_col = block % N_CY
    offset_row = jax.random.randint(first_key, (PATCHES, CPNEAR), 0, CXD + 2 * HALO)
    offset_col = jax.random.randint(second_key, (PATCHES, CPNEAR), 0, CYD + 2 * HALO)
    grid_row = (block_row * CXD - HALO + offset_row) % NXC
    grid_col = (block_col * CYD - HALO + offset_col) % NYC
    return (grid_row * NYC + grid_col).astype(jnp.int32)


def draw_patch_near(key, part):
    picked = jax.random.randint(jax.random.fold_in(key, 11), (PATCHES, PNEAR), 0, 3 * PATCH_DEV - 1)
    patch_ids = jnp.arange(PATCHES, dtype=jnp.int32)[:, None]
    itself = patch_ids % PATCH_DEV + PATCH_DEV
    picked = picked + (picked >= itself).astype(jnp.int32)
    base = patch_ids // PATCH_DEV * PATCH_DEV - PATCH_DEV
    return ((base + picked) % PATCHES).astype(jnp.int32)


def steps_of(rng, dims, shards, least, top_value):
    gain, own = 1.0, jax.random.fold_in(rng, 6)
    for position, shards_of in shards:
        heights = jnp.exp(jax.random.uniform(jax.random.fold_in(own, position), (shards_of,), jnp.float32, least / len(shards), top_value / len(shards)))
        gain = gain * jnp.repeat(heights, dims[position] // shards_of).reshape([-1 if axis == position else 1 for axis in range(len(dims))])
    return gain


def gaussian(rng, extent, deviation, most, shards=(), held_as=jnp.bfloat16):
    result = deviation * jax.random.normal(rng, extent, jnp.float32)
    if shards:
        result = result * steps_of(rng, extent, shards, -0.22, 0.18)
    return jnp.clip(result, -most, most).astype(held_as)


def setup_inputs(seed: int = 0) -> dict:
    splits = jax.random.split(jax.random.key(seed), 13)
    cell_pos = gaussian(splits[0], (NXC, NYC, 3, P_SIZE), 1.0, 6.0, ((0, 16), (1, 8)), jnp.float32)
    cell_drag = jnp.clip(jnp.exp(math.log(2.0) - 2.3025851 * jax.random.uniform(splits[1], (NXC, NYC), jnp.float32) ** steps_of(splits[1], (NXC, NYC), ((0, 16), (1, 8)), -0.2, 0.2)), 0.2, 2.0)
    cell_near = draw_cell_near(jax.random.fold_in(splits[12], 71), 0)
    analysis = gaussian(splits[3], (P_SIZE, Q), P_SIZE ** -0.5, 0.1875)
    stiffness = jnp.clip(jnp.exp(jax.random.uniform(splits[4], (Q,), jnp.float32, math.log(0.1), math.log(1.0))), 0.1, 1.0)
    synthesis = gaussian(splits[5], (Q, P_SIZE), Q ** -0.5, 0.1875)
    wall_pos = gaussian(splits[6], (PATCHES, 3, PP), 1.5, 9.0, ((0, 128),), jnp.float32)
    wall_normal = gaussian(splits[7], (PATCHES, 3, PP), 1.0, 6.0, ((0, 128),), jnp.float32)
    wall_weight = jnp.clip(jnp.exp(math.log(0.2) - 2.3025851 * jax.random.uniform(splits[8], (PATCHES, PP), jnp.float32) ** steps_of(splits[8], (PATCHES, PP), ((0, 128),), -0.2, 0.2)), 0.02, 0.2)
    density = gaussian(splits[9], (PATCHES, 3, PP), 1.0, 6.0, ((0, 128),), jnp.float32)
    patch_near = draw_patch_near(jax.random.fold_in(splits[12], 71), 0)
    cell_to_patch = draw_cell_to_patch(jax.random.fold_in(splits[12], 71), 0)
    return dict(cell_pos=cell_pos, cell_drag=cell_drag, cell_near=cell_near, analysis=analysis, stiffness=stiffness, synthesis=synthesis, wall_pos=wall_pos, wall_normal=wall_normal, wall_weight=wall_weight, density=density, patch_near=patch_near, cell_to_patch=cell_to_patch)


soften = 0.25
stokes_scale = 1.0 / (8.0 * math.pi)
layer_scale = 3.0 / (4.0 * math.pi)

def membrane(positions, analysis, stiffness, synthesis):
    points = positions.shape[-1]
    centred = positions - lax.optimization_barrier(jnp.mean(positions, axis=-1, keepdims=True))
    flat = centred.reshape(-1, points).astype(jnp.bfloat16)
    coeff = jnp.dot(flat, analysis, preferred_element_type=jnp.float32)
    scaled = (coeff * stiffness[None, :]).astype(jnp.bfloat16)
    force = -jnp.dot(scaled, synthesis, preferred_element_type=jnp.float32)
    return force.reshape(positions.shape)

def stokeslet(targets, sources, forces):
    delta_x = targets[0][:, None] - sources[0][None, :]
    delta_y = targets[1][:, None] - sources[1][None, :]
    delta_z = targets[2][:, None] - sources[2][None, :]
    square = delta_x * delta_x + delta_y * delta_y + delta_z * delta_z + soften
    factor = lax.rsqrt(square) / square
    along = delta_x * forces[0][None, :] + delta_y * forces[1][None, :] + delta_z * forces[2][None, :]
    direct = (square + soften) * factor
    tangent = along * factor
    out_x = lax.optimization_barrier(jnp.sum(direct * forces[0][None, :] + tangent * delta_x, axis=1))
    out_y = lax.optimization_barrier(jnp.sum(direct * forces[1][None, :] + tangent * delta_y, axis=1))
    out_z = lax.optimization_barrier(jnp.sum(direct * forces[2][None, :] + tangent * delta_z, axis=1))
    return stokes_scale * jnp.stack([out_x, out_y, out_z])

def double_layer(targets, sources, normals, weights, values):
    delta_x = targets[0][:, None] - sources[0][None, :]
    delta_y = targets[1][:, None] - sources[1][None, :]
    delta_z = targets[2][:, None] - sources[2][None, :]
    square = delta_x * delta_x + delta_y * delta_y + delta_z * delta_z + soften
    factor = lax.rsqrt(square) / (square * square)
    along_q = delta_x * values[0][None, :] + delta_y * values[1][None, :] + delta_z * values[2][None, :]
    along_n = delta_x * normals[0][None, :] + delta_y * normals[1][None, :] + delta_z * normals[2][None, :]
    scalar = -layer_scale * weights[None, :] * along_q * along_n * factor
    return jnp.stack([lax.optimization_barrier(jnp.sum(scalar * delta_x, axis=1)), lax.optimization_barrier(jnp.sum(scalar * delta_y, axis=1)), lax.optimization_barrier(jnp.sum(scalar * delta_z, axis=1))])

def spread(picked):
    count = picked.shape[0]
    return jnp.swapaxes(picked, 0, 1).reshape(3, count * picked.shape[-1])

def reference(cell_pos, cell_drag, cell_near, analysis, stiffness, synthesis, wall_pos, wall_normal, wall_weight, density, patch_near, cell_to_patch):
    forces = membrane(cell_pos, analysis, stiffness, synthesis)
    flat_pos = cell_pos.reshape(NXC * NYC, 3, P_SIZE)
    flat_force = forces.reshape(NXC * NYC, 3, P_SIZE)

    def one_cell(target, neighbours):
        return stokeslet(target, spread(flat_pos[neighbours]), spread(flat_force[neighbours]))

    def one_row(pieces):
        return jax.vmap(one_cell)(pieces[0], pieces[1])
    near = lax.map(one_row, (cell_pos, cell_near))
    velocity = cell_drag[:, :, None, None] * forces + near
    speed = jnp.sqrt(lax.optimization_barrier(jnp.sum(velocity * velocity, axis=2)))
    step = 1.0 / (jnp.max(speed) + 1e-06)
    moved_cells = cell_pos + step * velocity

    def wall_from_cells(pieces):
        target, listed = pieces
        return stokeslet(target, spread(flat_pos[listed]), spread(flat_force[listed]))
    wall_velocity = lax.map(wall_from_cells, (wall_pos, cell_to_patch))
    patch_ids = jnp.arange(PATCHES, dtype=jnp.int32)

    def layer_patch(pieces):
        own, target, listed = pieces
        chosen = jnp.concatenate([own[None], listed]).astype(jnp.int32)
        return double_layer(target, spread(wall_pos[chosen]), spread(wall_normal[chosen]), wall_weight[chosen].reshape(-1), spread(density[chosen]))
    layer = lax.map(layer_patch, (patch_ids, wall_pos, patch_near))
    density_next = 2.0 * layer + 2.0 * wall_velocity
    return (moved_cells, density_next)
```

```python
import math

import jax
import jax.numpy as jnp
from jax import lax
from jax.experimental import pallas as pl
from jax.experimental.pallas import tpu as pltpu
from jax.sharding import PartitionSpec as P

HALO = 3
AXES = ("cx", "cy")
SOFT = 0.25
STOKES_SCALE = 1.0 / (8.0 * math.pi)
LAYER_SCALE = 3.0 / (4.0 * math.pi)
F32 = jnp.float32
BF16 = jnp.bfloat16
LANES = 128

GROUPS = ((0, 0), (0, 1), (1, 0), (0, 2), (2, 0), (1, 1), (1, 2), (2, 1))
STOKES_ROWS = 24
LAYER_ROWS = 32


def parts(v):
    high = v.astype(BF16)
    rest = v - high.astype(F32)
    middle = rest.astype(BF16)
    low = (rest - middle.astype(F32)).astype(BF16)
    return high, middle, low


def target_rows(raw):
    split = [p.astype(F32) for p in parts(raw)]
    return jnp.concatenate([split[a] for a, _ in GROUPS], axis=0).astype(BF16)


def source_rows(raw):
    split = [p.astype(F32) for p in parts(raw)]
    stacked = jnp.concatenate([split[b] for _, b in GROUPS], axis=0)
    return jnp.transpose(stacked).astype(BF16)


def feature_rows(raw):
    return jnp.concatenate(parts(raw), axis=0)


def put_rows(ref, first, count, stride, value):
    for tile in range(ref.shape[0]):
        ref[tile, pl.ds(first, count, stride=stride), :] = value[
            :, tile * LANES : (tile + 1) * LANES
        ]


def get_rows(ref, first, count):
    return jnp.concatenate(
        [ref[tile, pl.ds(first, count), :] for tile in range(ref.shape[0])], axis=1
    )


def stokes_raw(ref, first, pos, force):
    square = pos[0] * pos[0] + pos[1] * pos[1] + pos[2] * pos[2]
    along = pos[0] * force[0] + pos[1] * force[1] + pos[2] * force[2]
    rows = [-2.0 * pos[0], -2.0 * pos[1], -2.0 * pos[2], square, jnp.ones_like(square)]
    rows += [jnp.zeros_like(square)] * 3
    rows += [force[0], force[1], force[2]]
    rows += [pos[j] * force[i] for j in range(3) for i in range(3)]
    rows += [square * force[i] + pos[i] * along for i in range(3)]
    rows += [jnp.zeros_like(square)]
    for k, row in enumerate(rows):
        put_rows(ref, first + k, 8, STOKES_ROWS, row)


def target_raw(ref, first, pos):
    square = pos[0] * pos[0] + pos[1] * pos[1] + pos[2] * pos[2] + SOFT
    rows = [pos[0], pos[1], pos[2], jnp.ones_like(square), square]
    rows += [jnp.zeros_like(square)] * 3
    for k, row in enumerate(rows):
        put_rows(ref, first + k, 8, 8, row)


def stokes_moments(raw_ref, slots, target):
    total = None
    for slot in slots:
        base = pl.multiple_of(slot * STOKES_ROWS, 8)
        left = source_rows(get_rows(raw_ref, base, 8))
        square = jnp.dot(left, target, preferred_element_type=F32)
        root = lax.rsqrt(jnp.maximum(square, SOFT))
        factor = (root * root * root).astype(BF16)
        features = feature_rows(get_rows(raw_ref, base + 8, 16))
        part = jnp.dot(features, factor, preferred_element_type=F32)
        total = part if total is None else total + part
    return total[0:16] + total[16:32] + total[32:48]


def stokes_finish(pos, moments):
    m0 = moments[0:3]
    m1 = [[moments[3 + 3 * j + i] for i in range(3)] for j in range(3)]
    m2 = moments[12:15]
    square = pos[0] * pos[0] + pos[1] * pos[1] + pos[2] * pos[2] + 2.0 * SOFT
    along = pos[0] * m0[0] + pos[1] * m0[1] + pos[2] * m0[2]
    along = along - (m1[0][0] + m1[1][1] + m1[2][2])
    out = []
    for i in range(3):
        cross = sum(pos[j] * (2.0 * m1[j][i] + m1[i][j]) for j in range(3))
        out.append(square * m0[i] + m2[i] + pos[i] * along - cross)
    return out


def near_kernel(
    near_ref,
    wall_ref,
    middle_ref,
    left_ref,
    right_ref,
    drag_ref,
    analysis_ref,
    stiffness_ref,
    synthesis_ref,
    velocity_ref,
    top_ref,
    wall_raw_ref,
    ext_ref,
    pos_ref,
    raw_ref,
    target_ref,
    moment_ref,
):
    rows = middle_ref.shape[0] - 2 * HALO
    cols = middle_ref.shape[2]
    points = middle_ref.shape[3]
    own = rows * cols
    near = near_ref.shape[0]
    wall = wall_ref.shape[0]
    slots = own + near + wall
    ext_ref[:, :, 0:HALO, :] = left_ref[...]
    ext_ref[:, :, HALO : HALO + cols, :] = middle_ref[...]
    ext_ref[:, :, HALO + cols :, :] = right_ref[...]
    for r in range(rows):
        for d in range(3):
            pos_ref[d, r * cols : (r + 1) * cols, :] = middle_ref[HALO + r, d]
    for i in range(near + wall):
        code = near_ref[i] if i < near else wall_ref[i - near]
        row = code // 16
        col = code % 16
        for d in range(3):
            pos_ref[d, own + i : own + i + 1, :] = ext_ref[row, d, pl.ds(col, 1), :]
    everything = [pos_ref[d] for d in range(3)]
    centred = [v - jnp.sum(v, axis=1, keepdims=True) * (1.0 / points) for v in everything]
    flat = jnp.concatenate(centred, axis=0).astype(BF16)
    coeff = jnp.dot(flat, analysis_ref[...], preferred_element_type=F32)
    scaled = (coeff * stiffness_ref[...]).astype(BF16)
    force = -jnp.dot(scaled, synthesis_ref[...], preferred_element_type=F32)
    forces = [force[d * slots : (d + 1) * slots] for d in range(3)]
    for g in range((near + wall) // 8):
        a = own + 8 * g
        into, base = (raw_ref, 8 * g) if 8 * g < near else (wall_raw_ref, 8 * g - near)
        stokes_raw(
            into,
            base * STOKES_ROWS,
            [v[a : a + 8] for v in everything],
            [v[a : a + 8] for v in forces],
        )
    for g in range(own // 8):
        target_raw(target_ref, 64 * g, [v[8 * g : 8 * g + 8] for v in everything])

    def cell(c, carry):
        target = target_rows(get_rows(target_ref, pl.multiple_of(c * 8, 8), 8))
        per = near // own
        moments = stokes_moments(raw_ref, [c * per + k for k in range(per)], target)
        put_rows(moment_ref, c, 16, own, moments)
        return carry

    lax.fori_loop(0, own, cell, 0)
    moments = [get_rows(moment_ref, k * own, own) for k in range(15)]
    own_pos = [v[0:own] for v in everything]
    sums = stokes_finish(own_pos, moments)
    speed = jnp.zeros_like(sums[0])
    for d in range(3):
        velocity = drag_ref[...] * forces[d][0:own] + STOKES_SCALE * sums[d]
        speed = speed + velocity * velocity
        for r in range(rows):
            velocity_ref[r, d] = velocity[r * cols : (r + 1) * cols]
    top_ref[...] = jnp.sqrt(jnp.max(speed, axis=(0, 1), keepdims=True))


def near_part(near_code, wall_code, middle, left, right, drag, analysis, stiffness, synthesis):
    rows, _, cols, points = middle.shape
    rows = rows - 2 * HALO
    own = rows * cols
    near, wall = near_code.shape[0], wall_code.shape[0]
    slots = own + near + wall
    tiles = points // LANES
    in_vmem = pl.BlockSpec(memory_space=pltpu.VMEM)
    in_smem = pl.BlockSpec(memory_space=pltpu.SMEM)
    pairs = own * points * (near // own) * points
    return pl.pallas_call(
        near_kernel,
        in_specs=[in_smem] * 2 + [in_vmem] * 7,
        out_specs=[in_vmem] * 3,
        out_shape=[
            jax.ShapeDtypeStruct((rows, 3, cols, points), F32),
            jax.ShapeDtypeStruct((1, 1), F32),
            jax.ShapeDtypeStruct((tiles, wall * STOKES_ROWS, LANES), F32),
        ],
        scratch_shapes=[
            pltpu.VMEM((rows + 2 * HALO, 3, cols + 2 * HALO, points), F32),
            pltpu.VMEM((3, slots, points), F32),
            pltpu.VMEM((tiles, near * STOKES_ROWS, LANES), F32),
            pltpu.VMEM((tiles, own * 8, LANES), F32),
            pltpu.VMEM((tiles, own * 16, LANES), F32),
        ],
        compiler_params=pltpu.CompilerParams(vmem_limit_bytes=50 * 2**20),
        cost_estimate=pl.CostEstimate(
            flops=1000 * pairs, bytes_accessed=8 * 2**20, transcendentals=pairs
        ),
        name="near",
    )(near_code, wall_code, middle, left, right, drag, analysis, stiffness, synthesis)


def wall_kernel(raw_ref, pos_ref, layer_ref, out_ref, target_ref, moment_ref):
    patches = pos_ref.shape[1]
    per = raw_ref.shape[1] // STOKES_ROWS // patches
    pos = [pos_ref[d] for d in range(3)]
    target_raw(target_ref, 0, pos)

    def patch(p, carry):
        target = target_rows(get_rows(target_ref, pl.multiple_of(p * 8, 8), 8))
        moments = stokes_moments(raw_ref, [p * per + k for k in range(per)], target)
        put_rows(moment_ref, p, 16, patches, moments)
        return carry

    lax.fori_loop(0, patches, patch, 0)
    sums = stokes_finish(pos, [get_rows(moment_ref, k * patches, patches) for k in range(15)])
    for d in range(3):
        out_ref[d] = layer_ref[d] + (2.0 * STOKES_SCALE) * sums[d]


def wall_part(raw, pos, layer):
    _, patches, points = pos.shape
    tiles = points // LANES
    in_vmem = pl.BlockSpec(memory_space=pltpu.VMEM)
    pairs = raw.shape[0] * raw.shape[1] // STOKES_ROWS * LANES * points
    return pl.pallas_call(
        wall_kernel,
        in_specs=[in_vmem] * 3,
        out_specs=in_vmem,
        out_shape=jax.ShapeDtypeStruct(pos.shape, F32),
        scratch_shapes=[
            pltpu.VMEM((tiles, patches * 8, LANES), F32),
            pltpu.VMEM((tiles, patches * 16, LANES), F32),
        ],
        compiler_params=pltpu.CompilerParams(vmem_limit_bytes=24 * 2**20),
        cost_estimate=pl.CostEstimate(
            flops=1000 * pairs, bytes_accessed=2 * 2**20, transcendentals=pairs
        ),
        name="wall",
    )(raw, pos, layer)


def layer_kernel(listed_ref, own_ref, before_ref, after_ref, out_ref, raw_ref, target_ref, left_ref, feature_ref, moment_ref):
    patches = own_ref.shape[1]
    for block, ref in enumerate((before_ref, own_ref, after_ref)):
        y = [ref[d] for d in range(3)]
        normal = [ref[3 + d] for d in range(3)]
        weight = ref[9]
        value = [ref[6 + d] * weight for d in range(3)]
        square = y[0] * y[0] + y[1] * y[1] + y[2] * y[2]
        one, zero = jnp.ones_like(square), jnp.zeros_like(square)
        rows = [-2.0 * y[0], -2.0 * y[1], -2.0 * y[2], square, one, zero, zero, zero]
        for v in (value, normal):
            rows += [v[0], v[1], v[2], -(y[0] * v[0] + y[1] * v[1] + y[2] * v[2])]
            rows += [zero] * 4
        rows += [y[0], y[1], y[2], one, zero, zero, zero, zero]
        for k, row in enumerate(rows):
            put_rows(raw_ref, block * patches * LAYER_ROWS + k, patches, LAYER_ROWS, row)
    pos = [own_ref[d] for d in range(3)]
    target_raw(target_ref, 0, pos)

    def prepare(s, carry):
        raw = get_rows(raw_ref, pl.multiple_of(s * LAYER_ROWS, 8), LAYER_ROWS)
        for k in range(3):
            left_ref[s, k] = source_rows(raw[8 * k : 8 * k + 8])
        split = [p.astype(F32) for p in parts(raw[24:32])]
        split.append(jnp.zeros_like(split[0]))
        feature_ref[s] = jnp.concatenate(split, axis=0).astype(BF16)
        return carry

    lax.fori_loop(0, 3 * patches, prepare, 0)
    listed = listed_ref.shape[1]

    def patch(p, carry):
        target = target_rows(get_rows(target_ref, pl.multiple_of(p * 8, 8), 8))
        total = None
        for k in range(listed + 1):
            s = patches + p if k == 0 else listed_ref[p, k - 1]
            square = jnp.dot(left_ref[s, 0], target, preferred_element_type=F32)
            along_q = jnp.dot(left_ref[s, 1], target, preferred_element_type=F32)
            along_n = jnp.dot(left_ref[s, 2], target, preferred_element_type=F32)
            root = lax.rsqrt(jnp.maximum(square, SOFT))
            double = root * root
            scalar = (along_q * along_n * (double * double * root)).astype(BF16)
            part = jnp.dot(feature_ref[s], scalar, preferred_element_type=F32)
            total = part if total is None else total + part
        moments = total[0:8] + total[8:16] + total[16:24]
        put_rows(moment_ref, p, 8, patches, moments)
        return carry

    lax.fori_loop(0, patches, patch, 0)
    moments = [get_rows(moment_ref, k * patches, patches) for k in range(4)]
    for d in range(3):
        out_ref[d] = (-2.0 * LAYER_SCALE) * (pos[d] * moments[3] - moments[d])


def layer_part(listed, own, before, after):
    _, patches, points = own.shape
    tiles = points // LANES
    in_vmem = pl.BlockSpec(memory_space=pltpu.VMEM)
    pairs = patches * points * (listed.shape[1] + 1) * points
    return pl.pallas_call(
        layer_kernel,
        in_specs=[pl.BlockSpec(memory_space=pltpu.SMEM)] + [in_vmem] * 3,
        out_specs=in_vmem,
        out_shape=jax.ShapeDtypeStruct((3, patches, points), F32),
        scratch_shapes=[
            pltpu.VMEM((tiles, 3 * patches * LAYER_ROWS, LANES), F32),
            pltpu.VMEM((tiles, patches * 8, LANES), F32),
            pltpu.VMEM((3 * patches, 3, points, 64), BF16),
            pltpu.VMEM((3 * patches, 32, points), BF16),
            pltpu.VMEM((tiles, patches * 8, LANES), F32),
        ],
        compiler_params=pltpu.CompilerParams(vmem_limit_bytes=24 * 2**20),
        cost_estimate=pl.CostEstimate(
            flops=1000 * pairs, bytes_accessed=2**20, transcendentals=pairs
        ),
        name="layer",
    )(listed, own, before, after)


def neighbours(low, high, axis):
    size = lax.axis_size(axis)
    up = [(i, (i + 1) % size) for i in range(size)]
    down = [(b, a) for a, b in up]
    return lax.ppermute(high, axis, up), lax.ppermute(low, axis, down)


def body(
    cell_pos,
    cell_drag,
    cell_near,
    analysis,
    stiffness,
    synthesis,
    wall_pos,
    wall_normal,
    wall_weight,
    density,
    patch_near,
    cell_to_patch,
):
    rows, cols = cell_pos.shape[:2]
    all_rows = rows * lax.axis_size("cx")
    all_cols = cols * lax.axis_size("cy")
    first_row = lax.axis_index("cx") * rows
    first_col = lax.axis_index("cy") * cols

    pos = jnp.transpose(cell_pos, (0, 2, 1, 3))
    walls = [jnp.transpose(v, (1, 0, 2)) for v in (wall_pos, wall_normal, density)]
    packed = jnp.concatenate(walls + [wall_weight[None]], axis=0)

    below, above = neighbours(pos[:HALO], pos[rows - HALO :], "cx")
    wall_below, wall_above = neighbours(packed, packed, AXES)
    middle = jnp.concatenate([below, pos, above], axis=0)
    left, right = neighbours(middle[:, :, :HALO], middle[:, :, cols - HALO :], "cy")

    patches = wall_pos.shape[0]
    all_patches = patches * lax.axis_size(AXES)
    start = lax.axis_index(AXES) * patches
    listed = (patch_near - start + patches) % all_patches
    layer = layer_part(listed, packed, wall_below, wall_above)

    def code(cell):
        row = (cell // all_cols - first_row + HALO) % all_rows
        col = (cell % all_cols - first_col + HALO) % all_cols
        return (row * 16 + col).reshape(-1)

    velocity, top, wall_raw = near_part(
        code(cell_near),
        code(cell_to_patch),
        middle,
        left,
        right,
        cell_drag.reshape(-1, 1),
        analysis,
        stiffness[None, :],
        synthesis,
    )
    top = lax.pmax(top, AXES)
    density_next = wall_part(wall_raw, walls[0], layer)
    step = 1.0 / (top[0, 0] + 1e-06)
    moved = pos + step * velocity
    return jnp.transpose(moved, (0, 2, 1, 3)), jnp.transpose(density_next, (1, 0, 2))


def solution(mesh):
    patch = P(AXES, None, None)
    return jax.shard_map(
        body,
        mesh=mesh,
        in_specs=(
            P("cx", "cy", None, None),
            P("cx", "cy"),
            P("cx", "cy", None),
            P(),
            P(),
            P(),
            patch,
            patch,
            P(AXES, None),
            patch,
            P(AXES, None),
            P(AXES, None),
        ),
        out_specs=(P("cx", "cy", None, None), patch),
        check_vma=False,
    )
```

```python
import functools
import math

import jax
import jax.numpy as jnp
from jax import lax
from jax.experimental import pallas as pl
from jax.experimental.pallas import tpu as pltpu
from jax.sharding import PartitionSpec as P

HALO = 3
AXES = ("cx", "cy")
SOFT = 0.25
STOKES_SCALE = 1.0 / (8.0 * math.pi)
LAYER_SCALE = 3.0 / (4.0 * math.pi)
F32 = jnp.float32
BF16 = jnp.bfloat16
LANES = 128

GROUPS = ((0, 0), (0, 1), (1, 0), (0, 2), (2, 0), (1, 1), (1, 2), (2, 1))
STOKES_ROWS = 24
LAYER_ROWS = 32


def parts(v):
    high = v.astype(BF16)
    rest = v - high.astype(F32)
    middle = rest.astype(BF16)
    low = (rest - middle.astype(F32)).astype(BF16)
    return high, middle, low


def target_rows(raw):
    split = [p.astype(F32) for p in parts(raw)]
    return jnp.concatenate([split[a] for a, _ in GROUPS], axis=0).astype(BF16)


def source_rows(raw):
    split = [p.astype(F32) for p in parts(raw)]
    return jnp.concatenate([split[b] for _, b in GROUPS], axis=0).astype(BF16)


def product(left, right):
    return lax.dot_general(left, right, (((0,), (0,)), ((), ())), preferred_element_type=F32)


def feature_rows(raw):
    return jnp.concatenate(parts(raw), axis=0)


def put_rows(ref, first, count, stride, value):
    for tile in range(ref.shape[0]):
        ref[tile, pl.ds(first, count, stride=stride), :] = value[
            :, tile * LANES : (tile + 1) * LANES
        ]


def get_rows(ref, first, count):
    return jnp.concatenate(
        [ref[tile, pl.ds(first, count), :] for tile in range(ref.shape[0])], axis=1
    )


def stokes_raw(ref, first, pos, force):
    square = pos[0] * pos[0] + pos[1] * pos[1] + pos[2] * pos[2]
    along = pos[0] * force[0] + pos[1] * force[1] + pos[2] * force[2]
    rows = [-2.0 * pos[0], -2.0 * pos[1], -2.0 * pos[2], square, jnp.ones_like(square)]
    rows += [jnp.zeros_like(square)] * 3
    rows += [force[0], force[1], force[2]]
    rows += [pos[j] * force[i] for j in range(3) for i in range(3)]
    rows += [square * force[i] + pos[i] * along for i in range(3)]
    rows += [jnp.zeros_like(square)]
    for k, row in enumerate(rows):
        put_rows(ref, first + k, 8, STOKES_ROWS, row)


def target_raw(ref, first, pos):
    square = pos[0] * pos[0] + pos[1] * pos[1] + pos[2] * pos[2] + SOFT
    rows = [pos[0], pos[1], pos[2], jnp.ones_like(square), square]
    rows += [jnp.zeros_like(square)] * 3
    for k, row in enumerate(rows):
        put_rows(ref, first + k, 8, 8, row)


def stokes_moments(raw_ref, slots, target):
    total = None
    for slot in slots:
        base = pl.multiple_of(slot * STOKES_ROWS, 8)
        left = source_rows(get_rows(raw_ref, base, 8))
        square = product(left, target)
        root = lax.rsqrt(jnp.maximum(square, SOFT))
        factor = (root * root * root).astype(BF16)
        features = feature_rows(get_rows(raw_ref, base + 8, 16))
        part = jnp.dot(features, factor, preferred_element_type=F32)
        total = part if total is None else total + part
    return total[0:16] + total[16:32] + total[32:48]


def stokes_finish(pos, moments):
    m0 = moments[0:3]
    m1 = [[moments[3 + 3 * j + i] for i in range(3)] for j in range(3)]
    m2 = moments[12:15]
    square = pos[0] * pos[0] + pos[1] * pos[1] + pos[2] * pos[2] + 2.0 * SOFT
    along = pos[0] * m0[0] + pos[1] * m0[1] + pos[2] * m0[2]
    along = along - (m1[0][0] + m1[1][1] + m1[2][2])
    out = []
    for i in range(3):
        cross = sum(pos[j] * (2.0 * m1[j][i] + m1[i][j]) for j in range(3))
        out.append(square * m0[i] + m2[i] + pos[i] * along - cross)
    return out


def near_kernel(
    near_ref,
    wall_ref,
    below_ref,
    own_ref,
    above_ref,
    left_ref,
    right_ref,
    drag_ref,
    analysis_ref,
    stiffness_ref,
    synthesis_ref,
    velocity_ref,
    top_ref,
    wall_raw_ref,
    ext_ref,
    pos_ref,
    raw_ref,
    target_ref,
    moment_ref,
):
    rows, _, cols, points = own_ref.shape
    own = rows * cols
    near = near_ref.shape[0]
    wall = wall_ref.shape[0]
    slots = own + near + wall
    ext_ref[:, :, 0:HALO, :] = left_ref[...]
    inner = slice(HALO, HALO + cols)
    ext_ref[0:HALO, :, inner, :] = below_ref[rows - HALO :]
    ext_ref[HALO : HALO + rows, :, inner, :] = own_ref[...]
    ext_ref[HALO + rows :, :, inner, :] = above_ref[0:HALO]
    ext_ref[:, :, HALO + cols :, :] = right_ref[...]
    for r in range(rows):
        for d in range(3):
            pos_ref[d, r * cols : (r + 1) * cols, :] = own_ref[r, d]
    for i in range(near + wall):
        code = near_ref[i] if i < near else wall_ref[i - near]
        row = code // 16
        col = code % 16
        for d in range(3):
            pos_ref[d, own + i : own + i + 1, :] = ext_ref[row, d, pl.ds(col, 1), :]
    everything = [pos_ref[d] for d in range(3)]
    centred = [v - jnp.sum(v, axis=1, keepdims=True) * (1.0 / points) for v in everything]
    flat = jnp.concatenate(centred, axis=0).astype(BF16)
    coeff = jnp.dot(flat, analysis_ref[...], preferred_element_type=F32)
    scaled = (coeff * stiffness_ref[...]).astype(BF16)
    force = -jnp.dot(scaled, synthesis_ref[...], preferred_element_type=F32)
    forces = [force[d * slots : (d + 1) * slots] for d in range(3)]
    for g in range((near + wall) // 8):
        a = own + 8 * g
        into, base = (raw_ref, 8 * g) if 8 * g < near else (wall_raw_ref, 8 * g - near)
        stokes_raw(
            into,
            base * STOKES_ROWS,
            [v[a : a + 8] for v in everything],
            [v[a : a + 8] for v in forces],
        )
    for g in range(own // 8):
        target_raw(target_ref, 64 * g, [v[8 * g : 8 * g + 8] for v in everything])

    def cell(c, carry):
        target = target_rows(get_rows(target_ref, pl.multiple_of(c * 8, 8), 8))
        per = near // own
        moments = stokes_moments(raw_ref, [c * per + k for k in range(per)], target)
        put_rows(moment_ref, c, 16, own, moments)
        return carry

    lax.fori_loop(0, own, cell, 0)
    moments = [get_rows(moment_ref, k * own, own) for k in range(15)]
    own_pos = [v[0:own] for v in everything]
    sums = stokes_finish(own_pos, moments)
    speed = jnp.zeros_like(sums[0])
    for d in range(3):
        velocity = drag_ref[...] * forces[d][0:own] + STOKES_SCALE * sums[d]
        speed = speed + velocity * velocity
        for r in range(rows):
            velocity_ref[r, d] = velocity[r * cols : (r + 1) * cols]
    top = jnp.sqrt(jnp.max(speed, axis=(0, 1), keepdims=True))
    top_ref[...] = jnp.broadcast_to(top, top_ref.shape)


def near_part(near_code, wall_code, below, pos, above, left, right, drag, tables):
    rows, _, cols, points = pos.shape
    own = rows * cols
    near, wall = near_code.shape[0], wall_code.shape[0]
    slots = own + near + wall
    tiles = points // LANES
    in_vmem = pl.BlockSpec(memory_space=pltpu.VMEM)
    in_smem = pl.BlockSpec(memory_space=pltpu.SMEM)
    pairs = own * points * (near // own) * points
    return pl.pallas_call(
        near_kernel,
        in_specs=[in_smem] * 2 + [in_vmem] * 9,
        out_specs=[in_vmem] * 3,
        out_shape=[
            jax.ShapeDtypeStruct((rows, 3, cols, points), F32),
            jax.ShapeDtypeStruct((8, LANES), F32),
            jax.ShapeDtypeStruct((tiles, wall * STOKES_ROWS, LANES), F32),
        ],
        scratch_shapes=[
            pltpu.VMEM((rows + 2 * HALO, 3, cols + 2 * HALO, points), F32),
            pltpu.VMEM((3, slots, points), F32),
            pltpu.VMEM((tiles, near * STOKES_ROWS, LANES), F32),
            pltpu.VMEM((tiles, own * 8, LANES), F32),
            pltpu.VMEM((tiles, own * 16, LANES), F32),
        ],
        compiler_params=pltpu.CompilerParams(vmem_limit_bytes=50 * 2**20),
        cost_estimate=pl.CostEstimate(
            flops=1000 * pairs, bytes_accessed=8 * 2**20, transcendentals=pairs
        ),
        name="near",
    )(near_code, wall_code, below, pos, above, left, right, drag, *tables)


def wall_kernel(stage, per, raw_ref, pos_ref, layer_ref, out_ref, target_ref, moment_ref):
    patches = pos_ref.shape[1]
    pos = [pos_ref[d] for d in range(3)]
    target_raw(target_ref, 0, pos)

    def patch(p, carry):
        target = target_rows(get_rows(target_ref, pl.multiple_of(p * 8, 8), 8))
        moments = stokes_moments(raw_ref, [p * per + stage], target)
        put_rows(moment_ref, p, 16, patches, moments)
        return carry

    lax.fori_loop(0, patches, patch, 0)
    sums = stokes_finish(pos, [get_rows(moment_ref, k * patches, patches) for k in range(15)])
    for d in range(3):
        out_ref[d] = layer_ref[d] + (2.0 * STOKES_SCALE) * sums[d]


def wall_part(stage, per, raw, pos, layer):
    _, patches, points = pos.shape
    tiles = points // LANES
    in_vmem = pl.BlockSpec(memory_space=pltpu.VMEM)
    pairs = patches * raw.shape[0] * LANES * points
    return pl.pallas_call(
        functools.partial(wall_kernel, stage, per),
        in_specs=[in_vmem] * 3,
        out_specs=in_vmem,
        out_shape=jax.ShapeDtypeStruct(pos.shape, F32),
        scratch_shapes=[
            pltpu.VMEM((tiles, patches * 8, LANES), F32),
            pltpu.VMEM((tiles, patches * 16, LANES), F32),
        ],
        compiler_params=pltpu.CompilerParams(vmem_limit_bytes=24 * 2**20),
        cost_estimate=pl.CostEstimate(
            flops=1000 * pairs, bytes_accessed=2 * 2**20, transcendentals=pairs
        ),
        name=f"wall_{stage}",
    )(raw, pos, layer)


def layer_kernel(listed_ref, own_ref, before_ref, after_ref, out_ref, raw_ref, target_ref, left_ref, feature_ref, moment_ref):
    patches = own_ref.shape[1]
    for block, ref in enumerate((before_ref, own_ref, after_ref)):
        y = [ref[d] for d in range(3)]
        normal = [ref[3 + d] for d in range(3)]
        weight = ref[9]
        value = [ref[6 + d] * weight for d in range(3)]
        square = y[0] * y[0] + y[1] * y[1] + y[2] * y[2]
        one, zero = jnp.ones_like(square), jnp.zeros_like(square)
        rows = [-2.0 * y[0], -2.0 * y[1], -2.0 * y[2], square, one, zero, zero, zero]
        for v in (value, normal):
            rows += [v[0], v[1], v[2], -(y[0] * v[0] + y[1] * v[1] + y[2] * v[2])]
            rows += [zero] * 4
        rows += [y[0], y[1], y[2], one, zero, zero, zero, zero]
        for k, row in enumerate(rows):
            put_rows(raw_ref, block * patches * LAYER_ROWS + k, patches, LAYER_ROWS, row)
    pos = [own_ref[d] for d in range(3)]
    target_raw(target_ref, 0, pos)

    def prepare(s, carry):
        raw = get_rows(raw_ref, pl.multiple_of(s * LAYER_ROWS, 8), LAYER_ROWS)
        for k in range(3):
            left_ref[s, k] = source_rows(raw[8 * k : 8 * k + 8])
        split = [p.astype(F32) for p in parts(raw[24:32])]
        split.append(jnp.zeros_like(split[0]))
        feature_ref[s] = jnp.concatenate(split, axis=0).astype(BF16)
        return carry

    lax.fori_loop(0, 3 * patches, prepare, 0)
    listed = listed_ref.shape[1]

    def patch(p, carry):
        target = target_rows(get_rows(target_ref, pl.multiple_of(p * 8, 8), 8))
        total = None
        for k in range(listed + 1):
            s = patches + p if k == 0 else listed_ref[p, k - 1]
            square = product(left_ref[s, 0], target)
            along_q = product(left_ref[s, 1], target)
            along_n = product(left_ref[s, 2], target)
            root = lax.rsqrt(jnp.maximum(square, SOFT))
            double = root * root
            scalar = (along_q * along_n * (double * double * root)).astype(BF16)
            part = jnp.dot(feature_ref[s], scalar, preferred_element_type=F32)
            total = part if total is None else total + part
        moments = total[0:8] + total[8:16] + total[16:24]
        put_rows(moment_ref, p, 8, patches, moments)
        return carry

    lax.fori_loop(0, patches, patch, 0)
    moments = [get_rows(moment_ref, k * patches, patches) for k in range(4)]
    for d in range(3):
        out_ref[d] = (-2.0 * LAYER_SCALE) * (pos[d] * moments[3] - moments[d])


def layer_part(listed, own, before, after):
    _, patches, points = own.shape
    tiles = points // LANES
    in_vmem = pl.BlockSpec(memory_space=pltpu.VMEM)
    pairs = patches * points * (listed.shape[1] + 1) * points
    return pl.pallas_call(
        layer_kernel,
        in_specs=[pl.BlockSpec(memory_space=pltpu.SMEM)] + [in_vmem] * 3,
        out_specs=in_vmem,
        out_shape=jax.ShapeDtypeStruct((3, patches, points), F32),
        scratch_shapes=[
            pltpu.VMEM((tiles, 3 * patches * LAYER_ROWS, LANES), F32),
            pltpu.VMEM((tiles, patches * 8, LANES), F32),
            pltpu.VMEM((3 * patches, 3, 64, points), BF16),
            pltpu.VMEM((3 * patches, 32, points), BF16),
            pltpu.VMEM((tiles, patches * 8, LANES), F32),
        ],
        compiler_params=pltpu.CompilerParams(vmem_limit_bytes=24 * 2**20),
        cost_estimate=pl.CostEstimate(
            flops=1000 * pairs, bytes_accessed=2**20, transcendentals=pairs
        ),
        name="layer",
    )(listed, own, before, after)


def neighbours(low, high, axis):
    size = lax.axis_size(axis)
    up = [(i, (i + 1) % size) for i in range(size)]
    down = [(b, a) for a, b in up]
    return lax.ppermute(high, axis, up), lax.ppermute(low, axis, down)


def rotations(outer, inner, along_outer):
    size = outer if along_outer else inner
    for turn in range(1, size):
        yield [
            (
                a * inner + b,
                (a + turn) % outer * inner + b if along_outer else a * inner + (b + turn) % inner,
            )
            for a in range(outer)
            for b in range(inner)
        ]


def over_all(value):
    for axis, inner in (("cy", 2), ("cx", 4)):
        outer = lax.axis_size(axis) // inner
        for along_outer in (False, True):
            came = [
                lax.ppermute(value, axis, pairs)
                for pairs in rotations(outer, inner, along_outer)
            ]
            value = functools.reduce(jnp.maximum, came, value)
    return value


def body(
    cell_pos,
    cell_drag,
    cell_near,
    analysis,
    stiffness,
    synthesis,
    wall_pos,
    wall_normal,
    wall_weight,
    density,
    patch_near,
    cell_to_patch,
):
    rows, cols = cell_pos.shape[:2]
    all_rows = rows * lax.axis_size("cx")
    all_cols = cols * lax.axis_size("cy")
    first_row = lax.axis_index("cx") * rows
    first_col = lax.axis_index("cy") * cols

    pos = jnp.transpose(cell_pos, (0, 2, 1, 3))
    walls = [jnp.transpose(v, (1, 0, 2)) for v in (wall_pos, wall_normal, density)]
    packed = jnp.concatenate(walls + [wall_weight[None]], axis=0)

    below, above = neighbours(pos, pos, "cx")
    wall_below, wall_above = neighbours(packed, packed, AXES)
    strips = [v[:, :, c : c + HALO] for c in (0, cols - HALO) for v in (below[rows - HALO :], pos, above[:HALO])]
    left, right = neighbours(
        jnp.concatenate(strips[:3], axis=0), jnp.concatenate(strips[3:], axis=0), "cy"
    )

    patches = wall_pos.shape[0]
    all_patches = patches * lax.axis_size(AXES)
    start = lax.axis_index(AXES) * patches
    listed = (patch_near - start + patches) % all_patches
    layer = layer_part(listed, packed, wall_below, wall_above)

    def code(cell):
        row = (cell // all_cols - first_row + HALO) % all_rows
        col = (cell % all_cols - first_col + HALO) % all_cols
        return (row * 16 + col).reshape(-1)

    velocity, top, wall_raw = near_part(
        code(cell_near),
        code(cell_to_patch),
        below,
        pos,
        above,
        left,
        right,
        cell_drag.reshape(-1, 1),
        (analysis, stiffness[None, :], synthesis),
    )
    top = over_all(top)
    density_next = layer
    per = cell_to_patch.shape[1]
    for stage in range(per):
        density_next = wall_part(stage, per, wall_raw, walls[0], density_next)
    step = 1.0 / (top[0, 0] + 1e-06)
    moved = pos + step * velocity
    return jnp.transpose(moved, (0, 2, 1, 3)), jnp.transpose(density_next, (1, 0, 2))


def solution(mesh):
    patch = P(AXES, None, None)
    return jax.shard_map(
        body,
        mesh=mesh,
        in_specs=(
            P("cx", "cy", None, None),
            P("cx", "cy"),
            P("cx", "cy", None),
            P(),
            P(),
            P(),
            patch,
            patch,
            P(AXES, None),
            patch,
            P(AXES, None),
            P(AXES, None),
        ),
        out_specs=(P("cx", "cy", None, None), patch),
        check_vma=False,
    )
```

```python
import functools
import math

import jax
import jax.numpy as jnp
from jax import lax
from jax.experimental import pallas as pl
from jax.experimental.pallas import tpu as pltpu
from jax.sharding import PartitionSpec as P

HALO = 3
FIRST = 2
AXES = ("cx", "cy")
SOFT = 0.25
STOKES_SCALE = 1.0 / (8.0 * math.pi)
LAYER_SCALE = 3.0 / (4.0 * math.pi)
F32 = jnp.float32
BF16 = jnp.bfloat16
LANES = 128

GROUPS = ((0, 0), (0, 1), (1, 0), (0, 2), (2, 0), (1, 1), (1, 2), (2, 1))
STOKES_ROWS = 24
LAYER_ROWS = 32
TARGET_ROWS = 24


def parts(v):
    high = v.astype(BF16)
    rest = v - high.astype(F32)
    middle = rest.astype(BF16)
    low = (rest - middle.astype(F32)).astype(BF16)
    return high, middle, low


def target_rows(raw):
    split = [p.astype(F32) for p in parts(raw)]
    return jnp.concatenate([split[a] for a, _ in GROUPS], axis=0).astype(BF16)


def source_rows(raw):
    split = [p.astype(F32) for p in parts(raw)]
    return jnp.concatenate([split[b] for _, b in GROUPS], axis=0).astype(BF16)


def product(left, right):
    return lax.dot_general(left, right, (((0,), (0,)), ((), ())), preferred_element_type=F32)


def feature_rows(raw):
    return jnp.concatenate(parts(raw), axis=0)


def put_rows(ref, first, count, stride, value):
    for tile in range(ref.shape[0]):
        ref[tile, pl.ds(first, count, stride=stride), :] = value[
            :, tile * LANES : (tile + 1) * LANES
        ]


def get_rows(ref, first, count):
    return jnp.concatenate(
        [ref[tile, pl.ds(first, count), :] for tile in range(ref.shape[0])], axis=1
    )


def stokes_raw(ref, first, pos, force):
    square = pos[0] * pos[0] + pos[1] * pos[1] + pos[2] * pos[2]
    along = pos[0] * force[0] + pos[1] * force[1] + pos[2] * force[2]
    rows = [-2.0 * pos[0], -2.0 * pos[1], -2.0 * pos[2], square, jnp.ones_like(square)]
    rows += [jnp.zeros_like(square)] * 3
    rows += [force[0], force[1], force[2]]
    rows += [pos[j] * force[i] for j in range(3) for i in range(3)]
    rows += [square * force[i] + pos[i] * along for i in range(3)]
    rows += [jnp.zeros_like(square)]
    for k, row in enumerate(rows):
        put_rows(ref, first + k, 8, STOKES_ROWS, row)


def target_raw(ref, first, pos, stride=8):
    square = pos[0] * pos[0] + pos[1] * pos[1] + pos[2] * pos[2] + SOFT
    rows = [pos[0], pos[1], pos[2], jnp.ones_like(square), square]
    rows += [jnp.zeros_like(square)] * 3
    for k, row in enumerate(rows):
        put_rows(ref, first + k, 8, stride, row)


def stokes_moments(raw_ref, slots, target):
    total = None
    for slot in slots:
        base = pl.multiple_of(slot * STOKES_ROWS, 8)
        left = source_rows(get_rows(raw_ref, base, 8))
        square = product(left, target)
        root = lax.rsqrt(jnp.maximum(square, SOFT))
        factor = (root * root * root).astype(BF16)
        features = feature_rows(get_rows(raw_ref, base + 8, 16))
        part = jnp.dot(features, factor, preferred_element_type=F32)
        total = part if total is None else total + part
    return total[0:16] + total[16:32] + total[32:48]


def stokes_finish(pos, moments):
    m0 = moments[0:3]
    m1 = [[moments[3 + 3 * j + i] for i in range(3)] for j in range(3)]
    m2 = moments[12:15]
    square = pos[0] * pos[0] + pos[1] * pos[1] + pos[2] * pos[2] + 2.0 * SOFT
    along = pos[0] * m0[0] + pos[1] * m0[1] + pos[2] * m0[2]
    along = along - (m1[0][0] + m1[1][1] + m1[2][2])
    out = []
    for i in range(3):
        cross = sum(pos[j] * (2.0 * m1[j][i] + m1[i][j]) for j in range(3))
        out.append(square * m0[i] + m2[i] + pos[i] * along - cross)
    return out


def near_kernel(
    near_ref,
    wall_ref,
    below_ref,
    own_ref,
    above_ref,
    left_ref,
    right_ref,
    drag_ref,
    analysis_ref,
    stiffness_ref,
    synthesis_ref,
    velocity_ref,
    top_ref,
    wall_raw_ref,
    ext_ref,
    pos_ref,
    raw_ref,
    target_ref,
    moment_ref,
    first_ref,
    second_ref,
    sems,
):
    tables = [
        pltpu.make_async_copy(a, b, sems.at[k])
        for k, (a, b) in enumerate(((analysis_ref, first_ref), (synthesis_ref, second_ref)))
    ]
    for table in tables:
        table.start()
    rows, _, cols, points = own_ref.shape
    own = rows * cols
    near = near_ref.shape[0]
    wall = wall_ref.shape[0]
    slots = own + near + wall
    ext_ref[:, :, 0:HALO, :] = left_ref[...]
    inner = slice(HALO, HALO + cols)
    ext_ref[0:HALO, :, inner, :] = below_ref[rows - HALO :]
    ext_ref[HALO : HALO + rows, :, inner, :] = own_ref[...]
    ext_ref[HALO + rows :, :, inner, :] = above_ref[0:HALO]
    ext_ref[:, :, HALO + cols :, :] = right_ref[...]
    for r in range(rows):
        for d in range(3):
            pos_ref[d, r * cols : (r + 1) * cols, :] = own_ref[r, d]
    for i in range(near + wall):
        code = near_ref[i] if i < near else wall_ref[i - near]
        row = code // 16
        col = code % 16
        for d in range(3):
            pos_ref[d, own + i : own + i + 1, :] = ext_ref[row, d, pl.ds(col, 1), :]
    everything = [pos_ref[d] for d in range(3)]
    centred = [v - jnp.sum(v, axis=1, keepdims=True) * (1.0 / points) for v in everything]
    flat = jnp.concatenate(centred, axis=0).astype(BF16)
    tables[0].wait()
    coeff = jnp.dot(flat, first_ref[...], preferred_element_type=F32)
    scaled = (coeff * stiffness_ref[...]).astype(BF16)
    tables[1].wait()
    force = -jnp.dot(scaled, second_ref[...], preferred_element_type=F32)
    forces = [force[d * slots : (d + 1) * slots] for d in range(3)]
    for g in range((near + wall) // 8):
        a = own + 8 * g
        into, base = (raw_ref, 8 * g) if 8 * g < near else (wall_raw_ref, 8 * g - near)
        stokes_raw(
            into,
            base * STOKES_ROWS,
            [v[a : a + 8] for v in everything],
            [v[a : a + 8] for v in forces],
        )
    for g in range(own // 8):
        target_raw(target_ref, 64 * g, [v[8 * g : 8 * g + 8] for v in everything])

    def cell(c, carry):
        target = target_rows(get_rows(target_ref, pl.multiple_of(c * 8, 8), 8))
        per = near // own
        moments = stokes_moments(raw_ref, [c * per + k for k in range(per)], target)
        put_rows(moment_ref, c, 16, own, moments)
        return carry

    lax.fori_loop(0, own, cell, 0, unroll=2)
    moments = [get_rows(moment_ref, k * own, own) for k in range(15)]
    own_pos = [v[0:own] for v in everything]
    sums = stokes_finish(own_pos, moments)
    speed = jnp.zeros_like(sums[0])
    for d in range(3):
        velocity = drag_ref[...] * forces[d][0:own] + STOKES_SCALE * sums[d]
        speed = speed + velocity * velocity
        for r in range(rows):
            velocity_ref[r, d] = velocity[r * cols : (r + 1) * cols]
    top = jnp.sqrt(jnp.max(speed, axis=(0, 1), keepdims=True))
    top_ref[...] = jnp.broadcast_to(top, top_ref.shape)


def near_part(near_code, wall_code, below, pos, above, left, right, drag, tables):
    rows, _, cols, points = pos.shape
    own = rows * cols
    near, wall = near_code.shape[0], wall_code.shape[0]
    slots = own + near + wall
    tiles = points // LANES
    in_vmem = pl.BlockSpec(memory_space=pltpu.VMEM)
    in_smem = pl.BlockSpec(memory_space=pltpu.SMEM)
    in_hbm = pl.BlockSpec(memory_space=pl.ANY)
    pairs = own * points * (near // own) * points
    return pl.pallas_call(
        near_kernel,
        in_specs=[in_smem] * 2 + [in_vmem] * 6 + [in_hbm, in_vmem, in_hbm],
        out_specs=[in_vmem] * 3,
        out_shape=[
            jax.ShapeDtypeStruct((rows, 3, cols, points), F32),
            jax.ShapeDtypeStruct((8, LANES), F32),
            jax.ShapeDtypeStruct((tiles, wall * STOKES_ROWS, LANES), F32),
        ],
        scratch_shapes=[
            pltpu.VMEM((rows + 2 * HALO, 3, cols + 2 * HALO, points), F32),
            pltpu.VMEM((3, slots, points), F32),
            pltpu.VMEM((tiles, near * STOKES_ROWS, LANES), F32),
            pltpu.VMEM((tiles, own * 8, LANES), F32),
            pltpu.VMEM((tiles, own * 16, LANES), F32),
            pltpu.VMEM(tables[0].shape, BF16),
            pltpu.VMEM(tables[2].shape, BF16),
            pltpu.SemaphoreType.DMA((2,)),
        ],
        compiler_params=pltpu.CompilerParams(vmem_limit_bytes=50 * 2**20),
        cost_estimate=pl.CostEstimate(
            flops=1000 * pairs, bytes_accessed=8 * 2**20, transcendentals=pairs
        ),
        name="near",
    )(near_code, wall_code, below, pos, above, left, right, drag, *tables)


def wall_kernel(stage, per, raw_ref, pos_ref, layer_ref, out_ref, target_ref, moment_ref):
    patches = pos_ref.shape[1]
    pos = [pos_ref[d] for d in range(3)]
    target_raw(target_ref, 0, pos)

    def patch(p, carry):
        target = target_rows(get_rows(target_ref, pl.multiple_of(p * 8, 8), 8))
        moments = stokes_moments(raw_ref, [p * per + stage], target)
        put_rows(moment_ref, p, 16, patches, moments)
        return carry

    lax.fori_loop(0, patches, patch, 0, unroll=True)
    sums = stokes_finish(pos, [get_rows(moment_ref, k * patches, patches) for k in range(15)])
    for d in range(3):
        out_ref[d] = layer_ref[d] + (2.0 * STOKES_SCALE) * sums[d]


def wall_part(stage, per, raw, pos, layer):
    _, patches, points = pos.shape
    tiles = points // LANES
    in_vmem = pl.BlockSpec(memory_space=pltpu.VMEM)
    pairs = patches * raw.shape[0] * LANES * points
    return pl.pallas_call(
        functools.partial(wall_kernel, stage, per),
        in_specs=[in_vmem] * 3,
        out_specs=in_vmem,
        out_shape=jax.ShapeDtypeStruct(pos.shape, F32),
        scratch_shapes=[
            pltpu.VMEM((tiles, patches * 8, LANES), F32),
            pltpu.VMEM((tiles, patches * 16, LANES), F32),
        ],
        compiler_params=pltpu.CompilerParams(vmem_limit_bytes=24 * 2**20),
        cost_estimate=pl.CostEstimate(
            flops=1000 * pairs, bytes_accessed=2 * 2**20, transcendentals=pairs
        ),
        name=f"wall_{stage}",
    )(raw, pos, layer)


def layer_sums(listed_ref, own_ref, left_ref, feature_ref, target_ref, moment_ref):
    patches = own_ref.shape[1]
    x = [own_ref[d] for d in range(3)]
    target_raw(target_ref, 0, x, TARGET_ROWS)
    rows = [x[0] * x[0], x[1] * x[1], x[2] * x[2], x[0] * x[1], x[0] * x[2], x[1] * x[2]]
    rows += x + [jnp.ones_like(x[0])] + [jnp.zeros_like(x[0])] * 6
    for k, row in enumerate(rows):
        put_rows(target_ref, 8 + k, patches, TARGET_ROWS, row)

    def patch(p, carry):
        raw = get_rows(target_ref, pl.multiple_of(p * TARGET_ROWS, 8), TARGET_ROWS)
        near, form = target_rows(raw[0:8]), target_rows(raw[8:24])
        total = None
        for k in range(listed_ref.shape[1]):
            s = listed_ref[p, k]
            square = product(left_ref[s, 0:64], near)
            scalar = product(left_ref[s, 64:192], form)
            root = lax.rsqrt(jnp.maximum(square, SOFT))
            double = root * root
            scalar = (scalar * (double * double * root)).astype(BF16)
            part = jnp.dot(feature_ref[s], scalar, preferred_element_type=F32)
            total = part if total is None else total + part
        moments = total[0:8] + total[8:16] + total[16:24]
        put_rows(moment_ref, p, 8, patches, moments)
        return carry

    lax.fori_loop(0, patches, patch, 0, unroll=True)
    moments = [get_rows(moment_ref, k * patches, patches) for k in range(4)]
    return [(-2.0 * LAYER_SCALE) * (x[d] * moments[3] - moments[d]) for d in range(3)]


def layer_first(listed_ref, own_ref, before_ref, after_ref, out_ref, left_ref, feature_ref, raw_ref, target_ref, moment_ref):
    patches = own_ref.shape[1]
    for block, ref in enumerate((before_ref, own_ref, after_ref)):
        y = [ref[d] for d in range(3)]
        n = [ref[3 + d] for d in range(3)]
        v = [ref[6 + d] * ref[9] for d in range(3)]
        square = y[0] * y[0] + y[1] * y[1] + y[2] * y[2]
        along_n = y[0] * n[0] + y[1] * n[1] + y[2] * n[2]
        along_v = y[0] * v[0] + y[1] * v[1] + y[2] * v[2]
        one, zero = jnp.ones_like(square), jnp.zeros_like(square)
        rows = [-2.0 * y[0], -2.0 * y[1], -2.0 * y[2], square, one, zero, zero, zero]
        rows += [v[d] * n[d] for d in range(3)]
        rows += [v[a] * n[b] + v[b] * n[a] for a, b in ((0, 1), (0, 2), (1, 2))]
        rows += [-(v[d] * along_n + n[d] * along_v) for d in range(3)]
        rows += [along_v * along_n] + [zero] * 6
        rows += [y[0], y[1], y[2], one, zero, zero, zero, zero]
        for k, row in enumerate(rows):
            put_rows(raw_ref, block * patches * LAYER_ROWS + k, patches, LAYER_ROWS, row)

    def prepare(s, carry):
        raw = get_rows(raw_ref, pl.multiple_of(s * LAYER_ROWS, 8), LAYER_ROWS)
        left_ref[s, 0:64] = source_rows(raw[0:8])
        left_ref[s, 64:192] = source_rows(raw[8:24])
        split = [p.astype(F32) for p in parts(raw[24:32])]
        split.append(jnp.zeros_like(split[0]))
        feature_ref[s] = jnp.concatenate(split, axis=0).astype(BF16)
        return carry

    lax.fori_loop(0, 3 * patches, prepare, 0, unroll=4)
    sums = layer_sums(listed_ref, own_ref, left_ref, feature_ref, target_ref, moment_ref)
    for d in range(3):
        out_ref[d] = sums[d]


def layer_second(listed_ref, own_ref, left_ref, feature_ref, so_far_ref, out_ref, target_ref, moment_ref):
    sums = layer_sums(listed_ref, own_ref, left_ref, feature_ref, target_ref, moment_ref)
    for d in range(3):
        out_ref[d] = so_far_ref[d] + sums[d]


def layer_part(kernel, listed, *arrays):
    _, patches, points = arrays[0].shape
    tiles = points // LANES
    in_vmem = pl.BlockSpec(memory_space=pltpu.VMEM)
    pairs = patches * points * listed.shape[1] * points
    out_shape = [jax.ShapeDtypeStruct((3, patches, points), F32)]
    scratch = [
        pltpu.VMEM((tiles, patches * TARGET_ROWS, LANES), F32),
        pltpu.VMEM((tiles, patches * 8, LANES), F32),
    ]
    if kernel is layer_first:
        out_shape += [
            jax.ShapeDtypeStruct((3 * patches, 192, points), BF16),
            jax.ShapeDtypeStruct((3 * patches, 32, points), BF16),
        ]
        scratch.insert(0, pltpu.VMEM((tiles, 3 * patches * LAYER_ROWS, LANES), F32))
    return pl.pallas_call(
        kernel,
        in_specs=[pl.BlockSpec(memory_space=pltpu.SMEM)] + [in_vmem] * len(arrays),
        out_specs=[in_vmem] * len(out_shape),
        out_shape=out_shape,
        scratch_shapes=scratch,
        compiler_params=pltpu.CompilerParams(vmem_limit_bytes=24 * 2**20),
        cost_estimate=pl.CostEstimate(
            flops=1000 * pairs, bytes_accessed=2**20, transcendentals=pairs
        ),
        name=kernel.__name__,
    )(listed, *arrays)


def move_kernel(*refs):
    *tops, pos_ref, velocity_ref, out_ref = refs
    top = functools.reduce(jnp.maximum, [t[...] for t in tops])
    step = 1.0 / (top[0:1, 0:1] + 1e-06)
    rows, _, cols, _ = pos_ref.shape
    for r in range(rows):
        for d in range(3):
            out_ref[r, d] = pos_ref[r, d] + step * velocity_ref[r, d]


def move_part(tops, pos, velocity):
    in_vmem = pl.BlockSpec(memory_space=pltpu.VMEM)
    return pl.pallas_call(
        move_kernel,
        in_specs=[in_vmem] * (len(tops) + 2),
        out_specs=in_vmem,
        out_shape=jax.ShapeDtypeStruct(pos.shape, F32),
        name="move",
    )(*tops, pos, velocity)


def neighbours(low, high, axis):
    size = lax.axis_size(axis)
    up = [(i, (i + 1) % size) for i in range(size)]
    down = [(b, a) for a, b in up]
    return lax.ppermute(high, axis, up), lax.ppermute(low, axis, down)


def rotations(outer, inner, along_outer):
    size = outer if along_outer else inner
    for turn in range(1, size):
        yield [
            (
                a * inner + b,
                (a + turn) % outer * inner + b if along_outer else a * inner + (b + turn) % inner,
            )
            for a in range(outer)
            for b in range(inner)
        ]


def over_all(value):
    values = [value]
    for axis, inner in (("cy", 2), ("cx", 4)):
        outer = lax.axis_size(axis) // inner
        for along_outer in (False, True):
            value = functools.reduce(jnp.maximum, values)
            values = [value] + [
                lax.ppermute(value, axis, pairs)
                for pairs in rotations(outer, inner, along_outer)
            ]
    return values


def body(
    cell_pos,
    cell_drag,
    cell_near,
    analysis,
    stiffness,
    synthesis,
    wall_pos,
    wall_normal,
    wall_weight,
    density,
    patch_near,
    cell_to_patch,
):
    rows, cols = cell_pos.shape[:2]
    all_rows = rows * lax.axis_size("cx")
    all_cols = cols * lax.axis_size("cy")
    first_row = lax.axis_index("cx") * rows
    first_col = lax.axis_index("cy") * cols

    pos = jnp.transpose(cell_pos, (0, 2, 1, 3))
    walls = [jnp.transpose(v, (1, 0, 2)) for v in (wall_pos, wall_normal, density)]
    packed = jnp.concatenate(walls + [wall_weight[None]], axis=0)

    below, above = neighbours(pos, pos, "cx")
    wall_below, wall_above = neighbours(packed, packed, AXES)
    strips = [v[:, :, c : c + HALO] for c in (0, cols - HALO) for v in (below[rows - HALO :], pos, above[:HALO])]
    left, right = neighbours(
        jnp.concatenate(strips[:3], axis=0), jnp.concatenate(strips[3:], axis=0), "cy"
    )

    patches = wall_pos.shape[0]
    all_patches = patches * lax.axis_size(AXES)
    start = lax.axis_index(AXES) * patches
    listed = (patch_near - start + patches) % all_patches
    itself = patches + jnp.arange(patches, dtype=jnp.int32)[:, None]
    listed = jnp.concatenate([itself, listed], axis=1)
    early = listed[:, :FIRST]
    layer, lefts, features = layer_part(layer_first, early, packed, wall_below, wall_above)

    def code(cell):
        row = (cell // all_cols - first_row + HALO) % all_rows
        col = (cell % all_cols - first_col + HALO) % all_cols
        return (row * 16 + col).reshape(-1)

    near_code, layer = lax.optimization_barrier((code(cell_near), layer))
    velocity, top, wall_raw = near_part(
        near_code,
        code(cell_to_patch),
        below,
        pos,
        above,
        left,
        right,
        cell_drag.reshape(-1, 1),
        (analysis, stiffness[None, :], synthesis),
    )
    top, late = lax.optimization_barrier((top, listed[:, FIRST:]))
    tops = over_all(top)
    [density_next] = layer_part(layer_second, late, packed, lefts, features, layer)
    per = cell_to_patch.shape[1]
    for stage in range(per):
        density_next = wall_part(stage, per, wall_raw, walls[0], density_next)
    moved = move_part(tops, pos, velocity)
    return jnp.transpose(moved, (0, 2, 1, 3)), jnp.transpose(density_next, (1, 0, 2))


def solution(mesh):
    patch = P(AXES, None, None)
    return jax.shard_map(
        body,
        mesh=mesh,
        in_specs=(
            P("cx", "cy", None, None),
            P("cx", "cy"),
            P("cx", "cy", None),
            P(),
            P(),
            P(),
            patch,
            patch,
            P(AXES, None),
            patch,
            P(AXES, None),
            P(AXES, None),
        ),
        out_specs=(P("cx", "cy", None, None), patch),
        check_vma=False,
    )
```

```python
import functools
import math

import jax
import jax.numpy as jnp
from jax import lax
from jax.experimental import pallas as pl
from jax.experimental.pallas import tpu as pltpu
from jax.sharding import PartitionSpec as P

HALO = 3
FIRST = 2
AXES = ("cx", "cy")
SOFT = 0.25
STOKES_SCALE = 1.0 / (8.0 * math.pi)
LAYER_SCALE = 3.0 / (4.0 * math.pi)
F32 = jnp.float32
BF16 = jnp.bfloat16
LANES = 128

GROUPS = ((0, 0), (0, 1), (1, 0), (0, 2), (2, 0), (1, 1), (1, 2), (2, 1))
STOKES_ROWS = 24
LAYER_ROWS = 32
TARGET_ROWS = 24


def parts(v):
    high = v.astype(BF16)
    rest = v - high.astype(F32)
    middle = rest.astype(BF16)
    low = (rest - middle.astype(F32)).astype(BF16)
    return high, middle, low


def target_rows(raw):
    split = [p.astype(F32) for p in parts(raw)]
    return jnp.concatenate([split[a] for a, _ in GROUPS], axis=0).astype(BF16)


def source_rows(raw):
    split = [p.astype(F32) for p in parts(raw)]
    return jnp.concatenate([split[b] for _, b in GROUPS], axis=0).astype(BF16)


def product(left, right):
    return lax.dot_general(left, right, (((0,), (0,)), ((), ())), preferred_element_type=F32)


def feature_rows(raw):
    return jnp.concatenate(parts(raw), axis=0)


def put_rows(ref, first, count, stride, value):
    for tile in range(ref.shape[0]):
        ref[tile, pl.ds(first, count, stride=stride), :] = value[
            :, tile * LANES : (tile + 1) * LANES
        ]


def get_rows(ref, first, count):
    return jnp.concatenate(
        [ref[tile, pl.ds(first, count), :] for tile in range(ref.shape[0])], axis=1
    )


def stokes_raw(ref, first, pos, force):
    square = pos[0] * pos[0] + pos[1] * pos[1] + pos[2] * pos[2]
    along = pos[0] * force[0] + pos[1] * force[1] + pos[2] * force[2]
    rows = [-2.0 * pos[0], -2.0 * pos[1], -2.0 * pos[2], square, jnp.ones_like(square)]
    rows += [jnp.zeros_like(square)] * 3
    rows += [force[0], force[1], force[2]]
    rows += [pos[j] * force[i] for j in range(3) for i in range(3)]
    rows += [square * force[i] + pos[i] * along for i in range(3)]
    rows += [jnp.zeros_like(square)]
    for k, row in enumerate(rows):
        put_rows(ref, first + k, 8, STOKES_ROWS, row)


def target_raw(ref, first, pos, stride=8):
    square = pos[0] * pos[0] + pos[1] * pos[1] + pos[2] * pos[2] + SOFT
    rows = [pos[0], pos[1], pos[2], jnp.ones_like(square), square]
    rows += [jnp.zeros_like(square)] * 3
    for k, row in enumerate(rows):
        put_rows(ref, first + k, 8, stride, row)


def stokes_moments(raw_ref, slots, target):
    total = None
    for slot in slots:
        base = pl.multiple_of(slot * STOKES_ROWS, 8)
        left = source_rows(get_rows(raw_ref, base, 8))
        square = product(left, target)
        root = lax.rsqrt(jnp.maximum(square, SOFT))
        factor = (root * root * root).astype(BF16)
        features = feature_rows(get_rows(raw_ref, base + 8, 16))
        part = jnp.dot(features, factor, preferred_element_type=F32)
        total = part if total is None else total + part
    return total[0:16] + total[16:32] + total[32:48]


def stokes_finish(pos, moments):
    m0 = moments[0:3]
    m1 = [[moments[3 + 3 * j + i] for i in range(3)] for j in range(3)]
    m2 = moments[12:15]
    square = pos[0] * pos[0] + pos[1] * pos[1] + pos[2] * pos[2] + 2.0 * SOFT
    along = pos[0] * m0[0] + pos[1] * m0[1] + pos[2] * m0[2]
    along = along - (m1[0][0] + m1[1][1] + m1[2][2])
    out = []
    for i in range(3):
        cross = sum(pos[j] * (2.0 * m1[j][i] + m1[i][j]) for j in range(3))
        out.append(square * m0[i] + m2[i] + pos[i] * along - cross)
    return out


def near_kernel(
    near_ref,
    wall_ref,
    below_ref,
    own_ref,
    above_ref,
    left_below_ref,
    left_ref,
    left_above_ref,
    right_below_ref,
    right_ref,
    right_above_ref,
    drag_ref,
    analysis_ref,
    stiffness_ref,
    synthesis_ref,
    velocity_ref,
    top_ref,
    wall_raw_ref,
    ext_ref,
    pos_ref,
    raw_ref,
    target_ref,
    moment_ref,
    first_ref,
    second_ref,
    sems,
):
    tables = [
        pltpu.make_async_copy(a, b, sems.at[k])
        for k, (a, b) in enumerate(((analysis_ref, first_ref), (synthesis_ref, second_ref)))
    ]
    for table in tables:
        table.start()
    rows, _, cols, points = own_ref.shape
    own = rows * cols
    near = near_ref.shape[0]
    wall = wall_ref.shape[0]
    slots = own + near + wall
    columns = (
        (slice(0, HALO), (left_below_ref, left_ref, left_above_ref)),
        (slice(HALO, HALO + cols), (below_ref, own_ref, above_ref)),
        (slice(HALO + cols, cols + 2 * HALO), (right_below_ref, right_ref, right_above_ref)),
    )
    for where, (before, beside, after) in columns:
        ext_ref[0:HALO, :, where, :] = before[rows - HALO :]
        ext_ref[HALO : HALO + rows, :, where, :] = beside[...]
        ext_ref[HALO + rows :, :, where, :] = after[0:HALO]
    for r in range(rows):
        for d in range(3):
            pos_ref[d, r * cols : (r + 1) * cols, :] = own_ref[r, d]
    for i in range(near + wall):
        code = near_ref[i] if i < near else wall_ref[i - near]
        row = code // 16
        col = code % 16
        for d in range(3):
            pos_ref[d, own + i : own + i + 1, :] = ext_ref[row, d, pl.ds(col, 1), :]
    everything = [pos_ref[d] for d in range(3)]
    centred = [v - jnp.sum(v, axis=1, keepdims=True) * (1.0 / points) for v in everything]
    flat = jnp.concatenate(centred, axis=0).astype(BF16)
    tables[0].wait()
    coeff = jnp.dot(flat, first_ref[...], preferred_element_type=F32)
    scaled = (coeff * stiffness_ref[...]).astype(BF16)
    tables[1].wait()
    force = -jnp.dot(scaled, second_ref[...], preferred_element_type=F32)
    forces = [force[d * slots : (d + 1) * slots] for d in range(3)]
    for g in range((near + wall) // 8):
        a = own + 8 * g
        into, base = (raw_ref, 8 * g) if 8 * g < near else (wall_raw_ref, 8 * g - near)
        stokes_raw(
            into,
            base * STOKES_ROWS,
            [v[a : a + 8] for v in everything],
            [v[a : a + 8] for v in forces],
        )
    for g in range(own // 8):
        target_raw(target_ref, 64 * g, [v[8 * g : 8 * g + 8] for v in everything])

    def cell(c, carry):
        target = target_rows(get_rows(target_ref, pl.multiple_of(c * 8, 8), 8))
        per = near // own
        moments = stokes_moments(raw_ref, [c * per + k for k in range(per)], target)
        put_rows(moment_ref, c, 16, own, moments)
        return carry

    lax.fori_loop(0, own, cell, 0, unroll=2)
    moments = [get_rows(moment_ref, k * own, own) for k in range(15)]
    own_pos = [v[0:own] for v in everything]
    sums = stokes_finish(own_pos, moments)
    speed = jnp.zeros_like(sums[0])
    for d in range(3):
        velocity = drag_ref[...] * forces[d][0:own] + STOKES_SCALE * sums[d]
        speed = speed + velocity * velocity
        for r in range(rows):
            velocity_ref[r, d] = velocity[r * cols : (r + 1) * cols]
    top = jnp.sqrt(jnp.max(speed, axis=(0, 1), keepdims=True))
    top_ref[...] = jnp.broadcast_to(top, top_ref.shape)


def near_part(near_code, wall_code, below, pos, above, left, right, drag, tables):
    rows, _, cols, points = pos.shape
    own = rows * cols
    near, wall = near_code.shape[0], wall_code.shape[0]
    slots = own + near + wall
    tiles = points // LANES
    in_vmem = pl.BlockSpec(memory_space=pltpu.VMEM)
    in_smem = pl.BlockSpec(memory_space=pltpu.SMEM)
    in_hbm = pl.BlockSpec(memory_space=pl.ANY)
    pairs = own * points * (near // own) * points
    return pl.pallas_call(
        near_kernel,
        in_specs=[in_smem] * 2 + [in_vmem] * 10 + [in_hbm, in_vmem, in_hbm],
        out_specs=[in_vmem] * 3,
        out_shape=[
            jax.ShapeDtypeStruct((rows, 3, cols, points), F32),
            jax.ShapeDtypeStruct((8, LANES), F32),
            jax.ShapeDtypeStruct((tiles, wall * STOKES_ROWS, LANES), F32),
        ],
        scratch_shapes=[
            pltpu.VMEM((rows + 2 * HALO, 3, cols + 2 * HALO, points), F32),
            pltpu.VMEM((3, slots, points), F32),
            pltpu.VMEM((tiles, near * STOKES_ROWS, LANES), F32),
            pltpu.VMEM((tiles, own * 8, LANES), F32),
            pltpu.VMEM((tiles, own * 16, LANES), F32),
            pltpu.VMEM(tables[0].shape, BF16),
            pltpu.VMEM(tables[2].shape, BF16),
            pltpu.SemaphoreType.DMA((2,)),
        ],
        compiler_params=pltpu.CompilerParams(vmem_limit_bytes=50 * 2**20),
        cost_estimate=pl.CostEstimate(
            flops=1000 * pairs, bytes_accessed=8 * 2**20, transcendentals=pairs
        ),
        name="near",
    )(near_code, wall_code, below, pos, above, *left, *right, drag, *tables)


def wall_kernel(stage, per, raw_ref, pos_ref, layer_ref, out_ref, target_ref, moment_ref):
    patches = pos_ref.shape[1]
    pos = [pos_ref[d] for d in range(3)]
    target_raw(target_ref, 0, pos)

    def patch(p, carry):
        target = target_rows(get_rows(target_ref, pl.multiple_of(p * 8, 8), 8))
        moments = stokes_moments(raw_ref, [p * per + stage], target)
        put_rows(moment_ref, p, 16, patches, moments)
        return carry

    lax.fori_loop(0, patches, patch, 0, unroll=True)
    sums = stokes_finish(pos, [get_rows(moment_ref, k * patches, patches) for k in range(15)])
    for d in range(3):
        out_ref[d] = layer_ref[d] + (2.0 * STOKES_SCALE) * sums[d]


def wall_part(stage, per, raw, pos, layer):
    _, patches, points = pos.shape
    tiles = points // LANES
    in_vmem = pl.BlockSpec(memory_space=pltpu.VMEM)
    pairs = patches * raw.shape[0] * LANES * points
    return pl.pallas_call(
        functools.partial(wall_kernel, stage, per),
        in_specs=[in_vmem] * 3,
        out_specs=in_vmem,
        out_shape=jax.ShapeDtypeStruct(pos.shape, F32),
        scratch_shapes=[
            pltpu.VMEM((tiles, patches * 8, LANES), F32),
            pltpu.VMEM((tiles, patches * 16, LANES), F32),
        ],
        compiler_params=pltpu.CompilerParams(vmem_limit_bytes=24 * 2**20),
        cost_estimate=pl.CostEstimate(
            flops=1000 * pairs, bytes_accessed=2 * 2**20, transcendentals=pairs
        ),
        name=f"wall_{stage}",
    )(raw, pos, layer)


def layer_sums(listed_ref, own_ref, left_ref, feature_ref, target_ref, moment_ref):
    patches = own_ref.shape[1]
    x = [own_ref[d] for d in range(3)]
    target_raw(target_ref, 0, x, TARGET_ROWS)
    rows = [x[0] * x[0], x[1] * x[1], x[2] * x[2], x[0] * x[1], x[0] * x[2], x[1] * x[2]]
    rows += x + [jnp.ones_like(x[0])] + [jnp.zeros_like(x[0])] * 6
    for k, row in enumerate(rows):
        put_rows(target_ref, 8 + k, patches, TARGET_ROWS, row)

    def patch(p, carry):
        raw = get_rows(target_ref, pl.multiple_of(p * TARGET_ROWS, 8), TARGET_ROWS)
        near, form = target_rows(raw[0:8]), target_rows(raw[8:24])
        total = None
        for k in range(listed_ref.shape[1]):
            s = listed_ref[p, k]
            square = product(left_ref[s, 0:64], near)
            scalar = product(left_ref[s, 64:192], form)
            root = lax.rsqrt(jnp.maximum(square, SOFT))
            double = root * root
            scalar = (scalar * (double * double * root)).astype(BF16)
            part = jnp.dot(feature_ref[s], scalar, preferred_element_type=F32)
            total = part if total is None else total + part
        moments = total[0:8] + total[8:16] + total[16:24]
        put_rows(moment_ref, p, 8, patches, moments)
        return carry

    lax.fori_loop(0, patches, patch, 0, unroll=True)
    moments = [get_rows(moment_ref, k * patches, patches) for k in range(4)]
    return [(-2.0 * LAYER_SCALE) * (x[d] * moments[3] - moments[d]) for d in range(3)]


def layer_first(listed_ref, own_ref, before_ref, after_ref, out_ref, left_ref, feature_ref, raw_ref, target_ref, moment_ref):
    patches = own_ref.shape[1]
    for block, ref in enumerate((before_ref, own_ref, after_ref)):
        y = [ref[d] for d in range(3)]
        n = [ref[3 + d] for d in range(3)]
        v = [ref[6 + d] * ref[9] for d in range(3)]
        square = y[0] * y[0] + y[1] * y[1] + y[2] * y[2]
        along_n = y[0] * n[0] + y[1] * n[1] + y[2] * n[2]
        along_v = y[0] * v[0] + y[1] * v[1] + y[2] * v[2]
        one, zero = jnp.ones_like(square), jnp.zeros_like(square)
        rows = [-2.0 * y[0], -2.0 * y[1], -2.0 * y[2], square, one, zero, zero, zero]
        rows += [v[d] * n[d] for d in range(3)]
        rows += [v[a] * n[b] + v[b] * n[a] for a, b in ((0, 1), (0, 2), (1, 2))]
        rows += [-(v[d] * along_n + n[d] * along_v) for d in range(3)]
        rows += [along_v * along_n] + [zero] * 6
        rows += [y[0], y[1], y[2], one, zero, zero, zero, zero]
        for k, row in enumerate(rows):
            put_rows(raw_ref, block * patches * LAYER_ROWS + k, patches, LAYER_ROWS, row)

    def prepare(s, carry):
        raw = get_rows(raw_ref, pl.multiple_of(s * LAYER_ROWS, 8), LAYER_ROWS)
        left_ref[s, 0:64] = source_rows(raw[0:8])
        left_ref[s, 64:192] = source_rows(raw[8:24])
        split = [p.astype(F32) for p in parts(raw[24:32])]
        split.append(jnp.zeros_like(split[0]))
        feature_ref[s] = jnp.concatenate(split, axis=0).astype(BF16)
        return carry

    lax.fori_loop(0, 3 * patches, prepare, 0, unroll=4)
    sums = layer_sums(listed_ref, own_ref, left_ref, feature_ref, target_ref, moment_ref)
    for d in range(3):
        out_ref[d] = sums[d]


def layer_second(listed_ref, own_ref, left_ref, feature_ref, so_far_ref, out_ref, target_ref, moment_ref):
    sums = layer_sums(listed_ref, own_ref, left_ref, feature_ref, target_ref, moment_ref)
    for d in range(3):
        out_ref[d] = so_far_ref[d] + sums[d]


def layer_part(kernel, listed, *arrays):
    _, patches, points = arrays[0].shape
    tiles = points // LANES
    in_vmem = pl.BlockSpec(memory_space=pltpu.VMEM)
    pairs = patches * points * listed.shape[1] * points
    out_shape = [jax.ShapeDtypeStruct((3, patches, points), F32)]
    scratch = [
        pltpu.VMEM((tiles, patches * TARGET_ROWS, LANES), F32),
        pltpu.VMEM((tiles, patches * 8, LANES), F32),
    ]
    if kernel is layer_first:
        out_shape += [
            jax.ShapeDtypeStruct((3 * patches, 192, points), BF16),
            jax.ShapeDtypeStruct((3 * patches, 32, points), BF16),
        ]
        scratch.insert(0, pltpu.VMEM((tiles, 3 * patches * LAYER_ROWS, LANES), F32))
    return pl.pallas_call(
        kernel,
        in_specs=[pl.BlockSpec(memory_space=pltpu.SMEM)] + [in_vmem] * len(arrays),
        out_specs=[in_vmem] * len(out_shape),
        out_shape=out_shape,
        scratch_shapes=scratch,
        compiler_params=pltpu.CompilerParams(vmem_limit_bytes=24 * 2**20),
        cost_estimate=pl.CostEstimate(
            flops=1000 * pairs, bytes_accessed=2**20, transcendentals=pairs
        ),
        name=kernel.__name__,
    )(listed, *arrays)


def move_kernel(*refs):
    *tops, pos_ref, velocity_ref, out_ref = refs
    top = functools.reduce(jnp.maximum, [t[...] for t in tops])
    step = 1.0 / (top[0:1, 0:1] + 1e-06)
    rows, _, cols, _ = pos_ref.shape
    for r in range(rows):
        for d in range(3):
            out_ref[r, d] = pos_ref[r, d] + step * velocity_ref[r, d]


def move_part(tops, pos, velocity):
    in_vmem = pl.BlockSpec(memory_space=pltpu.VMEM)
    return pl.pallas_call(
        move_kernel,
        in_specs=[in_vmem] * (len(tops) + 2),
        out_specs=in_vmem,
        out_shape=jax.ShapeDtypeStruct(pos.shape, F32),
        compiler_params=pltpu.CompilerParams(vmem_limit_bytes=8 * 2**20),
        name="move",
    )(*tops, pos, velocity)


def neighbours(low, high, axis):
    size = lax.axis_size(axis)
    up = [(i, (i + 1) % size) for i in range(size)]
    down = [(b, a) for a, b in up]
    return lax.ppermute(high, axis, up), lax.ppermute(low, axis, down)


def shifted(value, up, along):
    rows, cols = lax.axis_size("cx"), lax.axis_size("cy")
    pairs = [
        (i * cols + j, (i + up) % rows * cols + (j + along) % cols)
        for i in range(rows)
        for j in range(cols)
    ]
    return lax.ppermute(value, AXES, pairs)


def rotations(outer, inner, along_outer):
    size = outer if along_outer else inner
    for turn in range(1, size):
        yield [
            (
                a * inner + b,
                (a + turn) % outer * inner + b if along_outer else a * inner + (b + turn) % inner,
            )
            for a in range(outer)
            for b in range(inner)
        ]


def over_all(value):
    values = [value]
    for axis, inner in (("cy", 2), ("cx", 4)):
        outer = lax.axis_size(axis) // inner
        for along_outer in (False, True):
            value = functools.reduce(jnp.maximum, values)
            values = [value] + [
                lax.ppermute(value, axis, pairs)
                for pairs in rotations(outer, inner, along_outer)
            ]
    return values


def body(
    cell_pos,
    cell_drag,
    cell_near,
    analysis,
    stiffness,
    synthesis,
    wall_pos,
    wall_normal,
    wall_weight,
    density,
    patch_near,
    cell_to_patch,
):
    rows, cols = cell_pos.shape[:2]
    all_rows = rows * lax.axis_size("cx")
    all_cols = cols * lax.axis_size("cy")
    first_row = lax.axis_index("cx") * rows
    first_col = lax.axis_index("cy") * cols

    pos = jnp.transpose(cell_pos, (0, 2, 1, 3))
    walls = [jnp.transpose(v, (1, 0, 2)) for v in (wall_pos, wall_normal, density)]
    packed = jnp.concatenate(walls + [wall_weight[None]], axis=0)

    below, above = shifted(pos, 1, 0), shifted(pos, -1, 0)
    wall_below, wall_above = neighbours(packed, packed, AXES)
    low, high = pos[:, :, :HALO], pos[:, :, cols - HALO :]
    left = [shifted(high, up, 1) for up in (1, 0, -1)]
    right = [shifted(low, up, -1) for up in (1, 0, -1)]

    patches = wall_pos.shape[0]
    all_patches = patches * lax.axis_size(AXES)
    start = lax.axis_index(AXES) * patches
    listed = (patch_near - start + patches) % all_patches
    itself = patches + jnp.arange(patches, dtype=jnp.int32)[:, None]
    listed = jnp.concatenate([itself, listed], axis=1)
    early = listed[:, :FIRST]
    layer, lefts, features = layer_part(layer_first, early, packed, wall_below, wall_above)

    def code(cell):
        row = (cell // all_cols - first_row + HALO) % all_rows
        col = (cell % all_cols - first_col + HALO) % all_cols
        return (row * 16 + col).reshape(-1)

    near_code, layer = lax.optimization_barrier((code(cell_near), layer))
    velocity, top, wall_raw = near_part(
        near_code,
        code(cell_to_patch),
        below,
        pos,
        above,
        left,
        right,
        cell_drag.reshape(-1, 1),
        (analysis, stiffness[None, :], synthesis),
    )
    top, late = lax.optimization_barrier((top, listed[:, FIRST:]))
    tops = over_all(top)
    [density_next] = layer_part(layer_second, late, packed, lefts, features, layer)
    per = cell_to_patch.shape[1]
    for stage in range(per):
        density_next = wall_part(stage, per, wall_raw, walls[0], density_next)
    moved = move_part(tops, pos, velocity)
    return jnp.transpose(moved, (0, 2, 1, 3)), jnp.transpose(density_next, (1, 0, 2))


def solution(mesh):
    patch = P(AXES, None, None)
    return jax.shard_map(
        body,
        mesh=mesh,
        in_specs=(
            P("cx", "cy", None, None),
            P("cx", "cy"),
            P("cx", "cy", None),
            P(),
            P(),
            P(),
            patch,
            patch,
            P(AXES, None),
            patch,
            P(AXES, None),
            P(AXES, None),
        ),
        out_specs=(P("cx", "cy", None, None), patch),
        check_vma=False,
    )
```

```python
import functools
import math

import jax
import jax.numpy as jnp
from jax import lax
from jax.experimental import pallas as pl
from jax.experimental.pallas import tpu as pltpu
from jax.sharding import PartitionSpec as P

HALO = 3
FIRST = 2
AXES = ("cx", "cy")
SOFT = 0.25
STOKES_SCALE = 1.0 / (8.0 * math.pi)
LAYER_SCALE = 3.0 / (4.0 * math.pi)
F32 = jnp.float32
BF16 = jnp.bfloat16
LANES = 128

GROUPS = ((0, 0), (0, 1), (1, 0), (0, 2), (2, 0), (1, 1), (1, 2), (2, 1))
STOKES_ROWS = 24
LAYER_ROWS = 32
TARGET_ROWS = 24


def parts(v):
    high = v.astype(BF16)
    rest = v - high.astype(F32)
    middle = rest.astype(BF16)
    low = (rest - middle.astype(F32)).astype(BF16)
    return high, middle, low


def target_rows(raw):
    split = [p.astype(F32) for p in parts(raw)]
    return jnp.concatenate([split[a] for a, _ in GROUPS], axis=0).astype(BF16)


def source_rows(raw):
    split = [p.astype(F32) for p in parts(raw)]
    return jnp.concatenate([split[b] for _, b in GROUPS], axis=0).astype(BF16)


def product(left, right):
    return lax.dot_general(left, right, (((0,), (0,)), ((), ())), preferred_element_type=F32)


def feature_rows(raw):
    return jnp.concatenate(parts(raw), axis=0)


def put_rows(ref, first, count, stride, value):
    for tile in range(ref.shape[0]):
        ref[tile, pl.ds(first, count, stride=stride), :] = value[
            :, tile * LANES : (tile + 1) * LANES
        ]


def get_rows(ref, first, count):
    return jnp.concatenate(
        [ref[tile, pl.ds(first, count), :] for tile in range(ref.shape[0])], axis=1
    )


def stokes_raw(ref, first, pos, force):
    square = pos[0] * pos[0] + pos[1] * pos[1] + pos[2] * pos[2]
    along = pos[0] * force[0] + pos[1] * force[1] + pos[2] * force[2]
    rows = [-2.0 * pos[0], -2.0 * pos[1], -2.0 * pos[2], square, jnp.ones_like(square)]
    rows += [jnp.zeros_like(square)] * 3
    rows += [force[0], force[1], force[2]]
    rows += [pos[j] * force[i] for j in range(3) for i in range(3)]
    rows += [square * force[i] + pos[i] * along for i in range(3)]
    rows += [jnp.zeros_like(square)]
    for k, row in enumerate(rows):
        put_rows(ref, first + k, 8, STOKES_ROWS, row)


def target_raw(ref, first, pos, stride=8):
    square = pos[0] * pos[0] + pos[1] * pos[1] + pos[2] * pos[2] + SOFT
    rows = [pos[0], pos[1], pos[2], jnp.ones_like(square), square]
    rows += [jnp.zeros_like(square)] * 3
    for k, row in enumerate(rows):
        put_rows(ref, first + k, 8, stride, row)


def stokes_moments(raw_ref, slots, target):
    total = None
    for slot in slots:
        base = pl.multiple_of(slot * STOKES_ROWS, 8)
        left = source_rows(get_rows(raw_ref, base, 8))
        square = product(left, target)
        root = lax.rsqrt(jnp.maximum(square, SOFT))
        factor = (root * root * root).astype(BF16)
        features = feature_rows(get_rows(raw_ref, base + 8, 16))
        part = jnp.dot(features, factor, preferred_element_type=F32)
        total = part if total is None else total + part
    return total[0:16] + total[16:32] + total[32:48]


def stokes_finish(pos, moments):
    m0 = moments[0:3]
    m1 = [[moments[3 + 3 * j + i] for i in range(3)] for j in range(3)]
    m2 = moments[12:15]
    square = pos[0] * pos[0] + pos[1] * pos[1] + pos[2] * pos[2] + 2.0 * SOFT
    along = pos[0] * m0[0] + pos[1] * m0[1] + pos[2] * m0[2]
    along = along - (m1[0][0] + m1[1][1] + m1[2][2])
    out = []
    for i in range(3):
        cross = sum(pos[j] * (2.0 * m1[j][i] + m1[i][j]) for j in range(3))
        out.append(square * m0[i] + m2[i] + pos[i] * along - cross)
    return out


def near_kernel(
    near_ref,
    wall_ref,
    below_ref,
    own_ref,
    above_ref,
    left_ref,
    right_ref,
    drag_ref,
    analysis_ref,
    stiffness_ref,
    synthesis_ref,
    velocity_ref,
    top_ref,
    wall_raw_ref,
    ext_ref,
    pos_ref,
    raw_ref,
    target_ref,
    moment_ref,
    first_ref,
    second_ref,
    sems,
):
    tables = [
        pltpu.make_async_copy(a, b, sems.at[k])
        for k, (a, b) in enumerate(((analysis_ref, first_ref), (synthesis_ref, second_ref)))
    ]
    for table in tables:
        table.start()
    rows, _, cols, points = own_ref.shape
    own = rows * cols
    near = near_ref.shape[0]
    wall = wall_ref.shape[0]
    slots = own + near + wall
    ext_ref[:, :, 0:HALO, :] = left_ref[...]
    inner = slice(HALO, HALO + cols)
    ext_ref[0:HALO, :, inner, :] = below_ref[rows - HALO :]
    ext_ref[HALO : HALO + rows, :, inner, :] = own_ref[...]
    ext_ref[HALO + rows :, :, inner, :] = above_ref[0:HALO]
    ext_ref[:, :, HALO + cols :, :] = right_ref[...]
    for r in range(rows):
        for d in range(3):
            pos_ref[d, r * cols : (r + 1) * cols, :] = own_ref[r, d]
    for i in range(near + wall):
        code = near_ref[i] if i < near else wall_ref[i - near]
        row = code // 16
        col = code % 16
        for d in range(3):
            pos_ref[d, own + i : own + i + 1, :] = ext_ref[row, d, pl.ds(col, 1), :]
    everything = [pos_ref[d] for d in range(3)]
    centred = [v - jnp.sum(v, axis=1, keepdims=True) * (1.0 / points) for v in everything]
    flat = jnp.concatenate(centred, axis=0).astype(BF16)
    tables[0].wait()
    coeff = jnp.dot(flat, first_ref[...], preferred_element_type=F32)
    scaled = (coeff * stiffness_ref[...]).astype(BF16)
    tables[1].wait()
    force = -jnp.dot(scaled, second_ref[...], preferred_element_type=F32)
    forces = [force[d * slots : (d + 1) * slots] for d in range(3)]
    for g in range((near + wall) // 8):
        a = own + 8 * g
        into, base = (raw_ref, 8 * g) if 8 * g < near else (wall_raw_ref, 8 * g - near)
        stokes_raw(
            into,
            base * STOKES_ROWS,
            [v[a : a + 8] for v in everything],
            [v[a : a + 8] for v in forces],
        )
    for g in range(own // 8):
        target_raw(target_ref, 64 * g, [v[8 * g : 8 * g + 8] for v in everything])

    def cell(c, carry):
        target = target_rows(get_rows(target_ref, pl.multiple_of(c * 8, 8), 8))
        per = near // own
        moments = stokes_moments(raw_ref, [c * per + k for k in range(per)], target)
        put_rows(moment_ref, c, 16, own, moments)
        return carry

    lax.fori_loop(0, own, cell, 0, unroll=2)
    moments = [get_rows(moment_ref, k * own, own) for k in range(15)]
    own_pos = [v[0:own] for v in everything]
    sums = stokes_finish(own_pos, moments)
    speed = jnp.zeros_like(sums[0])
    for d in range(3):
        velocity = drag_ref[...] * forces[d][0:own] + STOKES_SCALE * sums[d]
        speed = speed + velocity * velocity
        for r in range(rows):
            velocity_ref[r, d] = velocity[r * cols : (r + 1) * cols]
    top = jnp.sqrt(jnp.max(speed, axis=(0, 1), keepdims=True))
    top_ref[...] = jnp.broadcast_to(top, top_ref.shape)


def near_part(near_code, wall_code, below, pos, above, left, right, drag, tables):
    rows, _, cols, points = pos.shape
    own = rows * cols
    near, wall = near_code.shape[0], wall_code.shape[0]
    slots = own + near + wall
    tiles = points // LANES
    in_vmem = pl.BlockSpec(memory_space=pltpu.VMEM)
    in_smem = pl.BlockSpec(memory_space=pltpu.SMEM)
    in_hbm = pl.BlockSpec(memory_space=pl.ANY)
    pairs = own * points * (near // own) * points
    return pl.pallas_call(
        near_kernel,
        in_specs=[in_smem] * 2 + [in_vmem] * 6 + [in_hbm, in_vmem, in_hbm],
        out_specs=[in_vmem] * 3,
        out_shape=[
            jax.ShapeDtypeStruct((rows, 3, cols, points), F32),
            jax.ShapeDtypeStruct((8, LANES), F32),
            jax.ShapeDtypeStruct((tiles, wall * STOKES_ROWS, LANES), F32),
        ],
        scratch_shapes=[
            pltpu.VMEM((rows + 2 * HALO, 3, cols + 2 * HALO, points), F32),
            pltpu.VMEM((3, slots, points), F32),
            pltpu.VMEM((tiles, near * STOKES_ROWS, LANES), F32),
            pltpu.VMEM((tiles, own * 8, LANES), F32),
            pltpu.VMEM((tiles, own * 16, LANES), F32),
            pltpu.VMEM(tables[0].shape, BF16),
            pltpu.VMEM(tables[2].shape, BF16),
            pltpu.SemaphoreType.DMA((2,)),
        ],
        compiler_params=pltpu.CompilerParams(vmem_limit_bytes=50 * 2**20),
        cost_estimate=pl.CostEstimate(
            flops=1000 * pairs, bytes_accessed=8 * 2**20, transcendentals=pairs
        ),
        name="near",
    )(near_code, wall_code, below, pos, above, left, right, drag, *tables)


def wall_kernel(stage, per, raw_ref, pos_ref, layer_ref, out_ref, target_ref, moment_ref):
    patches = pos_ref.shape[1]
    pos = [pos_ref[d] for d in range(3)]
    target_raw(target_ref, 0, pos)

    def patch(p, carry):
        target = target_rows(get_rows(target_ref, pl.multiple_of(p * 8, 8), 8))
        moments = stokes_moments(raw_ref, [p * per + stage], target)
        put_rows(moment_ref, p, 16, patches, moments)
        return carry

    lax.fori_loop(0, patches, patch, 0, unroll=True)
    sums = stokes_finish(pos, [get_rows(moment_ref, k * patches, patches) for k in range(15)])
    for d in range(3):
        out_ref[d] = layer_ref[d] + (2.0 * STOKES_SCALE) * sums[d]


def wall_part(stage, per, raw, pos, layer):
    _, patches, points = pos.shape
    tiles = points // LANES
    in_vmem = pl.BlockSpec(memory_space=pltpu.VMEM)
    pairs = patches * raw.shape[0] * LANES * points
    return pl.pallas_call(
        functools.partial(wall_kernel, stage, per),
        in_specs=[in_vmem] * 3,
        out_specs=in_vmem,
        out_shape=jax.ShapeDtypeStruct(pos.shape, F32),
        scratch_shapes=[
            pltpu.VMEM((tiles, patches * 8, LANES), F32),
            pltpu.VMEM((tiles, patches * 16, LANES), F32),
        ],
        compiler_params=pltpu.CompilerParams(vmem_limit_bytes=24 * 2**20),
        cost_estimate=pl.CostEstimate(
            flops=1000 * pairs, bytes_accessed=2 * 2**20, transcendentals=pairs
        ),
        name=f"wall_{stage}",
    )(raw, pos, layer)


def layer_sums(listed_ref, own_ref, left_ref, feature_ref, target_ref, moment_ref):
    patches = own_ref.shape[1]
    x = [own_ref[d] for d in range(3)]
    target_raw(target_ref, 0, x, TARGET_ROWS)
    rows = [x[0] * x[0], x[1] * x[1], x[2] * x[2], x[0] * x[1], x[0] * x[2], x[1] * x[2]]
    rows += x + [jnp.ones_like(x[0])] + [jnp.zeros_like(x[0])] * 6
    for k, row in enumerate(rows):
        put_rows(target_ref, 8 + k, patches, TARGET_ROWS, row)

    def patch(p, carry):
        raw = get_rows(target_ref, pl.multiple_of(p * TARGET_ROWS, 8), TARGET_ROWS)
        near, form = target_rows(raw[0:8]), target_rows(raw[8:24])
        total = None
        for k in range(listed_ref.shape[1]):
            s = listed_ref[p, k]
            square = product(left_ref[s, 0:64], near)
            scalar = product(left_ref[s, 64:192], form)
            root = lax.rsqrt(jnp.maximum(square, SOFT))
            double = root * root
            scalar = (scalar * (double * double * root)).astype(BF16)
            part = jnp.dot(feature_ref[s], scalar, preferred_element_type=F32)
            total = part if total is None else total + part
        moments = total[0:8] + total[8:16] + total[16:24]
        put_rows(moment_ref, p, 8, patches, moments)
        return carry

    lax.fori_loop(0, patches, patch, 0, unroll=True)
    moments = [get_rows(moment_ref, k * patches, patches) for k in range(4)]
    return [(-2.0 * LAYER_SCALE) * (x[d] * moments[3] - moments[d]) for d in range(3)]


def layer_first(listed_ref, own_ref, before_ref, after_ref, out_ref, left_ref, feature_ref, raw_ref, target_ref, moment_ref):
    patches = own_ref.shape[1]
    for block, ref in enumerate((before_ref, own_ref, after_ref)):
        y = [ref[d] for d in range(3)]
        n = [ref[3 + d] for d in range(3)]
        v = [ref[6 + d] * ref[9] for d in range(3)]
        square = y[0] * y[0] + y[1] * y[1] + y[2] * y[2]
        along_n = y[0] * n[0] + y[1] * n[1] + y[2] * n[2]
        along_v = y[0] * v[0] + y[1] * v[1] + y[2] * v[2]
        one, zero = jnp.ones_like(square), jnp.zeros_like(square)
        rows = [-2.0 * y[0], -2.0 * y[1], -2.0 * y[2], square, one, zero, zero, zero]
        rows += [v[d] * n[d] for d in range(3)]
        rows += [v[a] * n[b] + v[b] * n[a] for a, b in ((0, 1), (0, 2), (1, 2))]
        rows += [-(v[d] * along_n + n[d] * along_v) for d in range(3)]
        rows += [along_v * along_n] + [zero] * 6
        rows += [y[0], y[1], y[2], one, zero, zero, zero, zero]
        for k, row in enumerate(rows):
            put_rows(raw_ref, block * patches * LAYER_ROWS + k, patches, LAYER_ROWS, row)

    def prepare(s, carry):
        raw = get_rows(raw_ref, pl.multiple_of(s * LAYER_ROWS, 8), LAYER_ROWS)
        left_ref[s, 0:64] = source_rows(raw[0:8])
        left_ref[s, 64:192] = source_rows(raw[8:24])
        split = [p.astype(F32) for p in parts(raw[24:32])]
        split.append(jnp.zeros_like(split[0]))
        feature_ref[s] = jnp.concatenate(split, axis=0).astype(BF16)
        return carry

    lax.fori_loop(0, 3 * patches, prepare, 0, unroll=4)
    sums = layer_sums(listed_ref, own_ref, left_ref, feature_ref, target_ref, moment_ref)
    for d in range(3):
        out_ref[d] = sums[d]


def layer_second(listed_ref, own_ref, left_ref, feature_ref, so_far_ref, out_ref, target_ref, moment_ref):
    sums = layer_sums(listed_ref, own_ref, left_ref, feature_ref, target_ref, moment_ref)
    for d in range(3):
        out_ref[d] = so_far_ref[d] + sums[d]


def layer_part(kernel, listed, *arrays):
    _, patches, points = arrays[0].shape
    tiles = points // LANES
    in_vmem = pl.BlockSpec(memory_space=pltpu.VMEM)
    pairs = patches * points * listed.shape[1] * points
    out_shape = [jax.ShapeDtypeStruct((3, patches, points), F32)]
    scratch = [
        pltpu.VMEM((tiles, patches * TARGET_ROWS, LANES), F32),
        pltpu.VMEM((tiles, patches * 8, LANES), F32),
    ]
    if kernel is layer_first:
        out_shape += [
            jax.ShapeDtypeStruct((3 * patches, 192, points), BF16),
            jax.ShapeDtypeStruct((3 * patches, 32, points), BF16),
        ]
        scratch.insert(0, pltpu.VMEM((tiles, 3 * patches * LAYER_ROWS, LANES), F32))
    return pl.pallas_call(
        kernel,
        in_specs=[pl.BlockSpec(memory_space=pltpu.SMEM)] + [in_vmem] * len(arrays),
        out_specs=[in_vmem] * len(out_shape),
        out_shape=out_shape,
        scratch_shapes=scratch,
        compiler_params=pltpu.CompilerParams(vmem_limit_bytes=24 * 2**20),
        cost_estimate=pl.CostEstimate(
            flops=1000 * pairs, bytes_accessed=2**20, transcendentals=pairs
        ),
        name=kernel.__name__,
    )(listed, *arrays)


def move_kernel(*refs):
    *tops, pos_ref, velocity_ref, out_ref = refs
    top = functools.reduce(jnp.maximum, [t[...] for t in tops])
    step = 1.0 / (top[0:1, 0:1] + 1e-06)
    rows, _, cols, _ = pos_ref.shape
    for r in range(rows):
        for d in range(3):
            out_ref[r, d] = pos_ref[r, d] + step * velocity_ref[r, d]


def move_part(tops, pos, velocity):
    in_vmem = pl.BlockSpec(memory_space=pltpu.VMEM)
    return pl.pallas_call(
        move_kernel,
        in_specs=[in_vmem] * (len(tops) + 2),
        out_specs=in_vmem,
        out_shape=jax.ShapeDtypeStruct(pos.shape, F32),
        compiler_params=pltpu.CompilerParams(vmem_limit_bytes=8 * 2**20),
        name="move",
    )(*tops, pos, velocity)


def neighbours(low, high, axis):
    size = lax.axis_size(axis)
    up = [(i, (i + 1) % size) for i in range(size)]
    down = [(b, a) for a, b in up]
    return lax.ppermute(high, axis, up), lax.ppermute(low, axis, down)


def rotations(outer, inner, along_outer):
    size = outer if along_outer else inner
    for turn in range(1, size):
        yield [
            (
                a * inner + b,
                (a + turn) % outer * inner + b if along_outer else a * inner + (b + turn) % inner,
            )
            for a in range(outer)
            for b in range(inner)
        ]


def over_all(value):
    values = [value]
    for axis, inner in (("cy", 2), ("cx", 4)):
        outer = lax.axis_size(axis) // inner
        for along_outer in (False, True):
            value = functools.reduce(jnp.maximum, values)
            values = [value] + [
                lax.ppermute(value, axis, pairs)
                for pairs in rotations(outer, inner, along_outer)
            ]
    return values


def body(
    cell_pos,
    cell_drag,
    cell_near,
    analysis,
    stiffness,
    synthesis,
    wall_pos,
    wall_normal,
    wall_weight,
    density,
    patch_near,
    cell_to_patch,
):
    rows, cols = cell_pos.shape[:2]
    all_rows = rows * lax.axis_size("cx")
    all_cols = cols * lax.axis_size("cy")
    first_row = lax.axis_index("cx") * rows
    first_col = lax.axis_index("cy") * cols

    pos = jnp.transpose(cell_pos, (0, 2, 1, 3))
    walls = [jnp.transpose(v, (1, 0, 2)) for v in (wall_pos, wall_normal, density)]
    packed = jnp.concatenate(walls + [wall_weight[None]], axis=0)

    below, above = neighbours(pos, pos, "cx")
    below, above, packed = lax.optimization_barrier((below, above, packed))
    wall_below, wall_above = neighbours(packed, packed, AXES)
    strips = [v[:, :, c : c + HALO] for c in (0, cols - HALO) for v in (below[rows - HALO :], pos, above[:HALO])]
    left, right = neighbours(
        jnp.concatenate(strips[:3], axis=0), jnp.concatenate(strips[3:], axis=0), "cy"
    )

    patches = wall_pos.shape[0]
    all_patches = patches * lax.axis_size(AXES)
    start = lax.axis_index(AXES) * patches
    listed = (patch_near - start + patches) % all_patches
    itself = patches + jnp.arange(patches, dtype=jnp.int32)[:, None]
    listed = jnp.concatenate([itself, listed], axis=1)
    early = listed[:, :FIRST]
    layer, lefts, features = layer_part(layer_first, early, packed, wall_below, wall_above)

    def code(cell):
        row = (cell // all_cols - first_row + HALO) % all_rows
        col = (cell % all_cols - first_col + HALO) % all_cols
        return (row * 16 + col).reshape(-1)

    near_code, layer = lax.optimization_barrier((code(cell_near), layer))
    velocity, top, wall_raw = near_part(
        near_code,
        code(cell_to_patch),
        below,
        pos,
        above,
        left,
        right,
        cell_drag.reshape(-1, 1),
        (analysis, stiffness[None, :], synthesis),
    )
    top, late = lax.optimization_barrier((top, listed[:, FIRST:]))
    tops = over_all(top)
    [density_next] = layer_part(layer_second, late, packed, lefts, features, layer)
    per = cell_to_patch.shape[1]
    for stage in range(per):
        density_next = wall_part(stage, per, wall_raw, walls[0], density_next)
    moved = move_part(tops, pos, velocity)
    return jnp.transpose(moved, (0, 2, 1, 3)), jnp.transpose(density_next, (1, 0, 2))


def solution(mesh):
    patch = P(AXES, None, None)
    return jax.shard_map(
        body,
        mesh=mesh,
        in_specs=(
            P("cx", "cy", None, None),
            P("cx", "cy"),
            P("cx", "cy", None),
            P(),
            P(),
            P(),
            patch,
            patch,
            P(AXES, None),
            patch,
            P(AXES, None),
            P(AXES, None),
        ),
        out_specs=(P("cx", "cy", None, None), patch),
        check_vma=False,
    )
```

```python
import functools
import math

import jax
import jax.numpy as jnp
from jax import lax
from jax.experimental import pallas as pl
from jax.experimental.pallas import tpu as pltpu
from jax.sharding import PartitionSpec as P

HALO = 3
FIRST = 2
AXES = ("cx", "cy")
SOFT = 0.25
STOKES_SCALE = 1.0 / (8.0 * math.pi)
LAYER_SCALE = 3.0 / (4.0 * math.pi)
F32 = jnp.float32
BF16 = jnp.bfloat16
LANES = 128

GROUPS = ((0, 0), (0, 1), (1, 0), (0, 2), (2, 0), (1, 1), (1, 2), (2, 1))
STOKES_ROWS = 24
LAYER_ROWS = 32
TARGET_ROWS = 24


def parts(v):
    high = v.astype(BF16)
    rest = v - high.astype(F32)
    middle = rest.astype(BF16)
    low = (rest - middle.astype(F32)).astype(BF16)
    return high, middle, low


def target_rows(raw):
    split = [p.astype(F32) for p in parts(raw)]
    return jnp.concatenate([split[a] for a, _ in GROUPS], axis=0).astype(BF16)


def source_rows(raw):
    split = [p.astype(F32) for p in parts(raw)]
    return jnp.concatenate([split[b] for _, b in GROUPS], axis=0).astype(BF16)


def product(left, right):
    return lax.dot_general(left, right, (((0,), (0,)), ((), ())), preferred_element_type=F32)


def feature_rows(raw):
    return jnp.concatenate(parts(raw), axis=0)


def put_rows(ref, first, count, stride, value):
    for tile in range(ref.shape[0]):
        ref[tile, pl.ds(first, count, stride=stride), :] = value[
            :, tile * LANES : (tile + 1) * LANES
        ]


def get_rows(ref, first, count):
    return jnp.concatenate(
        [ref[tile, pl.ds(first, count), :] for tile in range(ref.shape[0])], axis=1
    )


def stokes_raw(ref, first, pos, force):
    square = pos[0] * pos[0] + pos[1] * pos[1] + pos[2] * pos[2]
    along = pos[0] * force[0] + pos[1] * force[1] + pos[2] * force[2]
    rows = [-2.0 * pos[0], -2.0 * pos[1], -2.0 * pos[2], square, jnp.ones_like(square)]
    rows += [jnp.zeros_like(square)] * 3
    rows += [force[0], force[1], force[2]]
    rows += [pos[j] * force[i] for j in range(3) for i in range(3)]
    rows += [square * force[i] + pos[i] * along for i in range(3)]
    rows += [jnp.zeros_like(square)]
    for k, row in enumerate(rows):
        put_rows(ref, first + k, 8, STOKES_ROWS, row)


def target_raw(ref, first, pos, stride=8):
    square = pos[0] * pos[0] + pos[1] * pos[1] + pos[2] * pos[2] + SOFT
    rows = [pos[0], pos[1], pos[2], jnp.ones_like(square), square]
    rows += [jnp.zeros_like(square)] * 3
    for k, row in enumerate(rows):
        put_rows(ref, first + k, 8, stride, row)


def stokes_moments(raw_ref, slots, target):
    total = None
    for slot in slots:
        base = pl.multiple_of(slot * STOKES_ROWS, 8)
        left = source_rows(get_rows(raw_ref, base, 8))
        square = product(left, target)
        root = lax.rsqrt(jnp.maximum(square, SOFT))
        factor = (root * root * root).astype(BF16)
        features = feature_rows(get_rows(raw_ref, base + 8, 16))
        part = jnp.dot(features, factor, preferred_element_type=F32)
        total = part if total is None else total + part
    return total[0:16] + total[16:32] + total[32:48]


def stokes_finish(pos, moments):
    m0 = moments[0:3]
    m1 = [[moments[3 + 3 * j + i] for i in range(3)] for j in range(3)]
    m2 = moments[12:15]
    square = pos[0] * pos[0] + pos[1] * pos[1] + pos[2] * pos[2] + 2.0 * SOFT
    along = pos[0] * m0[0] + pos[1] * m0[1] + pos[2] * m0[2]
    along = along - (m1[0][0] + m1[1][1] + m1[2][2])
    out = []
    for i in range(3):
        cross = sum(pos[j] * (2.0 * m1[j][i] + m1[i][j]) for j in range(3))
        out.append(square * m0[i] + m2[i] + pos[i] * along - cross)
    return out


def near_kernel(
    near_ref,
    wall_ref,
    below_ref,
    own_ref,
    above_ref,
    left_ref,
    right_ref,
    drag_ref,
    analysis_ref,
    stiffness_ref,
    synthesis_ref,
    velocity_ref,
    top_ref,
    wall_raw_ref,
    ext_ref,
    pos_ref,
    raw_ref,
    target_ref,
    moment_ref,
    first_ref,
    second_ref,
    sems,
):
    tables = [
        pltpu.make_async_copy(a, b, sems.at[k])
        for k, (a, b) in enumerate(((analysis_ref, first_ref), (synthesis_ref, second_ref)))
    ]
    for table in tables:
        table.start()
    rows, _, cols, points = own_ref.shape
    own = rows * cols
    near = near_ref.shape[0]
    wall = wall_ref.shape[0]
    slots = own + near + wall
    ext_ref[:, :, 0:HALO, :] = left_ref[...]
    inner = slice(HALO, HALO + cols)
    ext_ref[0:HALO, :, inner, :] = below_ref[rows - HALO :]
    ext_ref[HALO : HALO + rows, :, inner, :] = own_ref[...]
    ext_ref[HALO + rows :, :, inner, :] = above_ref[0:HALO]
    ext_ref[:, :, HALO + cols :, :] = right_ref[...]
    for r in range(rows):
        for d in range(3):
            pos_ref[d, r * cols : (r + 1) * cols, :] = own_ref[r, d]
    for i in range(near + wall):
        code = near_ref[i] if i < near else wall_ref[i - near]
        row = code // 16
        col = code % 16
        for d in range(3):
            pos_ref[d, own + i : own + i + 1, :] = ext_ref[row, d, pl.ds(col, 1), :]
    everything = [pos_ref[d] for d in range(3)]
    centred = [v - jnp.sum(v, axis=1, keepdims=True) * (1.0 / points) for v in everything]
    flat = jnp.concatenate(centred, axis=0).astype(BF16)
    tables[0].wait()
    coeff = jnp.dot(flat, first_ref[...], preferred_element_type=F32)
    scaled = (coeff * stiffness_ref[...]).astype(BF16)
    tables[1].wait()
    force = -jnp.dot(scaled, second_ref[...], preferred_element_type=F32)
    forces = [force[d * slots : (d + 1) * slots] for d in range(3)]
    for g in range((near + wall) // 8):
        a = own + 8 * g
        into, base = (raw_ref, 8 * g) if 8 * g < near else (wall_raw_ref, 8 * g - near)
        stokes_raw(
            into,
            base * STOKES_ROWS,
            [v[a : a + 8] for v in everything],
            [v[a : a + 8] for v in forces],
        )
    for g in range(own // 8):
        target_raw(target_ref, 64 * g, [v[8 * g : 8 * g + 8] for v in everything])

    def cell(c, carry):
        target = target_rows(get_rows(target_ref, pl.multiple_of(c * 8, 8), 8))
        per = near // own
        moments = stokes_moments(raw_ref, [c * per + k for k in range(per)], target)
        put_rows(moment_ref, c, 16, own, moments)
        return carry

    lax.fori_loop(0, own, cell, 0, unroll=2)
    moments = [get_rows(moment_ref, k * own, own) for k in range(15)]
    own_pos = [v[0:own] for v in everything]
    sums = stokes_finish(own_pos, moments)
    speed = jnp.zeros_like(sums[0])
    for d in range(3):
        velocity = drag_ref[...] * forces[d][0:own] + STOKES_SCALE * sums[d]
        speed = speed + velocity * velocity
        for r in range(rows):
            velocity_ref[r, d] = velocity[r * cols : (r + 1) * cols]
    top = jnp.sqrt(jnp.max(speed, axis=(0, 1), keepdims=True))
    top_ref[...] = jnp.broadcast_to(top, top_ref.shape)


def near_part(near_code, wall_code, below, pos, above, left, right, drag, tables):
    rows, _, cols, points = pos.shape
    own = rows * cols
    near, wall = near_code.shape[0], wall_code.shape[0]
    slots = own + near + wall
    tiles = points // LANES
    in_vmem = pl.BlockSpec(memory_space=pltpu.VMEM)
    in_smem = pl.BlockSpec(memory_space=pltpu.SMEM)
    in_hbm = pl.BlockSpec(memory_space=pl.ANY)
    pairs = own * points * (near // own) * points
    return pl.pallas_call(
        near_kernel,
        in_specs=[in_smem] * 2 + [in_vmem] * 6 + [in_hbm, in_vmem, in_hbm],
        out_specs=[in_vmem] * 3,
        out_shape=[
            jax.ShapeDtypeStruct((rows, 3, cols, points), F32),
            jax.ShapeDtypeStruct((8, LANES), F32),
            jax.ShapeDtypeStruct((tiles, wall * STOKES_ROWS, LANES), F32),
        ],
        scratch_shapes=[
            pltpu.VMEM((rows + 2 * HALO, 3, cols + 2 * HALO, points), F32),
            pltpu.VMEM((3, slots, points), F32),
            pltpu.VMEM((tiles, near * STOKES_ROWS, LANES), F32),
            pltpu.VMEM((tiles, own * 8, LANES), F32),
            pltpu.VMEM((tiles, own * 16, LANES), F32),
            pltpu.VMEM(tables[0].shape, BF16),
            pltpu.VMEM(tables[2].shape, BF16),
            pltpu.SemaphoreType.DMA((2,)),
        ],
        compiler_params=pltpu.CompilerParams(vmem_limit_bytes=50 * 2**20),
        cost_estimate=pl.CostEstimate(
            flops=1000 * pairs, bytes_accessed=8 * 2**20, transcendentals=pairs
        ),
        name="near",
    )(near_code, wall_code, below, pos, above, left, right, drag, *tables)


def wall_kernel(stage, per, raw_ref, pos_ref, layer_ref, out_ref, target_ref, moment_ref):
    patches = pos_ref.shape[1]
    pos = [pos_ref[d] for d in range(3)]
    target_raw(target_ref, 0, pos)

    def patch(p, carry):
        target = target_rows(get_rows(target_ref, pl.multiple_of(p * 8, 8), 8))
        moments = stokes_moments(raw_ref, [p * per + stage], target)
        put_rows(moment_ref, p, 16, patches, moments)
        return carry

    lax.fori_loop(0, patches, patch, 0, unroll=True)
    sums = stokes_finish(pos, [get_rows(moment_ref, k * patches, patches) for k in range(15)])
    for d in range(3):
        out_ref[d] = layer_ref[d] + (2.0 * STOKES_SCALE) * sums[d]


def wall_part(stage, per, raw, pos, layer):
    _, patches, points = pos.shape
    tiles = points // LANES
    in_vmem = pl.BlockSpec(memory_space=pltpu.VMEM)
    pairs = patches * raw.shape[0] * LANES * points
    return pl.pallas_call(
        functools.partial(wall_kernel, stage, per),
        in_specs=[in_vmem] * 3,
        out_specs=in_vmem,
        out_shape=jax.ShapeDtypeStruct(pos.shape, F32),
        scratch_shapes=[
            pltpu.VMEM((tiles, patches * 8, LANES), F32),
            pltpu.VMEM((tiles, patches * 16, LANES), F32),
        ],
        compiler_params=pltpu.CompilerParams(vmem_limit_bytes=24 * 2**20),
        cost_estimate=pl.CostEstimate(
            flops=1000 * pairs, bytes_accessed=2 * 2**20, transcendentals=pairs
        ),
        name=f"wall_{stage}",
    )(raw, pos, layer)


def layer_sums(listed_ref, own_ref, left_ref, feature_ref, target_ref, moment_ref):
    patches = own_ref.shape[1]
    x = [own_ref[d] for d in range(3)]
    target_raw(target_ref, 0, x, TARGET_ROWS)
    rows = [x[0] * x[0], x[1] * x[1], x[2] * x[2], x[0] * x[1], x[0] * x[2], x[1] * x[2]]
    rows += x + [jnp.ones_like(x[0])] + [jnp.zeros_like(x[0])] * 6
    for k, row in enumerate(rows):
        put_rows(target_ref, 8 + k, patches, TARGET_ROWS, row)

    def patch(p, carry):
        raw = get_rows(target_ref, pl.multiple_of(p * TARGET_ROWS, 8), TARGET_ROWS)
        near, form = target_rows(raw[0:8]), target_rows(raw[8:24])
        total = None
        for k in range(listed_ref.shape[1]):
            s = listed_ref[p, k]
            square = product(left_ref[s, 0:64], near)
            scalar = product(left_ref[s, 64:192], form)
            root = lax.rsqrt(jnp.maximum(square, SOFT))
            double = root * root
            scalar = (scalar * (double * double * root)).astype(BF16)
            part = jnp.dot(feature_ref[s], scalar, preferred_element_type=F32)
            total = part if total is None else total + part
        moments = total[0:8] + total[8:16] + total[16:24]
        put_rows(moment_ref, p, 8, patches, moments)
        return carry

    lax.fori_loop(0, patches, patch, 0, unroll=True)
    moments = [get_rows(moment_ref, k * patches, patches) for k in range(4)]
    return [(-2.0 * LAYER_SCALE) * (x[d] * moments[3] - moments[d]) for d in range(3)]


def layer_first(listed_ref, own_ref, before_ref, after_ref, out_ref, left_ref, feature_ref, raw_ref, target_ref, moment_ref):
    patches = own_ref.shape[1]
    for block, ref in enumerate((before_ref, own_ref, after_ref)):
        y = [ref[d] for d in range(3)]
        n = [ref[3 + d] for d in range(3)]
        v = [ref[6 + d] * ref[9] for d in range(3)]
        square = y[0] * y[0] + y[1] * y[1] + y[2] * y[2]
        along_n = y[0] * n[0] + y[1] * n[1] + y[2] * n[2]
        along_v = y[0] * v[0] + y[1] * v[1] + y[2] * v[2]
        one, zero = jnp.ones_like(square), jnp.zeros_like(square)
        rows = [-2.0 * y[0], -2.0 * y[1], -2.0 * y[2], square, one, zero, zero, zero]
        rows += [v[d] * n[d] for d in range(3)]
        rows += [v[a] * n[b] + v[b] * n[a] for a, b in ((0, 1), (0, 2), (1, 2))]
        rows += [-(v[d] * along_n + n[d] * along_v) for d in range(3)]
        rows += [along_v * along_n] + [zero] * 6
        rows += [y[0], y[1], y[2], one, zero, zero, zero, zero]
        for k, row in enumerate(rows):
            put_rows(raw_ref, block * patches * LAYER_ROWS + k, patches, LAYER_ROWS, row)

    def prepare(s, carry):
        raw = get_rows(raw_ref, pl.multiple_of(s * LAYER_ROWS, 8), LAYER_ROWS)
        left_ref[s, 0:64] = source_rows(raw[0:8])
        left_ref[s, 64:192] = source_rows(raw[8:24])
        split = [p.astype(F32) for p in parts(raw[24:32])]
        split.append(jnp.zeros_like(split[0]))
        feature_ref[s] = jnp.concatenate(split, axis=0).astype(BF16)
        return carry

    lax.fori_loop(0, 3 * patches, prepare, 0, unroll=4)
    sums = layer_sums(listed_ref, own_ref, left_ref, feature_ref, target_ref, moment_ref)
    for d in range(3):
        out_ref[d] = sums[d]


def layer_second(listed_ref, own_ref, left_ref, feature_ref, so_far_ref, out_ref, target_ref, moment_ref):
    sums = layer_sums(listed_ref, own_ref, left_ref, feature_ref, target_ref, moment_ref)
    for d in range(3):
        out_ref[d] = so_far_ref[d] + sums[d]


def layer_part(kernel, listed, *arrays):
    _, patches, points = arrays[0].shape
    tiles = points // LANES
    in_vmem = pl.BlockSpec(memory_space=pltpu.VMEM)
    pairs = patches * points * listed.shape[1] * points
    out_shape = [jax.ShapeDtypeStruct((3, patches, points), F32)]
    scratch = [
        pltpu.VMEM((tiles, patches * TARGET_ROWS, LANES), F32),
        pltpu.VMEM((tiles, patches * 8, LANES), F32),
    ]
    if kernel is layer_first:
        out_shape += [
            jax.ShapeDtypeStruct((3 * patches, 192, points), BF16),
            jax.ShapeDtypeStruct((3 * patches, 32, points), BF16),
        ]
        scratch.insert(0, pltpu.VMEM((tiles, 3 * patches * LAYER_ROWS, LANES), F32))
    return pl.pallas_call(
        kernel,
        in_specs=[pl.BlockSpec(memory_space=pltpu.SMEM)] + [in_vmem] * len(arrays),
        out_specs=[in_vmem] * len(out_shape),
        out_shape=out_shape,
        scratch_shapes=scratch,
        compiler_params=pltpu.CompilerParams(vmem_limit_bytes=24 * 2**20),
        cost_estimate=pl.CostEstimate(
            flops=1000 * pairs, bytes_accessed=2**20, transcendentals=pairs
        ),
        name=kernel.__name__,
    )(listed, *arrays)


def move_kernel(*refs):
    *tops, pos_ref, velocity_ref, out_ref = refs
    top = functools.reduce(jnp.maximum, [t[...] for t in tops])
    step = 1.0 / (top[0:1, 0:1] + 1e-06)
    rows, _, cols, _ = pos_ref.shape
    for r in range(rows):
        for d in range(3):
            out_ref[r, d] = pos_ref[r, d] + step * velocity_ref[r, d]


def move_part(tops, pos, velocity):
    in_vmem = pl.BlockSpec(memory_space=pltpu.VMEM)
    return pl.pallas_call(
        move_kernel,
        in_specs=[in_vmem] * (len(tops) + 2),
        out_specs=in_vmem,
        out_shape=jax.ShapeDtypeStruct(pos.shape, F32),
        compiler_params=pltpu.CompilerParams(vmem_limit_bytes=8 * 2**20),
        name="move",
    )(*tops, pos, velocity)


def neighbours(low, high, axis):
    size = lax.axis_size(axis)
    up = [(i, (i + 1) % size) for i in range(size)]
    down = [(b, a) for a, b in up]
    return lax.ppermute(high, axis, up), lax.ppermute(low, axis, down)


def rotations(outer, inner, along_outer):
    size = outer if along_outer else inner
    for turn in range(1, size):
        yield [
            (
                a * inner + b,
                (a + turn) % outer * inner + b if along_outer else a * inner + (b + turn) % inner,
            )
            for a in range(outer)
            for b in range(inner)
        ]


def over_all(value):
    values = [value]
    for axis, inner in (("cy", 2), ("cx", 4)):
        outer = lax.axis_size(axis) // inner
        for along_outer in (False, True):
            value = functools.reduce(jnp.maximum, values)
            values = [value] + [
                lax.ppermute(value, axis, pairs)
                for pairs in rotations(outer, inner, along_outer)
            ]
    return values


def body(
    cell_pos,
    cell_drag,
    cell_near,
    analysis,
    stiffness,
    synthesis,
    wall_pos,
    wall_normal,
    wall_weight,
    density,
    patch_near,
    cell_to_patch,
):
    rows, cols = cell_pos.shape[:2]
    all_rows = rows * lax.axis_size("cx")
    all_cols = cols * lax.axis_size("cy")
    first_row = lax.axis_index("cx") * rows
    first_col = lax.axis_index("cy") * cols

    pos = jnp.transpose(cell_pos, (0, 2, 1, 3))
    walls = [jnp.transpose(v, (1, 0, 2)) for v in (wall_pos, wall_normal, density)]
    packed = jnp.concatenate(walls + [wall_weight[None]], axis=0)

    below, above = neighbours(pos, pos, "cx")
    own_strips = pos[:, :, :HALO], pos[:, :, cols - HALO :]
    packed, own_strips = lax.optimization_barrier((packed, own_strips))
    wall_below, wall_above = neighbours(packed, packed, AXES)
    low, high = (
        jnp.concatenate([below[rows - HALO :, :, c : c + HALO], own, above[:HALO, :, c : c + HALO]])
        for c, own in zip((0, cols - HALO), own_strips)
    )
    left, right = neighbours(low, high, "cy")

    patches = wall_pos.shape[0]
    all_patches = patches * lax.axis_size(AXES)
    start = lax.axis_index(AXES) * patches
    listed = (patch_near - start + patches) % all_patches
    itself = patches + jnp.arange(patches, dtype=jnp.int32)[:, None]
    listed = jnp.concatenate([itself, listed], axis=1)
    early = listed[:, :FIRST]
    layer, lefts, features = layer_part(layer_first, early, packed, wall_below, wall_above)

    def code(cell):
        row = (cell // all_cols - first_row + HALO) % all_rows
        col = (cell % all_cols - first_col + HALO) % all_cols
        return (row * 16 + col).reshape(-1)

    near_code, layer = lax.optimization_barrier((code(cell_near), layer))
    velocity, top, wall_raw = near_part(
        near_code,
        code(cell_to_patch),
        below,
        pos,
        above,
        left,
        right,
        cell_drag.reshape(-1, 1),
        (analysis, stiffness[None, :], synthesis),
    )
    top, late = lax.optimization_barrier((top, listed[:, FIRST:]))
    tops = over_all(top)
    [density_next] = layer_part(layer_second, late, packed, lefts, features, layer)
    per = cell_to_patch.shape[1]
    for stage in range(per):
        density_next = wall_part(stage, per, wall_raw, walls[0], density_next)
    moved = move_part(tops, pos, velocity)
    return jnp.transpose(moved, (0, 2, 1, 3)), jnp.transpose(density_next, (1, 0, 2))


def solution(mesh):
    patch = P(AXES, None, None)
    return jax.shard_map(
        body,
        mesh=mesh,
        in_specs=(
            P("cx", "cy", None, None),
            P("cx", "cy"),
            P("cx", "cy", None),
            P(),
            P(),
            P(),
            patch,
            patch,
            P(AXES, None),
            patch,
            P(AXES, None),
            P(AXES, None),
        ),
        out_specs=(P("cx", "cy", None, None), patch),
        check_vma=False,
    )
```

```python
import functools
import math

import jax
import jax.numpy as jnp
from jax import lax
from jax.experimental import pallas as pl
from jax.experimental.pallas import tpu as pltpu
from jax.sharding import PartitionSpec as P

HALO = 3
AXES = ("cx", "cy")
SOFT = 0.25
STOKES_SCALE = 1.0 / (8.0 * math.pi)
LAYER_SCALE = 3.0 / (4.0 * math.pi)
F32 = jnp.float32
BF16 = jnp.bfloat16
LANES = 128

GROUPS = ((0, 0), (0, 1), (1, 0), (0, 2), (2, 0), (1, 1), (1, 2), (2, 1))
STOKES_ROWS = 24
LAYER_ROWS = 32
TARGET_ROWS = 24


def parts(v):
    high = v.astype(BF16)
    rest = v - high.astype(F32)
    middle = rest.astype(BF16)
    low = (rest - middle.astype(F32)).astype(BF16)
    return high, middle, low


def target_rows(raw):
    split = [p.astype(F32) for p in parts(raw)]
    return jnp.concatenate([split[a] for a, _ in GROUPS], axis=0).astype(BF16)


def source_rows(raw):
    split = [p.astype(F32) for p in parts(raw)]
    return jnp.concatenate([split[b] for _, b in GROUPS], axis=0).astype(BF16)


def product(left, right):
    return lax.dot_general(left, right, (((0,), (0,)), ((), ())), preferred_element_type=F32)


def feature_rows(raw):
    return jnp.concatenate(parts(raw), axis=0)


def put_rows(ref, first, count, stride, value):
    for tile in range(ref.shape[0]):
        ref[tile, pl.ds(first, count, stride=stride), :] = value[
            :, tile * LANES : (tile + 1) * LANES
        ]


def get_rows(ref, first, count):
    return jnp.concatenate(
        [ref[tile, pl.ds(first, count), :] for tile in range(ref.shape[0])], axis=1
    )


def stokes_raw(ref, first, pos, force):
    square = pos[0] * pos[0] + pos[1] * pos[1] + pos[2] * pos[2]
    along = pos[0] * force[0] + pos[1] * force[1] + pos[2] * force[2]
    rows = [-2.0 * pos[0], -2.0 * pos[1], -2.0 * pos[2], square, jnp.ones_like(square)]
    rows += [jnp.zeros_like(square)] * 3
    rows += [force[0], force[1], force[2]]
    rows += [pos[j] * force[i] for j in range(3) for i in range(3)]
    rows += [square * force[i] + pos[i] * along for i in range(3)]
    rows += [jnp.zeros_like(square)]
    for k, row in enumerate(rows):
        put_rows(ref, first + k, 8, STOKES_ROWS, row)


def target_raw(ref, first, pos, stride=8):
    square = pos[0] * pos[0] + pos[1] * pos[1] + pos[2] * pos[2] + SOFT
    rows = [pos[0], pos[1], pos[2], jnp.ones_like(square), square]
    rows += [jnp.zeros_like(square)] * 3
    for k, row in enumerate(rows):
        put_rows(ref, first + k, 8, stride, row)


def stokes_moments(raw_ref, slots, target):
    total = None
    for slot in slots:
        base = pl.multiple_of(slot * STOKES_ROWS, 8)
        left = source_rows(get_rows(raw_ref, base, 8))
        square = product(left, target)
        root = lax.rsqrt(jnp.maximum(square, SOFT))
        factor = (root * root * root).astype(BF16)
        features = feature_rows(get_rows(raw_ref, base + 8, 16))
        part = jnp.dot(features, factor, preferred_element_type=F32)
        total = part if total is None else total + part
    return total[0:16] + total[16:32] + total[32:48]


def stokes_finish(pos, moments):
    m0 = moments[0:3]
    m1 = [[moments[3 + 3 * j + i] for i in range(3)] for j in range(3)]
    m2 = moments[12:15]
    square = pos[0] * pos[0] + pos[1] * pos[1] + pos[2] * pos[2] + 2.0 * SOFT
    along = pos[0] * m0[0] + pos[1] * m0[1] + pos[2] * m0[2]
    along = along - (m1[0][0] + m1[1][1] + m1[2][2])
    out = []
    for i in range(3):
        cross = sum(pos[j] * (2.0 * m1[j][i] + m1[i][j]) for j in range(3))
        out.append(square * m0[i] + m2[i] + pos[i] * along - cross)
    return out


def near_kernel(
    near_ref,
    wall_ref,
    below_ref,
    own_ref,
    above_ref,
    left_ref,
    right_ref,
    drag_ref,
    analysis_ref,
    stiffness_ref,
    synthesis_ref,
    velocity_ref,
    top_ref,
    wall_raw_ref,
    ext_ref,
    pos_ref,
    raw_ref,
    target_ref,
    moment_ref,
    first_ref,
    second_ref,
    sems,
):
    tables = [
        pltpu.make_async_copy(a, b, sems.at[k])
        for k, (a, b) in enumerate(((analysis_ref, first_ref), (synthesis_ref, second_ref)))
    ]
    for table in tables:
        table.start()
    rows, _, cols, points = own_ref.shape
    own = rows * cols
    near = near_ref.shape[0]
    wall = wall_ref.shape[0]
    slots = own + near + wall
    ext_ref[:, :, 0:HALO, :] = left_ref[...]
    inner = slice(HALO, HALO + cols)
    ext_ref[0:HALO, :, inner, :] = below_ref[rows - HALO :]
    ext_ref[HALO : HALO + rows, :, inner, :] = own_ref[...]
    ext_ref[HALO + rows :, :, inner, :] = above_ref[0:HALO]
    ext_ref[:, :, HALO + cols :, :] = right_ref[...]
    for r in range(rows):
        for d in range(3):
            pos_ref[d, r * cols : (r + 1) * cols, :] = own_ref[r, d]
    for i in range(near + wall):
        code = near_ref[i] if i < near else wall_ref[i - near]
        row = code // 16
        col = code % 16
        for d in range(3):
            pos_ref[d, own + i : own + i + 1, :] = ext_ref[row, d, pl.ds(col, 1), :]
    everything = [pos_ref[d] for d in range(3)]
    centred = [v - jnp.sum(v, axis=1, keepdims=True) * (1.0 / points) for v in everything]
    flat = jnp.concatenate(centred, axis=0).astype(BF16)
    tables[0].wait()
    coeff = jnp.dot(flat, first_ref[...], preferred_element_type=F32)
    scaled = (coeff * stiffness_ref[...]).astype(BF16)
    tables[1].wait()
    force = -jnp.dot(scaled, second_ref[...], preferred_element_type=F32)
    forces = [force[d * slots : (d + 1) * slots] for d in range(3)]
    for g in range((near + wall) // 8):
        a = own + 8 * g
        into, base = (raw_ref, 8 * g) if 8 * g < near else (wall_raw_ref, 8 * g - near)
        stokes_raw(
            into,
            base * STOKES_ROWS,
            [v[a : a + 8] for v in everything],
            [v[a : a + 8] for v in forces],
        )
    for g in range(own // 8):
        target_raw(target_ref, 64 * g, [v[8 * g : 8 * g + 8] for v in everything])

    def cell(c, carry):
        target = target_rows(get_rows(target_ref, pl.multiple_of(c * 8, 8), 8))
        per = near // own
        moments = stokes_moments(raw_ref, [c * per + k for k in range(per)], target)
        put_rows(moment_ref, c, 16, own, moments)
        return carry

    lax.fori_loop(0, own, cell, 0, unroll=2)
    moments = [get_rows(moment_ref, k * own, own) for k in range(15)]
    own_pos = [v[0:own] for v in everything]
    sums = stokes_finish(own_pos, moments)
    speed = jnp.zeros_like(sums[0])
    for d in range(3):
        velocity = drag_ref[...] * forces[d][0:own] + STOKES_SCALE * sums[d]
        speed = speed + velocity * velocity
        for r in range(rows):
            velocity_ref[r, d] = velocity[r * cols : (r + 1) * cols]
    top = jnp.sqrt(jnp.max(speed, axis=(0, 1), keepdims=True))
    top_ref[...] = jnp.broadcast_to(top, top_ref.shape)


def near_part(near_code, wall_code, below, pos, above, left, right, drag, tables):
    rows, _, cols, points = pos.shape
    own = rows * cols
    near, wall = near_code.shape[0], wall_code.shape[0]
    slots = own + near + wall
    tiles = points // LANES
    in_vmem = pl.BlockSpec(memory_space=pltpu.VMEM)
    in_smem = pl.BlockSpec(memory_space=pltpu.SMEM)
    in_hbm = pl.BlockSpec(memory_space=pl.ANY)
    pairs = own * points * (near // own) * points
    return pl.pallas_call(
        near_kernel,
        in_specs=[in_smem] * 2 + [in_vmem] * 6 + [in_hbm, in_vmem, in_hbm],
        out_specs=[in_vmem] * 3,
        out_shape=[
            jax.ShapeDtypeStruct((rows, 3, cols, points), F32),
            jax.ShapeDtypeStruct((8, LANES), F32),
            jax.ShapeDtypeStruct((tiles, wall * STOKES_ROWS, LANES), F32),
        ],
        scratch_shapes=[
            pltpu.VMEM((rows + 2 * HALO, 3, cols + 2 * HALO, points), F32),
            pltpu.VMEM((3, slots, points), F32),
            pltpu.VMEM((tiles, near * STOKES_ROWS, LANES), F32),
            pltpu.VMEM((tiles, own * 8, LANES), F32),
            pltpu.VMEM((tiles, own * 16, LANES), F32),
            pltpu.VMEM(tables[0].shape, BF16),
            pltpu.VMEM(tables[2].shape, BF16),
            pltpu.SemaphoreType.DMA((2,)),
        ],
        compiler_params=pltpu.CompilerParams(vmem_limit_bytes=50 * 2**20),
        cost_estimate=pl.CostEstimate(
            flops=1000 * pairs, bytes_accessed=8 * 2**20, transcendentals=pairs
        ),
        name="near",
    )(near_code, wall_code, below, pos, above, left, right, drag, *tables)


def wall_kernel(stage, per, raw_ref, pos_ref, layer_ref, out_ref, target_ref, moment_ref):
    patches = pos_ref.shape[1]
    pos = [pos_ref[d] for d in range(3)]
    target_raw(target_ref, 0, pos)

    def patch(p, carry):
        target = target_rows(get_rows(target_ref, pl.multiple_of(p * 8, 8), 8))
        moments = stokes_moments(raw_ref, [p * per + stage], target)
        put_rows(moment_ref, p, 16, patches, moments)
        return carry

    lax.fori_loop(0, patches, patch, 0, unroll=True)
    sums = stokes_finish(pos, [get_rows(moment_ref, k * patches, patches) for k in range(15)])
    for d in range(3):
        out_ref[d] = layer_ref[d] + (2.0 * STOKES_SCALE) * sums[d]


def wall_part(stage, per, raw, pos, layer):
    _, patches, points = pos.shape
    tiles = points // LANES
    in_vmem = pl.BlockSpec(memory_space=pltpu.VMEM)
    pairs = patches * raw.shape[0] * LANES * points
    return pl.pallas_call(
        functools.partial(wall_kernel, stage, per),
        in_specs=[in_vmem] * 3,
        out_specs=in_vmem,
        out_shape=jax.ShapeDtypeStruct(pos.shape, F32),
        scratch_shapes=[
            pltpu.VMEM((tiles, patches * 8, LANES), F32),
            pltpu.VMEM((tiles, patches * 16, LANES), F32),
        ],
        compiler_params=pltpu.CompilerParams(vmem_limit_bytes=24 * 2**20),
        cost_estimate=pl.CostEstimate(
            flops=1000 * pairs, bytes_accessed=2 * 2**20, transcendentals=pairs
        ),
        name=f"wall_{stage}",
    )(raw, pos, layer)


def layer_sums(sources, own_ref, left_ref, feature_ref, target_ref, moment_ref):
    patches = own_ref.shape[1]
    x = [own_ref[d] for d in range(3)]
    target_raw(target_ref, 0, x, TARGET_ROWS)
    rows = [x[0] * x[0], x[1] * x[1], x[2] * x[2], x[0] * x[1], x[0] * x[2], x[1] * x[2]]
    rows += x + [jnp.ones_like(x[0])] + [jnp.zeros_like(x[0])] * 6
    for k, row in enumerate(rows):
        put_rows(target_ref, 8 + k, patches, TARGET_ROWS, row)

    def patch(p, carry):
        raw = get_rows(target_ref, pl.multiple_of(p * TARGET_ROWS, 8), TARGET_ROWS)
        near, form = target_rows(raw[0:8]), target_rows(raw[8:24])
        total = None
        for s in sources(p):
            square = product(left_ref[s, 0:64], near)
            scalar = product(left_ref[s, 64:192], form)
            root = lax.rsqrt(jnp.maximum(square, SOFT))
            double = root * root
            scalar = (scalar * (double * double * root)).astype(BF16)
            part = jnp.dot(feature_ref[s], scalar, preferred_element_type=F32)
            total = part if total is None else total + part
        moments = total[0:8] + total[8:16] + total[16:24]
        put_rows(moment_ref, p, 8, patches, moments)
        return carry

    lax.fori_loop(0, patches, patch, 0, unroll=True)
    moments = [get_rows(moment_ref, k * patches, patches) for k in range(4)]
    return [(-2.0 * LAYER_SCALE) * (x[d] * moments[3] - moments[d]) for d in range(3)]


def layer_prepare(blocks, left_ref, feature_ref, raw_ref):
    patches = blocks[0][0].shape[1]
    for block, (ref, _) in enumerate(blocks):
        y = [ref[d] for d in range(3)]
        n = [ref[3 + d] for d in range(3)]
        v = [ref[6 + d] * ref[9] for d in range(3)]
        square = y[0] * y[0] + y[1] * y[1] + y[2] * y[2]
        along_n = y[0] * n[0] + y[1] * n[1] + y[2] * n[2]
        along_v = y[0] * v[0] + y[1] * v[1] + y[2] * v[2]
        one, zero = jnp.ones_like(square), jnp.zeros_like(square)
        rows = [-2.0 * y[0], -2.0 * y[1], -2.0 * y[2], square, one, zero, zero, zero]
        rows += [v[d] * n[d] for d in range(3)]
        rows += [v[a] * n[b] + v[b] * n[a] for a, b in ((0, 1), (0, 2), (1, 2))]
        rows += [-(v[d] * along_n + n[d] * along_v) for d in range(3)]
        rows += [along_v * along_n] + [zero] * 6
        rows += [y[0], y[1], y[2], one, zero, zero, zero, zero]
        for k, row in enumerate(rows):
            put_rows(raw_ref, block * patches * LAYER_ROWS + k, patches, LAYER_ROWS, row)

    for block, (_, first) in enumerate(blocks):

        def prepare(i, carry, block=block, first=first):
            base = (block * patches + i) * LAYER_ROWS
            raw = get_rows(raw_ref, pl.multiple_of(base, 8), LAYER_ROWS)
            left_ref[first + i, 0:64] = source_rows(raw[0:8])
            left_ref[first + i, 64:192] = source_rows(raw[8:24])
            split = [p.astype(F32) for p in parts(raw[24:32])]
            split.append(jnp.zeros_like(split[0]))
            feature_ref[first + i] = jnp.concatenate(split, axis=0).astype(BF16)
            return carry

        lax.fori_loop(0, patches, prepare, 0, unroll=4)


def layer_first(own_ref, out_ref, left_ref, feature_ref, raw_ref, target_ref, moment_ref):
    layer_prepare([(own_ref, 0)], left_ref, feature_ref, raw_ref)
    sums = layer_sums(lambda p: [p], own_ref, left_ref, feature_ref, target_ref, moment_ref)
    for d in range(3):
        out_ref[d] = sums[d]


def layer_second(
    listed_ref,
    own_ref,
    before_ref,
    after_ref,
    own_left_ref,
    own_feature_ref,
    so_far_ref,
    out_ref,
    left_ref,
    feature_ref,
    raw_ref,
    target_ref,
    moment_ref,
):
    patches = own_ref.shape[1]
    left_ref[patches : 2 * patches] = own_left_ref[...]
    feature_ref[patches : 2 * patches] = own_feature_ref[...]
    blocks = [(before_ref, 0), (after_ref, 2 * patches)]
    layer_prepare(blocks, left_ref, feature_ref, raw_ref)
    count = listed_ref.shape[1]
    sums = layer_sums(
        lambda p: [listed_ref[p, k] for k in range(count)],
        own_ref,
        left_ref,
        feature_ref,
        target_ref,
        moment_ref,
    )
    for d in range(3):
        out_ref[d] = so_far_ref[d] + sums[d]


def layer_part(kernel, *arrays, listed=None):
    _, patches, points = arrays[0].shape
    tiles = points // LANES
    in_vmem = pl.BlockSpec(memory_space=pltpu.VMEM)
    in_smem = pl.BlockSpec(memory_space=pltpu.SMEM)
    out_shape = [jax.ShapeDtypeStruct((3, patches, points), F32)]
    blocks, sources = (2, listed.shape[1]) if listed is not None else (1, 1)
    scratch = [
        pltpu.VMEM((tiles, blocks * patches * LAYER_ROWS, LANES), F32),
        pltpu.VMEM((tiles, patches * TARGET_ROWS, LANES), F32),
        pltpu.VMEM((tiles, patches * 8, LANES), F32),
    ]
    if listed is None:
        sides = (patches, 192, points), (patches, 32, points)
        out_shape += [jax.ShapeDtypeStruct(side, BF16) for side in sides]
        scalars = ()
    else:
        sides = (3 * patches, 192, points), (3 * patches, 32, points)
        scratch = [pltpu.VMEM(side, BF16) for side in sides] + scratch
        scalars = (listed,)
    pairs = patches * points * sources * points
    return pl.pallas_call(
        kernel,
        in_specs=[in_smem] * len(scalars) + [in_vmem] * len(arrays),
        out_specs=[in_vmem] * len(out_shape),
        out_shape=out_shape,
        scratch_shapes=scratch,
        compiler_params=pltpu.CompilerParams(vmem_limit_bytes=24 * 2**20),
        cost_estimate=pl.CostEstimate(
            flops=1000 * pairs, bytes_accessed=2**20, transcendentals=pairs
        ),
        name=kernel.__name__,
    )(*scalars, *arrays)


def move_kernel(*refs):
    *tops, pos_ref, velocity_ref, out_ref = refs
    top = functools.reduce(jnp.maximum, [t[...] for t in tops])
    step = 1.0 / (top[0:1, 0:1] + 1e-06)
    rows, _, cols, _ = pos_ref.shape
    for r in range(rows):
        for d in range(3):
            out_ref[r, d] = pos_ref[r, d] + step * velocity_ref[r, d]


def move_part(tops, pos, velocity):
    in_vmem = pl.BlockSpec(memory_space=pltpu.VMEM)
    return pl.pallas_call(
        move_kernel,
        in_specs=[in_vmem] * (len(tops) + 2),
        out_specs=in_vmem,
        out_shape=jax.ShapeDtypeStruct(pos.shape, F32),
        compiler_params=pltpu.CompilerParams(vmem_limit_bytes=8 * 2**20),
        name="move",
    )(*tops, pos, velocity)


def neighbours(low, high, axis):
    size = lax.axis_size(axis)
    up = [(i, (i + 1) % size) for i in range(size)]
    down = [(b, a) for a, b in up]
    return lax.ppermute(high, axis, up), lax.ppermute(low, axis, down)


def rotations(outer, inner, along_outer):
    size = outer if along_outer else inner
    for turn in range(1, size):
        yield [
            (
                a * inner + b,
                (a + turn) % outer * inner + b if along_outer else a * inner + (b + turn) % inner,
            )
            for a in range(outer)
            for b in range(inner)
        ]


def over_all(value):
    values = [value]
    for axis, inner in (("cy", 2), ("cx", 4)):
        outer = lax.axis_size(axis) // inner
        for along_outer in (False, True):
            value = functools.reduce(jnp.maximum, values)
            values = [value] + [
                lax.ppermute(value, axis, pairs)
                for pairs in rotations(outer, inner, along_outer)
            ]
    return values


def body(
    cell_pos,
    cell_drag,
    cell_near,
    analysis,
    stiffness,
    synthesis,
    wall_pos,
    wall_normal,
    wall_weight,
    density,
    patch_near,
    cell_to_patch,
):
    rows, cols = cell_pos.shape[:2]
    all_rows = rows * lax.axis_size("cx")
    all_cols = cols * lax.axis_size("cy")
    first_row = lax.axis_index("cx") * rows
    first_col = lax.axis_index("cy") * cols

    pos = jnp.transpose(cell_pos, (0, 2, 1, 3))
    walls = [jnp.transpose(v, (1, 0, 2)) for v in (wall_pos, wall_normal, density)]
    packed = jnp.concatenate(walls + [wall_weight[None]], axis=0)

    below, above = neighbours(pos, pos, "cx")
    own_strips = pos[:, :, :HALO], pos[:, :, cols - HALO :]
    below, above, later = lax.optimization_barrier((below, above, packed))
    wall_below, wall_above = neighbours(later, later, AXES)
    low, high = (
        jnp.concatenate([below[rows - HALO :, :, c : c + HALO], own, above[:HALO, :, c : c + HALO]])
        for c, own in zip((0, cols - HALO), own_strips)
    )
    left, right = neighbours(low, high, "cy")

    patches = wall_pos.shape[0]
    all_patches = patches * lax.axis_size(AXES)
    start = lax.axis_index(AXES) * patches
    listed = (patch_near - start + patches) % all_patches
    layer, lefts, features = layer_part(layer_first, later)

    def code(cell):
        row = (cell // all_cols - first_row + HALO) % all_rows
        col = (cell % all_cols - first_col + HALO) % all_cols
        return (row * 16 + col).reshape(-1)

    near_code, layer = lax.optimization_barrier((code(cell_near), layer))
    velocity, top, wall_raw = near_part(
        near_code,
        code(cell_to_patch),
        below,
        pos,
        above,
        left,
        right,
        cell_drag.reshape(-1, 1),
        (analysis, stiffness[None, :], synthesis),
    )
    top, listed = lax.optimization_barrier((top, listed))
    tops = over_all(top)
    [density_next] = layer_part(
        layer_second, packed, wall_below, wall_above, lefts, features, layer, listed=listed
    )
    per = cell_to_patch.shape[1]
    for stage in range(per):
        density_next = wall_part(stage, per, wall_raw, walls[0], density_next)
    moved = move_part(tops, pos, velocity)
    return jnp.transpose(moved, (0, 2, 1, 3)), jnp.transpose(density_next, (1, 0, 2))


def solution(mesh):
    patch = P(AXES, None, None)
    return jax.shard_map(
        body,
        mesh=mesh,
        in_specs=(
            P("cx", "cy", None, None),
            P("cx", "cy"),
            P("cx", "cy", None),
            P(),
            P(),
            P(),
            patch,
            patch,
            P(AXES, None),
            patch,
            P(AXES, None),
            P(AXES, None),
        ),
        out_specs=(P("cx", "cy", None, None), patch),
        check_vma=False,
    )
```

```python
import functools
import math

import jax
import jax.numpy as jnp
from jax import lax
from jax.experimental import pallas as pl
from jax.experimental.pallas import tpu as pltpu
from jax.sharding import PartitionSpec as P

HALO = 3
AXES = ("cx", "cy")
SOFT = 0.25
STOKES_SCALE = 1.0 / (8.0 * math.pi)
LAYER_SCALE = 3.0 / (4.0 * math.pi)
F32 = jnp.float32
BF16 = jnp.bfloat16
LANES = 128

GROUPS = ((0, 0), (0, 1), (1, 0), (0, 2), (2, 0), (1, 1), (1, 2), (2, 1))
STOKES_ROWS = 24
LAYER_ROWS = 32
TARGET_ROWS = 24


def parts(v):
    high = v.astype(BF16)
    rest = v - high.astype(F32)
    middle = rest.astype(BF16)
    low = (rest - middle.astype(F32)).astype(BF16)
    return high, middle, low


def target_rows(raw):
    split = [p.astype(F32) for p in parts(raw)]
    return jnp.concatenate([split[a] for a, _ in GROUPS], axis=0).astype(BF16)


def source_rows(raw):
    split = [p.astype(F32) for p in parts(raw)]
    return jnp.concatenate([split[b] for _, b in GROUPS], axis=0).astype(BF16)


def product(left, right):
    return lax.dot_general(left, right, (((0,), (0,)), ((), ())), preferred_element_type=F32)


def feature_rows(raw):
    return jnp.concatenate(parts(raw), axis=0)


def put_rows(ref, first, count, stride, value):
    for tile in range(ref.shape[0]):
        ref[tile, pl.ds(first, count, stride=stride), :] = value[
            :, tile * LANES : (tile + 1) * LANES
        ]


def get_rows(ref, first, count):
    return jnp.concatenate(
        [ref[tile, pl.ds(first, count), :] for tile in range(ref.shape[0])], axis=1
    )


def stokes_raw(ref, first, pos, force):
    square = pos[0] * pos[0] + pos[1] * pos[1] + pos[2] * pos[2]
    along = pos[0] * force[0] + pos[1] * force[1] + pos[2] * force[2]
    rows = [-2.0 * pos[0], -2.0 * pos[1], -2.0 * pos[2], square, jnp.ones_like(square)]
    rows += [jnp.zeros_like(square)] * 3
    rows += [force[0], force[1], force[2]]
    rows += [pos[j] * force[i] for j in range(3) for i in range(3)]
    rows += [square * force[i] + pos[i] * along for i in range(3)]
    rows += [jnp.zeros_like(square)]
    for k, row in enumerate(rows):
        put_rows(ref, first + k, 8, STOKES_ROWS, row)


def target_raw(ref, first, pos, stride=8):
    square = pos[0] * pos[0] + pos[1] * pos[1] + pos[2] * pos[2] + SOFT
    rows = [pos[0], pos[1], pos[2], jnp.ones_like(square), square]
    rows += [jnp.zeros_like(square)] * 3
    for k, row in enumerate(rows):
        put_rows(ref, first + k, 8, stride, row)


def stokes_moments(raw_ref, slots, target):
    total = None
    for slot in slots:
        base = pl.multiple_of(slot * STOKES_ROWS, 8)
        left = source_rows(get_rows(raw_ref, base, 8))
        square = product(left, target)
        root = lax.rsqrt(jnp.maximum(square, SOFT))
        factor = (root * root * root).astype(BF16)
        features = feature_rows(get_rows(raw_ref, base + 8, 16))
        part = jnp.dot(features, factor, preferred_element_type=F32)
        total = part if total is None else total + part
    return total[0:16] + total[16:32] + total[32:48]


def stokes_finish(pos, moments):
    m0 = moments[0:3]
    m1 = [[moments[3 + 3 * j + i] for i in range(3)] for j in range(3)]
    m2 = moments[12:15]
    square = pos[0] * pos[0] + pos[1] * pos[1] + pos[2] * pos[2] + 2.0 * SOFT
    along = pos[0] * m0[0] + pos[1] * m0[1] + pos[2] * m0[2]
    along = along - (m1[0][0] + m1[1][1] + m1[2][2])
    out = []
    for i in range(3):
        cross = sum(pos[j] * (2.0 * m1[j][i] + m1[i][j]) for j in range(3))
        out.append(square * m0[i] + m2[i] + pos[i] * along - cross)
    return out


def near_kernel(
    near_ref,
    wall_ref,
    below_ref,
    own_ref,
    above_ref,
    left_ref,
    left_outer_ref,
    right_ref,
    right_outer_ref,
    drag_ref,
    analysis_ref,
    stiffness_ref,
    synthesis_ref,
    velocity_ref,
    top_ref,
    wall_raw_ref,
    ext_ref,
    pos_ref,
    raw_ref,
    target_ref,
    moment_ref,
    first_ref,
    second_ref,
    sems,
):
    tables = [
        pltpu.make_async_copy(a, b, sems.at[k])
        for k, (a, b) in enumerate(((analysis_ref, first_ref), (synthesis_ref, second_ref)))
    ]
    for table in tables:
        table.start()
    rows, _, cols, points = own_ref.shape
    own = rows * cols
    near = near_ref.shape[0]
    wall = wall_ref.shape[0]
    slots = own + near + wall
    columns = (
        (slice(0, HALO), left_outer_ref, 0, left_ref, left_outer_ref, HALO),
        (slice(HALO, HALO + cols), below_ref, rows - HALO, own_ref, above_ref, 0),
        (slice(HALO + cols, cols + 2 * HALO), right_outer_ref, 0, right_ref, right_outer_ref, HALO),
    )
    for where, before, low, beside, after, high in columns:
        ext_ref[0:HALO, :, where, :] = before[low : low + HALO]
        ext_ref[HALO : HALO + rows, :, where, :] = beside[...]
        ext_ref[HALO + rows :, :, where, :] = after[high : high + HALO]
    for r in range(rows):
        for d in range(3):
            pos_ref[d, r * cols : (r + 1) * cols, :] = own_ref[r, d]
    for i in range(near + wall):
        code = near_ref[i] if i < near else wall_ref[i - near]
        row = code // 16
        col = code % 16
        for d in range(3):
            pos_ref[d, own + i : own + i + 1, :] = ext_ref[row, d, pl.ds(col, 1), :]
    everything = [pos_ref[d] for d in range(3)]
    centred = [v - jnp.sum(v, axis=1, keepdims=True) * (1.0 / points) for v in everything]
    flat = jnp.concatenate(centred, axis=0).astype(BF16)
    tables[0].wait()
    coeff = jnp.dot(flat, first_ref[...], preferred_element_type=F32)
    scaled = (coeff * stiffness_ref[...]).astype(BF16)
    tables[1].wait()
    force = -jnp.dot(scaled, second_ref[...], preferred_element_type=F32)
    forces = [force[d * slots : (d + 1) * slots] for d in range(3)]
    for g in range((near + wall) // 8):
        a = own + 8 * g
        into, base = (raw_ref, 8 * g) if 8 * g < near else (wall_raw_ref, 8 * g - near)
        stokes_raw(
            into,
            base * STOKES_ROWS,
            [v[a : a + 8] for v in everything],
            [v[a : a + 8] for v in forces],
        )
    for g in range(own // 8):
        target_raw(target_ref, 64 * g, [v[8 * g : 8 * g + 8] for v in everything])

    def cell(c, carry):
        target = target_rows(get_rows(target_ref, pl.multiple_of(c * 8, 8), 8))
        per = near // own
        moments = stokes_moments(raw_ref, [c * per + k for k in range(per)], target)
        put_rows(moment_ref, c, 16, own, moments)
        return carry

    lax.fori_loop(0, own, cell, 0, unroll=2)
    moments = [get_rows(moment_ref, k * own, own) for k in range(15)]
    own_pos = [v[0:own] for v in everything]
    sums = stokes_finish(own_pos, moments)
    speed = jnp.zeros_like(sums[0])
    for d in range(3):
        velocity = drag_ref[...] * forces[d][0:own] + STOKES_SCALE * sums[d]
        speed = speed + velocity * velocity
        for r in range(rows):
            velocity_ref[r, d] = velocity[r * cols : (r + 1) * cols]
    top = jnp.sqrt(jnp.max(speed, axis=(0, 1), keepdims=True))
    top_ref[...] = jnp.broadcast_to(top, top_ref.shape)


def near_part(near_code, wall_code, below, pos, above, left, right, drag, tables):
    rows, _, cols, points = pos.shape
    own = rows * cols
    near, wall = near_code.shape[0], wall_code.shape[0]
    slots = own + near + wall
    tiles = points // LANES
    in_vmem = pl.BlockSpec(memory_space=pltpu.VMEM)
    in_smem = pl.BlockSpec(memory_space=pltpu.SMEM)
    in_hbm = pl.BlockSpec(memory_space=pl.ANY)
    pairs = own * points * (near // own) * points
    return pl.pallas_call(
        near_kernel,
        in_specs=[in_smem] * 2 + [in_vmem] * 8 + [in_hbm, in_vmem, in_hbm],
        out_specs=[in_vmem] * 3,
        out_shape=[
            jax.ShapeDtypeStruct((rows, 3, cols, points), F32),
            jax.ShapeDtypeStruct((8, LANES), F32),
            jax.ShapeDtypeStruct((tiles, wall * STOKES_ROWS, LANES), F32),
        ],
        scratch_shapes=[
            pltpu.VMEM((rows + 2 * HALO, 3, cols + 2 * HALO, points), F32),
            pltpu.VMEM((3, slots, points), F32),
            pltpu.VMEM((tiles, near * STOKES_ROWS, LANES), F32),
            pltpu.VMEM((tiles, own * 8, LANES), F32),
            pltpu.VMEM((tiles, own * 16, LANES), F32),
            pltpu.VMEM(tables[0].shape, BF16),
            pltpu.VMEM(tables[2].shape, BF16),
            pltpu.SemaphoreType.DMA((2,)),
        ],
        compiler_params=pltpu.CompilerParams(vmem_limit_bytes=50 * 2**20),
        cost_estimate=pl.CostEstimate(
            flops=1000 * pairs, bytes_accessed=8 * 2**20, transcendentals=pairs
        ),
        name="near",
    )(near_code, wall_code, below, pos, above, *left, *right, drag, *tables)


def wall_kernel(stage, per, raw_ref, pos_ref, layer_ref, out_ref, target_ref, moment_ref):
    patches = pos_ref.shape[1]
    pos = [pos_ref[d] for d in range(3)]
    target_raw(target_ref, 0, pos)

    def patch(p, carry):
        target = target_rows(get_rows(target_ref, pl.multiple_of(p * 8, 8), 8))
        moments = stokes_moments(raw_ref, [p * per + stage], target)
        put_rows(moment_ref, p, 16, patches, moments)
        return carry

    lax.fori_loop(0, patches, patch, 0, unroll=True)
    sums = stokes_finish(pos, [get_rows(moment_ref, k * patches, patches) for k in range(15)])
    for d in range(3):
        out_ref[d] = layer_ref[d] + (2.0 * STOKES_SCALE) * sums[d]


def wall_part(stage, per, raw, pos, layer):
    _, patches, points = pos.shape
    tiles = points // LANES
    in_vmem = pl.BlockSpec(memory_space=pltpu.VMEM)
    pairs = patches * raw.shape[0] * LANES * points
    return pl.pallas_call(
        functools.partial(wall_kernel, stage, per),
        in_specs=[in_vmem] * 3,
        out_specs=in_vmem,
        out_shape=jax.ShapeDtypeStruct(pos.shape, F32),
        scratch_shapes=[
            pltpu.VMEM((tiles, patches * 8, LANES), F32),
            pltpu.VMEM((tiles, patches * 16, LANES), F32),
        ],
        compiler_params=pltpu.CompilerParams(vmem_limit_bytes=24 * 2**20),
        cost_estimate=pl.CostEstimate(
            flops=1000 * pairs, bytes_accessed=2 * 2**20, transcendentals=pairs
        ),
        name=f"wall_{stage}",
    )(raw, pos, layer)


def layer_sums(sources, own_ref, left_ref, feature_ref, target_ref, moment_ref):
    patches = own_ref.shape[1]
    x = [own_ref[d] for d in range(3)]
    target_raw(target_ref, 0, x, TARGET_ROWS)
    rows = [x[0] * x[0], x[1] * x[1], x[2] * x[2], x[0] * x[1], x[0] * x[2], x[1] * x[2]]
    rows += x + [jnp.ones_like(x[0])] + [jnp.zeros_like(x[0])] * 6
    for k, row in enumerate(rows):
        put_rows(target_ref, 8 + k, patches, TARGET_ROWS, row)

    def patch(p, carry):
        raw = get_rows(target_ref, pl.multiple_of(p * TARGET_ROWS, 8), TARGET_ROWS)
        near, form = target_rows(raw[0:8]), target_rows(raw[8:24])
        total = None
        for s in sources(p):
            square = product(left_ref[s, 0:64], near)
            scalar = product(left_ref[s, 64:192], form)
            root = lax.rsqrt(jnp.maximum(square, SOFT))
            double = root * root
            scalar = (scalar * (double * double * root)).astype(BF16)
            part = jnp.dot(feature_ref[s], scalar, preferred_element_type=F32)
            total = part if total is None else total + part
        moments = total[0:8] + total[8:16] + total[16:24]
        put_rows(moment_ref, p, 8, patches, moments)
        return carry

    lax.fori_loop(0, patches, patch, 0, unroll=True)
    moments = [get_rows(moment_ref, k * patches, patches) for k in range(4)]
    return [(-2.0 * LAYER_SCALE) * (x[d] * moments[3] - moments[d]) for d in range(3)]


def layer_prepare(blocks, left_ref, feature_ref, raw_ref):
    patches = blocks[0][0].shape[1]
    for block, (ref, _) in enumerate(blocks):
        y = [ref[d] for d in range(3)]
        n = [ref[3 + d] for d in range(3)]
        v = [ref[6 + d] * ref[9] for d in range(3)]
        square = y[0] * y[0] + y[1] * y[1] + y[2] * y[2]
        along_n = y[0] * n[0] + y[1] * n[1] + y[2] * n[2]
        along_v = y[0] * v[0] + y[1] * v[1] + y[2] * v[2]
        one, zero = jnp.ones_like(square), jnp.zeros_like(square)
        rows = [-2.0 * y[0], -2.0 * y[1], -2.0 * y[2], square, one, zero, zero, zero]
        rows += [v[d] * n[d] for d in range(3)]
        rows += [v[a] * n[b] + v[b] * n[a] for a, b in ((0, 1), (0, 2), (1, 2))]
        rows += [-(v[d] * along_n + n[d] * along_v) for d in range(3)]
        rows += [along_v * along_n] + [zero] * 6
        rows += [y[0], y[1], y[2], one, zero, zero, zero, zero]
        for k, row in enumerate(rows):
            put_rows(raw_ref, block * patches * LAYER_ROWS + k, patches, LAYER_ROWS, row)

    for block, (_, first) in enumerate(blocks):

        def prepare(i, carry, block=block, first=first):
            base = (block * patches + i) * LAYER_ROWS
            raw = get_rows(raw_ref, pl.multiple_of(base, 8), LAYER_ROWS)
            left_ref[first + i, 0:64] = source_rows(raw[0:8])
            left_ref[first + i, 64:192] = source_rows(raw[8:24])
            split = [p.astype(F32) for p in parts(raw[24:32])]
            split.append(jnp.zeros_like(split[0]))
            feature_ref[first + i] = jnp.concatenate(split, axis=0).astype(BF16)
            return carry

        lax.fori_loop(0, patches, prepare, 0, unroll=4)


def layer_first(own_ref, out_ref, left_ref, feature_ref, raw_ref, target_ref, moment_ref):
    layer_prepare([(own_ref, 0)], left_ref, feature_ref, raw_ref)
    sums = layer_sums(lambda p: [p], own_ref, left_ref, feature_ref, target_ref, moment_ref)
    for d in range(3):
        out_ref[d] = sums[d]


def layer_second(
    listed_ref,
    own_ref,
    before_ref,
    after_ref,
    own_left_ref,
    own_feature_ref,
    so_far_ref,
    out_ref,
    left_ref,
    feature_ref,
    raw_ref,
    target_ref,
    moment_ref,
):
    patches = own_ref.shape[1]
    left_ref[patches : 2 * patches] = own_left_ref[...]
    feature_ref[patches : 2 * patches] = own_feature_ref[...]
    blocks = [(before_ref, 0), (after_ref, 2 * patches)]
    layer_prepare(blocks, left_ref, feature_ref, raw_ref)
    count = listed_ref.shape[1]
    sums = layer_sums(
        lambda p: [listed_ref[p, k] for k in range(count)],
        own_ref,
        left_ref,
        feature_ref,
        target_ref,
        moment_ref,
    )
    for d in range(3):
        out_ref[d] = so_far_ref[d] + sums[d]


def layer_part(kernel, *arrays, listed=None):
    _, patches, points = arrays[0].shape
    tiles = points // LANES
    in_vmem = pl.BlockSpec(memory_space=pltpu.VMEM)
    in_smem = pl.BlockSpec(memory_space=pltpu.SMEM)
    out_shape = [jax.ShapeDtypeStruct((3, patches, points), F32)]
    blocks, sources = (2, listed.shape[1]) if listed is not None else (1, 1)
    scratch = [
        pltpu.VMEM((tiles, blocks * patches * LAYER_ROWS, LANES), F32),
        pltpu.VMEM((tiles, patches * TARGET_ROWS, LANES), F32),
        pltpu.VMEM((tiles, patches * 8, LANES), F32),
    ]
    if listed is None:
        sides = (patches, 192, points), (patches, 32, points)
        out_shape += [jax.ShapeDtypeStruct(side, BF16) for side in sides]
        scalars = ()
    else:
        sides = (3 * patches, 192, points), (3 * patches, 32, points)
        scratch = [pltpu.VMEM(side, BF16) for side in sides] + scratch
        scalars = (listed,)
    pairs = patches * points * sources * points
    return pl.pallas_call(
        kernel,
        in_specs=[in_smem] * len(scalars) + [in_vmem] * len(arrays),
        out_specs=[in_vmem] * len(out_shape),
        out_shape=out_shape,
        scratch_shapes=scratch,
        compiler_params=pltpu.CompilerParams(vmem_limit_bytes=24 * 2**20),
        cost_estimate=pl.CostEstimate(
            flops=1000 * pairs, bytes_accessed=2**20, transcendentals=pairs
        ),
        name=kernel.__name__,
    )(*scalars, *arrays)


def move_kernel(*refs):
    *tops, pos_ref, velocity_ref, out_ref = refs
    top = functools.reduce(jnp.maximum, [t[...] for t in tops])
    step = 1.0 / (top[0:1, 0:1] + 1e-06)
    rows, _, cols, _ = pos_ref.shape
    for r in range(rows):
        for d in range(3):
            out_ref[r, d] = pos_ref[r, d] + step * velocity_ref[r, d]


def move_part(tops, pos, velocity):
    in_vmem = pl.BlockSpec(memory_space=pltpu.VMEM)
    return pl.pallas_call(
        move_kernel,
        in_specs=[in_vmem] * (len(tops) + 2),
        out_specs=in_vmem,
        out_shape=jax.ShapeDtypeStruct(pos.shape, F32),
        compiler_params=pltpu.CompilerParams(vmem_limit_bytes=8 * 2**20),
        name="move",
    )(*tops, pos, velocity)


def neighbours(low, high, axis):
    size = lax.axis_size(axis)
    up = [(i, (i + 1) % size) for i in range(size)]
    down = [(b, a) for a, b in up]
    return lax.ppermute(high, axis, up), lax.ppermute(low, axis, down)


def rotations(outer, inner, along_outer):
    size = outer if along_outer else inner
    for turn in range(1, size):
        yield [
            (
                a * inner + b,
                (a + turn) % outer * inner + b if along_outer else a * inner + (b + turn) % inner,
            )
            for a in range(outer)
            for b in range(inner)
        ]


def over_all(value):
    values = [value]
    for axis, inner in (("cy", 2), ("cx", 4)):
        outer = lax.axis_size(axis) // inner
        for along_outer in (False, True):
            value = functools.reduce(jnp.maximum, values)
            values = [value] + [
                lax.ppermute(value, axis, pairs)
                for pairs in rotations(outer, inner, along_outer)
            ]
    return values


def body(
    cell_pos,
    cell_drag,
    cell_near,
    analysis,
    stiffness,
    synthesis,
    wall_pos,
    wall_normal,
    wall_weight,
    density,
    patch_near,
    cell_to_patch,
):
    rows, cols = cell_pos.shape[:2]
    all_rows = rows * lax.axis_size("cx")
    all_cols = cols * lax.axis_size("cy")
    first_row = lax.axis_index("cx") * rows
    first_col = lax.axis_index("cy") * cols

    pos = jnp.transpose(cell_pos, (0, 2, 1, 3))
    walls = [jnp.transpose(v, (1, 0, 2)) for v in (wall_pos, wall_normal, density)]
    packed = jnp.concatenate(walls + [wall_weight[None]], axis=0)

    below, above = neighbours(pos, pos, "cx")
    inner_left, inner_right = neighbours(pos[:, :, :HALO], pos[:, :, cols - HALO :], "cy")
    below, above, later = lax.optimization_barrier((below, above, packed))
    wall_below, wall_above = neighbours(later, later, AXES)
    outer = [
        jnp.concatenate([v[:, :, c : c + HALO] for v in (below[rows - HALO :], above[:HALO])])
        for c in (0, cols - HALO)
    ]
    outer_left, outer_right = neighbours(*outer, "cy")

    patches = wall_pos.shape[0]
    all_patches = patches * lax.axis_size(AXES)
    start = lax.axis_index(AXES) * patches
    listed = (patch_near - start + patches) % all_patches
    layer, lefts, features = layer_part(layer_first, later)

    def code(cell):
        row = (cell // all_cols - first_row + HALO) % all_rows
        col = (cell % all_cols - first_col + HALO) % all_cols
        return (row * 16 + col).reshape(-1)

    near_code, layer = lax.optimization_barrier((code(cell_near), layer))
    velocity, top, wall_raw = near_part(
        near_code,
        code(cell_to_patch),
        below,
        pos,
        above,
        (inner_left, outer_left),
        (inner_right, outer_right),
        cell_drag.reshape(-1, 1),
        (analysis, stiffness[None, :], synthesis),
    )
    top, listed = lax.optimization_barrier((top, listed))
    tops = over_all(top)
    [density_next] = layer_part(
        layer_second, packed, wall_below, wall_above, lefts, features, layer, listed=listed
    )
    per = cell_to_patch.shape[1]
    for stage in range(per):
        density_next = wall_part(stage, per, wall_raw, walls[0], density_next)
    moved = move_part(tops, pos, velocity)
    return jnp.transpose(moved, (0, 2, 1, 3)), jnp.transpose(density_next, (1, 0, 2))


def solution(mesh):
    patch = P(AXES, None, None)
    return jax.shard_map(
        body,
        mesh=mesh,
        in_specs=(
            P("cx", "cy", None, None),
            P("cx", "cy"),
            P("cx", "cy", None),
            P(),
            P(),
            P(),
            patch,
            patch,
            P(AXES, None),
            patch,
            P(AXES, None),
            P(AXES, None),
        ),
        out_specs=(P("cx", "cy", None, None), patch),
        check_vma=False,
    )
```

```python
import functools
import math

import jax
import jax.numpy as jnp
from jax import lax
from jax.experimental import pallas as pl
from jax.experimental.pallas import tpu as pltpu
from jax.sharding import PartitionSpec as P

HALO = 3
AXES = ("cx", "cy")
SOFT = 0.25
STOKES_SCALE = 1.0 / (8.0 * math.pi)
LAYER_SCALE = 3.0 / (4.0 * math.pi)
F32 = jnp.float32
BF16 = jnp.bfloat16
LANES = 128

GROUPS = ((0, 0), (0, 1), (1, 0), (0, 2), (2, 0), (1, 1), (1, 2), (2, 1))
STOKES_ROWS = 24
LAYER_ROWS = 32
TARGET_ROWS = 24


def parts(v):
    high = v.astype(BF16)
    rest = v - high.astype(F32)
    middle = rest.astype(BF16)
    low = (rest - middle.astype(F32)).astype(BF16)
    return high, middle, low


def target_rows(raw):
    split = [p.astype(F32) for p in parts(raw)]
    return jnp.concatenate([split[a] for a, _ in GROUPS], axis=0).astype(BF16)


def source_rows(raw):
    split = [p.astype(F32) for p in parts(raw)]
    return jnp.concatenate([split[b] for _, b in GROUPS], axis=0).astype(BF16)


def product(left, right):
    return lax.dot_general(left, right, (((0,), (0,)), ((), ())), preferred_element_type=F32)


def feature_rows(raw):
    return jnp.concatenate(parts(raw), axis=0)


def put_rows(ref, first, count, stride, value):
    for tile in range(ref.shape[0]):
        ref[tile, pl.ds(first, count, stride=stride), :] = value[
            :, tile * LANES : (tile + 1) * LANES
        ]


def get_rows(ref, first, count):
    return jnp.concatenate(
        [ref[tile, pl.ds(first, count), :] for tile in range(ref.shape[0])], axis=1
    )


def stokes_raw(ref, first, pos, force):
    square = pos[0] * pos[0] + pos[1] * pos[1] + pos[2] * pos[2]
    along = pos[0] * force[0] + pos[1] * force[1] + pos[2] * force[2]
    rows = [-2.0 * pos[0], -2.0 * pos[1], -2.0 * pos[2], square, jnp.ones_like(square)]
    rows += [jnp.zeros_like(square)] * 3
    rows += [force[0], force[1], force[2]]
    rows += [pos[j] * force[i] for j in range(3) for i in range(3)]
    rows += [square * force[i] + pos[i] * along for i in range(3)]
    rows += [jnp.zeros_like(square)]
    for k, row in enumerate(rows):
        put_rows(ref, first + k, 8, STOKES_ROWS, row)


def target_raw(ref, first, pos, stride=8):
    square = pos[0] * pos[0] + pos[1] * pos[1] + pos[2] * pos[2] + SOFT
    rows = [pos[0], pos[1], pos[2], jnp.ones_like(square), square]
    rows += [jnp.zeros_like(square)] * 3
    for k, row in enumerate(rows):
        put_rows(ref, first + k, 8, stride, row)


def weighted(features, factor):
    return lax.dot_general(
        features, factor, (((1,), (1,)), ((), ())), preferred_element_type=F32
    )


def stokes_moments(raw_ref, slots, target):
    total = None
    for slot in slots:
        base = pl.multiple_of(slot * STOKES_ROWS, 8)
        left = source_rows(get_rows(raw_ref, base, 8))
        targets_first = target.shape[1] < left.shape[1]
        square = product(target, left) if targets_first else product(left, target)
        root = lax.rsqrt(jnp.maximum(square, SOFT))
        factor = (root * root * root).astype(BF16)
        features = feature_rows(get_rows(raw_ref, base + 8, 16))
        if targets_first:
            part = weighted(features, factor)
        else:
            part = jnp.dot(features, factor, preferred_element_type=F32)
        total = part if total is None else total + part
    return total[0:16] + total[16:32] + total[32:48]


def stokes_finish(pos, moments):
    m0 = moments[0:3]
    m1 = [[moments[3 + 3 * j + i] for i in range(3)] for j in range(3)]
    m2 = moments[12:15]
    square = pos[0] * pos[0] + pos[1] * pos[1] + pos[2] * pos[2] + 2.0 * SOFT
    along = pos[0] * m0[0] + pos[1] * m0[1] + pos[2] * m0[2]
    along = along - (m1[0][0] + m1[1][1] + m1[2][2])
    out = []
    for i in range(3):
        cross = sum(pos[j] * (2.0 * m1[j][i] + m1[i][j]) for j in range(3))
        out.append(square * m0[i] + m2[i] + pos[i] * along - cross)
    return out


def near_kernel(
    near_ref,
    wall_ref,
    below_ref,
    own_ref,
    above_ref,
    left_ref,
    left_outer_ref,
    right_ref,
    right_outer_ref,
    drag_ref,
    analysis_ref,
    stiffness_ref,
    synthesis_ref,
    velocity_ref,
    top_ref,
    wall_raw_ref,
    ext_ref,
    pos_ref,
    raw_ref,
    target_ref,
    moment_ref,
    first_ref,
    second_ref,
    sems,
):
    tables = [
        pltpu.make_async_copy(a, b, sems.at[k])
        for k, (a, b) in enumerate(((analysis_ref, first_ref), (synthesis_ref, second_ref)))
    ]
    for table in tables:
        table.start()
    rows, _, cols, points = own_ref.shape
    own = rows * cols
    near = near_ref.shape[0]
    wall = wall_ref.shape[0]
    slots = own + near + wall
    columns = (
        (slice(0, HALO), left_outer_ref, 0, left_ref, left_outer_ref, HALO),
        (slice(HALO, HALO + cols), below_ref, rows - HALO, own_ref, above_ref, 0),
        (slice(HALO + cols, cols + 2 * HALO), right_outer_ref, 0, right_ref, right_outer_ref, HALO),
    )
    for where, before, low, beside, after, high in columns:
        ext_ref[0:HALO, :, where, :] = before[low : low + HALO]
        ext_ref[HALO : HALO + rows, :, where, :] = beside[...]
        ext_ref[HALO + rows :, :, where, :] = after[high : high + HALO]
    for r in range(rows):
        for d in range(3):
            pos_ref[d, r * cols : (r + 1) * cols, :] = own_ref[r, d]
    for i in range(near + wall):
        code = near_ref[i] if i < near else wall_ref[i - near]
        row = code // 16
        col = code % 16
        for d in range(3):
            pos_ref[d, own + i : own + i + 1, :] = ext_ref[row, d, pl.ds(col, 1), :]
    everything = [pos_ref[d] for d in range(3)]
    centred = [v - jnp.sum(v, axis=1, keepdims=True) * (1.0 / points) for v in everything]
    flat = jnp.concatenate(centred, axis=0).astype(BF16)
    tables[0].wait()
    coeff = jnp.dot(flat, first_ref[...], preferred_element_type=F32)
    scaled = (coeff * stiffness_ref[...]).astype(BF16)
    tables[1].wait()
    force = -jnp.dot(scaled, second_ref[...], preferred_element_type=F32)
    forces = [force[d * slots : (d + 1) * slots] for d in range(3)]
    for g in range((near + wall) // 8):
        a = own + 8 * g
        into, base = (raw_ref, 8 * g) if 8 * g < near else (wall_raw_ref, 8 * g - near)
        stokes_raw(
            into,
            base * STOKES_ROWS,
            [v[a : a + 8] for v in everything],
            [v[a : a + 8] for v in forces],
        )
    for g in range(own // 8):
        target_raw(target_ref, 64 * g, [v[8 * g : 8 * g + 8] for v in everything])

    def cell(c, carry):
        target = target_rows(get_rows(target_ref, pl.multiple_of(c * 8, 8), 8))
        per = near // own
        moments = stokes_moments(raw_ref, [c * per + k for k in range(per)], target)
        put_rows(moment_ref, c, 16, own, moments)
        return carry

    lax.fori_loop(0, own, cell, 0, unroll=2)
    moments = [get_rows(moment_ref, k * own, own) for k in range(15)]
    own_pos = [v[0:own] for v in everything]
    sums = stokes_finish(own_pos, moments)
    speed = jnp.zeros_like(sums[0])
    for d in range(3):
        velocity = drag_ref[...] * forces[d][0:own] + STOKES_SCALE * sums[d]
        speed = speed + velocity * velocity
        for r in range(rows):
            velocity_ref[r, d] = velocity[r * cols : (r + 1) * cols]
    top = jnp.sqrt(jnp.max(speed, axis=(0, 1), keepdims=True))
    top_ref[...] = jnp.broadcast_to(top, top_ref.shape)


def near_part(near_code, wall_code, below, pos, above, left, right, drag, tables):
    rows, _, cols, points = pos.shape
    own = rows * cols
    near, wall = near_code.shape[0], wall_code.shape[0]
    slots = own + near + wall
    tiles = points // LANES
    in_vmem = pl.BlockSpec(memory_space=pltpu.VMEM)
    in_smem = pl.BlockSpec(memory_space=pltpu.SMEM)
    in_hbm = pl.BlockSpec(memory_space=pl.ANY)
    pairs = own * points * (near // own) * points
    return pl.pallas_call(
        near_kernel,
        in_specs=[in_smem] * 2 + [in_vmem] * 8 + [in_hbm, in_vmem, in_hbm],
        out_specs=[in_vmem] * 3,
        out_shape=[
            jax.ShapeDtypeStruct((rows, 3, cols, points), F32),
            jax.ShapeDtypeStruct((8, LANES), F32),
            jax.ShapeDtypeStruct((tiles, wall * STOKES_ROWS, LANES), F32),
        ],
        scratch_shapes=[
            pltpu.VMEM((rows + 2 * HALO, 3, cols + 2 * HALO, points), F32),
            pltpu.VMEM((3, slots, points), F32),
            pltpu.VMEM((tiles, near * STOKES_ROWS, LANES), F32),
            pltpu.VMEM((tiles, own * 8, LANES), F32),
            pltpu.VMEM((tiles, own * 16, LANES), F32),
            pltpu.VMEM(tables[0].shape, BF16),
            pltpu.VMEM(tables[2].shape, BF16),
            pltpu.SemaphoreType.DMA((2,)),
        ],
        compiler_params=pltpu.CompilerParams(vmem_limit_bytes=50 * 2**20),
        cost_estimate=pl.CostEstimate(
            flops=1000 * pairs, bytes_accessed=8 * 2**20, transcendentals=pairs
        ),
        name="near",
    )(near_code, wall_code, below, pos, above, *left, *right, drag, *tables)


def wall_kernel(stage, per, raw_ref, pos_ref, layer_ref, out_ref, target_ref, moment_ref):
    patches = pos_ref.shape[1]
    pos = [pos_ref[d] for d in range(3)]
    target_raw(target_ref, 0, pos)

    def patch(p, carry):
        target = target_rows(get_rows(target_ref, pl.multiple_of(p * 8, 8), 8))
        moments = stokes_moments(raw_ref, [p * per + stage], target)
        put_rows(moment_ref, p, 16, patches, moments)
        return carry

    lax.fori_loop(0, patches, patch, 0, unroll=True)
    sums = stokes_finish(pos, [get_rows(moment_ref, k * patches, patches) for k in range(15)])
    for d in range(3):
        out_ref[d] = layer_ref[d] + (2.0 * STOKES_SCALE) * sums[d]


def wall_part(stage, per, raw, pos, layer):
    _, patches, points = pos.shape
    tiles = points // LANES
    in_vmem = pl.BlockSpec(memory_space=pltpu.VMEM)
    pairs = patches * raw.shape[0] * LANES * points
    return pl.pallas_call(
        functools.partial(wall_kernel, stage, per),
        in_specs=[in_vmem] * 3,
        out_specs=in_vmem,
        out_shape=jax.ShapeDtypeStruct(pos.shape, F32),
        scratch_shapes=[
            pltpu.VMEM((tiles, patches * 8, LANES), F32),
            pltpu.VMEM((tiles, patches * 16, LANES), F32),
        ],
        compiler_params=pltpu.CompilerParams(vmem_limit_bytes=24 * 2**20),
        cost_estimate=pl.CostEstimate(
            flops=1000 * pairs, bytes_accessed=2 * 2**20, transcendentals=pairs
        ),
        name=f"wall_{stage}",
    )(raw, pos, layer)


def layer_sums(sources, own_ref, left_ref, feature_ref, target_ref, moment_ref):
    patches = own_ref.shape[1]
    x = [own_ref[d] for d in range(3)]
    target_raw(target_ref, 0, x, TARGET_ROWS)
    rows = [x[0] * x[0], x[1] * x[1], x[2] * x[2], x[0] * x[1], x[0] * x[2], x[1] * x[2]]
    rows += x + [jnp.ones_like(x[0])] + [jnp.zeros_like(x[0])] * 6
    for k, row in enumerate(rows):
        put_rows(target_ref, 8 + k, patches, TARGET_ROWS, row)

    def patch(p, carry):
        raw = get_rows(target_ref, pl.multiple_of(p * TARGET_ROWS, 8), TARGET_ROWS)
        near, form = target_rows(raw[0:8]), target_rows(raw[8:24])
        total = None
        for s in sources(p):
            square = product(near, left_ref[s, 0:64])
            scalar = product(form, left_ref[s, 64:192])
            root = lax.rsqrt(jnp.maximum(square, SOFT))
            double = root * root
            scalar = (scalar * (double * double * root)).astype(BF16)
            part = weighted(feature_ref[s], scalar)
            total = part if total is None else total + part
        moments = total[0:8] + total[8:16] + total[16:24]
        put_rows(moment_ref, p, 8, patches, moments)
        return carry

    lax.fori_loop(0, patches, patch, 0, unroll=True)
    moments = [get_rows(moment_ref, k * patches, patches) for k in range(4)]
    return [(-2.0 * LAYER_SCALE) * (x[d] * moments[3] - moments[d]) for d in range(3)]


def layer_prepare(blocks, left_ref, feature_ref, raw_ref):
    patches = blocks[0][0].shape[1]
    for block, (ref, _) in enumerate(blocks):
        y = [ref[d] for d in range(3)]
        n = [ref[3 + d] for d in range(3)]
        v = [ref[6 + d] * ref[9] for d in range(3)]
        square = y[0] * y[0] + y[1] * y[1] + y[2] * y[2]
        along_n = y[0] * n[0] + y[1] * n[1] + y[2] * n[2]
        along_v = y[0] * v[0] + y[1] * v[1] + y[2] * v[2]
        one, zero = jnp.ones_like(square), jnp.zeros_like(square)
        rows = [-2.0 * y[0], -2.0 * y[1], -2.0 * y[2], square, one, zero, zero, zero]
        rows += [v[d] * n[d] for d in range(3)]
        rows += [v[a] * n[b] + v[b] * n[a] for a, b in ((0, 1), (0, 2), (1, 2))]
        rows += [-(v[d] * along_n + n[d] * along_v) for d in range(3)]
        rows += [along_v * along_n] + [zero] * 6
        rows += [y[0], y[1], y[2], one, zero, zero, zero, zero]
        for k, row in enumerate(rows):
            put_rows(raw_ref, block * patches * LAYER_ROWS + k, patches, LAYER_ROWS, row)

    for block, (_, first) in enumerate(blocks):

        def prepare(i, carry, block=block, first=first):
            base = (block * patches + i) * LAYER_ROWS
            raw = get_rows(raw_ref, pl.multiple_of(base, 8), LAYER_ROWS)
            left_ref[first + i, 0:64] = source_rows(raw[0:8])
            left_ref[first + i, 64:192] = source_rows(raw[8:24])
            split = [p.astype(F32) for p in parts(raw[24:32])]
            split.append(jnp.zeros_like(split[0]))
            feature_ref[first + i] = jnp.concatenate(split, axis=0).astype(BF16)
            return carry

        lax.fori_loop(0, patches, prepare, 0, unroll=4)


def layer_first(own_ref, out_ref, left_ref, feature_ref, raw_ref, target_ref, moment_ref):
    layer_prepare([(own_ref, 0)], left_ref, feature_ref, raw_ref)
    sums = layer_sums(lambda p: [p], own_ref, left_ref, feature_ref, target_ref, moment_ref)
    for d in range(3):
        out_ref[d] = sums[d]


def layer_second(
    listed_ref,
    own_ref,
    before_ref,
    after_ref,
    own_left_ref,
    own_feature_ref,
    so_far_ref,
    out_ref,
    left_ref,
    feature_ref,
    raw_ref,
    target_ref,
    moment_ref,
):
    patches = own_ref.shape[1]
    left_ref[patches : 2 * patches] = own_left_ref[...]
    feature_ref[patches : 2 * patches] = own_feature_ref[...]
    blocks = [(before_ref, 0), (after_ref, 2 * patches)]
    layer_prepare(blocks, left_ref, feature_ref, raw_ref)
    count = listed_ref.shape[1]
    sums = layer_sums(
        lambda p: [listed_ref[p, k] for k in range(count)],
        own_ref,
        left_ref,
        feature_ref,
        target_ref,
        moment_ref,
    )
    for d in range(3):
        out_ref[d] = so_far_ref[d] + sums[d]


def layer_part(kernel, *arrays, listed=None):
    _, patches, points = arrays[0].shape
    tiles = points // LANES
    in_vmem = pl.BlockSpec(memory_space=pltpu.VMEM)
    in_smem = pl.BlockSpec(memory_space=pltpu.SMEM)
    out_shape = [jax.ShapeDtypeStruct((3, patches, points), F32)]
    blocks, sources = (2, listed.shape[1]) if listed is not None else (1, 1)
    scratch = [
        pltpu.VMEM((tiles, blocks * patches * LAYER_ROWS, LANES), F32),
        pltpu.VMEM((tiles, patches * TARGET_ROWS, LANES), F32),
        pltpu.VMEM((tiles, patches * 8, LANES), F32),
    ]
    if listed is None:
        sides = (patches, 192, points), (patches, 32, points)
        out_shape += [jax.ShapeDtypeStruct(side, BF16) for side in sides]
        scalars = ()
    else:
        sides = (3 * patches, 192, points), (3 * patches, 32, points)
        scratch = [pltpu.VMEM(side, BF16) for side in sides] + scratch
        scalars = (listed,)
    pairs = patches * points * sources * points
    return pl.pallas_call(
        kernel,
        in_specs=[in_smem] * len(scalars) + [in_vmem] * len(arrays),
        out_specs=[in_vmem] * len(out_shape),
        out_shape=out_shape,
        scratch_shapes=scratch,
        compiler_params=pltpu.CompilerParams(vmem_limit_bytes=24 * 2**20),
        cost_estimate=pl.CostEstimate(
            flops=1000 * pairs, bytes_accessed=2**20, transcendentals=pairs
        ),
        name=kernel.__name__,
    )(*scalars, *arrays)


def move_kernel(*refs):
    *tops, pos_ref, velocity_ref, out_ref = refs
    top = functools.reduce(jnp.maximum, [t[...] for t in tops])
    step = 1.0 / (top[0:1, 0:1] + 1e-06)
    rows, _, cols, _ = pos_ref.shape
    for r in range(rows):
        for d in range(3):
            out_ref[r, d] = pos_ref[r, d] + step * velocity_ref[r, d]


def move_part(tops, pos, velocity):
    in_vmem = pl.BlockSpec(memory_space=pltpu.VMEM)
    return pl.pallas_call(
        move_kernel,
        in_specs=[in_vmem] * (len(tops) + 2),
        out_specs=in_vmem,
        out_shape=jax.ShapeDtypeStruct(pos.shape, F32),
        compiler_params=pltpu.CompilerParams(vmem_limit_bytes=8 * 2**20),
        name="move",
    )(*tops, pos, velocity)


def neighbours(low, high, axis):
    size = lax.axis_size(axis)
    up = [(i, (i + 1) % size) for i in range(size)]
    down = [(b, a) for a, b in up]
    return lax.ppermute(high, axis, up), lax.ppermute(low, axis, down)


def rotations(outer, inner, along_outer):
    size = outer if along_outer else inner
    for turn in range(1, size):
        yield [
            (
                a * inner + b,
                (a + turn) % outer * inner + b if along_outer else a * inner + (b + turn) % inner,
            )
            for a in range(outer)
            for b in range(inner)
        ]


def over_all(value):
    values = [value]
    for axis, inner in (("cy", 2), ("cx", 4)):
        outer = lax.axis_size(axis) // inner
        for along_outer in (False, True):
            value = functools.reduce(jnp.maximum, values)
            values = [value] + [
                lax.ppermute(value, axis, pairs)
                for pairs in rotations(outer, inner, along_outer)
            ]
    return values


def body(
    cell_pos,
    cell_drag,
    cell_near,
    analysis,
    stiffness,
    synthesis,
    wall_pos,
    wall_normal,
    wall_weight,
    density,
    patch_near,
    cell_to_patch,
):
    rows, cols = cell_pos.shape[:2]
    all_rows = rows * lax.axis_size("cx")
    all_cols = cols * lax.axis_size("cy")
    first_row = lax.axis_index("cx") * rows
    first_col = lax.axis_index("cy") * cols

    pos = jnp.transpose(cell_pos, (0, 2, 1, 3))
    walls = [jnp.transpose(v, (1, 0, 2)) for v in (wall_pos, wall_normal, density)]
    packed = jnp.concatenate(walls + [wall_weight[None]], axis=0)

    below, above = neighbours(pos, pos, "cx")
    inner_left, inner_right = neighbours(pos[:, :, :HALO], pos[:, :, cols - HALO :], "cy")
    below, above, later = lax.optimization_barrier((below, above, packed))
    wall_below, wall_above = neighbours(later, later, AXES)
    outer = [
        jnp.concatenate([v[:, :, c : c + HALO] for v in (below[rows - HALO :], above[:HALO])])
        for c in (0, cols - HALO)
    ]
    outer_left, outer_right = neighbours(*outer, "cy")

    patches = wall_pos.shape[0]
    all_patches = patches * lax.axis_size(AXES)
    start = lax.axis_index(AXES) * patches
    listed = (patch_near - start + patches) % all_patches
    layer, lefts, features = layer_part(layer_first, later)

    def code(cell):
        row = (cell // all_cols - first_row + HALO) % all_rows
        col = (cell % all_cols - first_col + HALO) % all_cols
        return (row * 16 + col).reshape(-1)

    near_code, layer = lax.optimization_barrier((code(cell_near), layer))
    velocity, top, wall_raw = near_part(
        near_code,
        code(cell_to_patch),
        below,
        pos,
        above,
        (inner_left, outer_left),
        (inner_right, outer_right),
        cell_drag.reshape(-1, 1),
        (analysis, stiffness[None, :], synthesis),
    )
    top, listed = lax.optimization_barrier((top, listed))
    tops = over_all(top)
    [density_next] = layer_part(
        layer_second, packed, wall_below, wall_above, lefts, features, layer, listed=listed
    )
    per = cell_to_patch.shape[1]
    for stage in range(per):
        density_next = wall_part(stage, per, wall_raw, walls[0], density_next)
    moved = move_part(tops, pos, velocity)
    return jnp.transpose(moved, (0, 2, 1, 3)), jnp.transpose(density_next, (1, 0, 2))


def solution(mesh):
    patch = P(AXES, None, None)
    return jax.shard_map(
        body,
        mesh=mesh,
        in_specs=(
            P("cx", "cy", None, None),
            P("cx", "cy"),
            P("cx", "cy", None),
            P(),
            P(),
            P(),
            patch,
            patch,
            P(AXES, None),
            patch,
            P(AXES, None),
            P(AXES, None),
        ),
        out_specs=(P("cx", "cy", None, None), patch),
        check_vma=False,
    )
```

```python
import functools
import math

import jax
import jax.numpy as jnp
from jax import lax
from jax.experimental import pallas as pl
from jax.experimental.pallas import tpu as pltpu
from jax.sharding import PartitionSpec as P

HALO = 3
AXES = ("cx", "cy")
SOFT = 0.25
STOKES_SCALE = 1.0 / (8.0 * math.pi)
LAYER_SCALE = 3.0 / (4.0 * math.pi)
F32 = jnp.float32
BF16 = jnp.bfloat16
LANES = 128

GROUPS = ((0, 0), (0, 1), (1, 0), (0, 2), (2, 0), (1, 1), (1, 2), (2, 1))
STOKES_ROWS = 24
LAYER_ROWS = 32
TARGET_ROWS = 24


def parts(v):
    high = v.astype(BF16)
    rest = v - high.astype(F32)
    middle = rest.astype(BF16)
    low = (rest - middle.astype(F32)).astype(BF16)
    return high, middle, low


def target_rows(raw):
    split = [p.astype(F32) for p in parts(raw)]
    return jnp.concatenate([split[a] for a, _ in GROUPS], axis=0).astype(BF16)


def source_rows(raw):
    split = [p.astype(F32) for p in parts(raw)]
    return jnp.concatenate([split[b] for _, b in GROUPS], axis=0).astype(BF16)


def product(left, right):
    return lax.dot_general(left, right, (((0,), (0,)), ((), ())), preferred_element_type=F32)


def feature_rows(raw):
    return jnp.concatenate(parts(raw), axis=0)


def put_rows(ref, first, count, stride, value):
    for tile in range(ref.shape[0]):
        ref[tile, pl.ds(first, count, stride=stride), :] = value[
            :, tile * LANES : (tile + 1) * LANES
        ]


def get_rows(ref, first, count):
    return jnp.concatenate(
        [ref[tile, pl.ds(first, count), :] for tile in range(ref.shape[0])], axis=1
    )


def stokes_raw(ref, first, pos, force):
    square = pos[0] * pos[0] + pos[1] * pos[1] + pos[2] * pos[2]
    along = pos[0] * force[0] + pos[1] * force[1] + pos[2] * force[2]
    rows = [-2.0 * pos[0], -2.0 * pos[1], -2.0 * pos[2], square, jnp.ones_like(square)]
    rows += [jnp.zeros_like(square)] * 3
    rows += [force[0], force[1], force[2]]
    rows += [pos[j] * force[i] for j in range(3) for i in range(3)]
    rows += [square * force[i] + pos[i] * along for i in range(3)]
    rows += [jnp.zeros_like(square)]
    for k, row in enumerate(rows):
        put_rows(ref, first + k, 8, STOKES_ROWS, row)


def target_raw(ref, first, pos, stride=8):
    square = pos[0] * pos[0] + pos[1] * pos[1] + pos[2] * pos[2] + SOFT
    rows = [pos[0], pos[1], pos[2], jnp.ones_like(square), square]
    rows += [jnp.zeros_like(square)] * 3
    for k, row in enumerate(rows):
        put_rows(ref, first + k, 8, stride, row)


def weighted(features, factor):
    return lax.dot_general(
        features, factor, (((1,), (1,)), ((), ())), preferred_element_type=F32
    )


def stokes_moments(raw_ref, slots, target):
    total = None
    for slot in slots:
        base = pl.multiple_of(slot * STOKES_ROWS, 8)
        left = source_rows(get_rows(raw_ref, base, 8))
        targets_first = target.shape[1] < left.shape[1]
        square = product(target, left) if targets_first else product(left, target)
        root = lax.rsqrt(jnp.maximum(square, SOFT))
        factor = (root * root * root).astype(BF16)
        features = feature_rows(get_rows(raw_ref, base + 8, 16))
        if targets_first:
            part = weighted(features, factor)
        else:
            part = jnp.dot(features, factor, preferred_element_type=F32)
        total = part if total is None else total + part
    return total[0:16] + total[16:32] + total[32:48]


def stokes_finish(pos, moments):
    m0 = moments[0:3]
    m1 = [[moments[3 + 3 * j + i] for i in range(3)] for j in range(3)]
    m2 = moments[12:15]
    square = pos[0] * pos[0] + pos[1] * pos[1] + pos[2] * pos[2] + 2.0 * SOFT
    along = pos[0] * m0[0] + pos[1] * m0[1] + pos[2] * m0[2]
    along = along - (m1[0][0] + m1[1][1] + m1[2][2])
    out = []
    for i in range(3):
        cross = sum(pos[j] * (2.0 * m1[j][i] + m1[i][j]) for j in range(3))
        out.append(square * m0[i] + m2[i] + pos[i] * along - cross)
    return out


def near_kernel(
    near_ref,
    wall_ref,
    below_ref,
    own_ref,
    above_ref,
    left_ref,
    left_outer_ref,
    right_ref,
    right_outer_ref,
    drag_ref,
    analysis_ref,
    stiffness_ref,
    synthesis_ref,
    velocity_ref,
    top_ref,
    wall_raw_ref,
    ext_ref,
    pos_ref,
    raw_ref,
    target_ref,
    moment_ref,
):
    rows, _, cols, points = own_ref.shape
    own = rows * cols
    near = near_ref.shape[0]
    wall = wall_ref.shape[0]
    slots = own + near + wall
    columns = (
        (slice(0, HALO), left_outer_ref, 0, left_ref, left_outer_ref, HALO),
        (slice(HALO, HALO + cols), below_ref, rows - HALO, own_ref, above_ref, 0),
        (slice(HALO + cols, cols + 2 * HALO), right_outer_ref, 0, right_ref, right_outer_ref, HALO),
    )
    for where, before, low, beside, after, high in columns:
        ext_ref[0:HALO, :, where, :] = before[low : low + HALO]
        ext_ref[HALO : HALO + rows, :, where, :] = beside[...]
        ext_ref[HALO + rows :, :, where, :] = after[high : high + HALO]
    for r in range(rows):
        for d in range(3):
            pos_ref[d, r * cols : (r + 1) * cols, :] = own_ref[r, d]
    for i in range(near + wall):
        code = near_ref[i] if i < near else wall_ref[i - near]
        row = code // 16
        col = code % 16
        for d in range(3):
            pos_ref[d, own + i : own + i + 1, :] = ext_ref[row, d, pl.ds(col, 1), :]
    everything = [pos_ref[d] for d in range(3)]
    centred = [v - jnp.sum(v, axis=1, keepdims=True) * (1.0 / points) for v in everything]
    flat = jnp.concatenate(centred, axis=0).astype(BF16)
    coeff = jnp.dot(flat, analysis_ref[...], preferred_element_type=F32)
    scaled = (coeff * stiffness_ref[...]).astype(BF16)
    force = -jnp.dot(scaled, synthesis_ref[...], preferred_element_type=F32)
    forces = [force[d * slots : (d + 1) * slots] for d in range(3)]
    for g in range((near + wall) // 8):
        a = own + 8 * g
        into, base = (raw_ref, 8 * g) if 8 * g < near else (wall_raw_ref, 8 * g - near)
        stokes_raw(
            into,
            base * STOKES_ROWS,
            [v[a : a + 8] for v in everything],
            [v[a : a + 8] for v in forces],
        )
    for g in range(own // 8):
        target_raw(target_ref, 64 * g, [v[8 * g : 8 * g + 8] for v in everything])

    def cell(c, carry):
        target = target_rows(get_rows(target_ref, pl.multiple_of(c * 8, 8), 8))
        per = near // own
        moments = stokes_moments(raw_ref, [c * per + k for k in range(per)], target)
        put_rows(moment_ref, c, 16, own, moments)
        return carry

    lax.fori_loop(0, own, cell, 0, unroll=4)
    moments = [get_rows(moment_ref, k * own, own) for k in range(15)]
    own_pos = [v[0:own] for v in everything]
    sums = stokes_finish(own_pos, moments)
    speed = jnp.zeros_like(sums[0])
    for d in range(3):
        velocity = drag_ref[...] * forces[d][0:own] + STOKES_SCALE * sums[d]
        speed = speed + velocity * velocity
        for r in range(rows):
            velocity_ref[r, d] = velocity[r * cols : (r + 1) * cols]
    top = jnp.sqrt(jnp.max(speed, axis=(0, 1), keepdims=True))
    top_ref[...] = jnp.broadcast_to(top, top_ref.shape)


def near_part(near_code, wall_code, below, pos, above, left, right, drag, tables):
    rows, _, cols, points = pos.shape
    own = rows * cols
    near, wall = near_code.shape[0], wall_code.shape[0]
    slots = own + near + wall
    tiles = points // LANES
    in_vmem = pl.BlockSpec(memory_space=pltpu.VMEM)
    in_smem = pl.BlockSpec(memory_space=pltpu.SMEM)
    pairs = own * points * (near // own) * points
    return pl.pallas_call(
        near_kernel,
        in_specs=[in_smem] * 2 + [in_vmem] * 11,
        out_specs=[in_vmem] * 3,
        out_shape=[
            jax.ShapeDtypeStruct((rows, 3, cols, points), F32),
            jax.ShapeDtypeStruct((8, LANES), F32),
            jax.ShapeDtypeStruct((tiles, wall * STOKES_ROWS, LANES), F32),
        ],
        scratch_shapes=[
            pltpu.VMEM((rows + 2 * HALO, 3, cols + 2 * HALO, points), F32),
            pltpu.VMEM((3, slots, points), F32),
            pltpu.VMEM((tiles, near * STOKES_ROWS, LANES), F32),
            pltpu.VMEM((tiles, own * 8, LANES), F32),
            pltpu.VMEM((tiles, own * 16, LANES), F32),
        ],
        compiler_params=pltpu.CompilerParams(vmem_limit_bytes=32 * 2**20),
        cost_estimate=pl.CostEstimate(
            flops=1000 * pairs, bytes_accessed=8 * 2**20, transcendentals=pairs
        ),
        name="near",
    )(near_code, wall_code, below, pos, above, *left, *right, drag, *tables)


def wall_kernel(stage, per, raw_ref, pos_ref, layer_ref, out_ref, target_ref, moment_ref):
    patches = pos_ref.shape[1]
    pos = [pos_ref[d] for d in range(3)]
    target_raw(target_ref, 0, pos)

    def patch(p, carry):
        target = target_rows(get_rows(target_ref, pl.multiple_of(p * 8, 8), 8))
        moments = stokes_moments(raw_ref, [p * per + stage], target)
        put_rows(moment_ref, p, 16, patches, moments)
        return carry

    lax.fori_loop(0, patches, patch, 0, unroll=True)
    sums = stokes_finish(pos, [get_rows(moment_ref, k * patches, patches) for k in range(15)])
    for d in range(3):
        out_ref[d] = layer_ref[d] + (2.0 * STOKES_SCALE) * sums[d]


def wall_part(stage, per, raw, pos, layer):
    _, patches, points = pos.shape
    tiles = points // LANES
    in_vmem = pl.BlockSpec(memory_space=pltpu.VMEM)
    pairs = patches * raw.shape[0] * LANES * points
    return pl.pallas_call(
        functools.partial(wall_kernel, stage, per),
        in_specs=[in_vmem] * 3,
        out_specs=in_vmem,
        out_shape=jax.ShapeDtypeStruct(pos.shape, F32),
        scratch_shapes=[
            pltpu.VMEM((tiles, patches * 8, LANES), F32),
            pltpu.VMEM((tiles, patches * 16, LANES), F32),
        ],
        compiler_params=pltpu.CompilerParams(vmem_limit_bytes=24 * 2**20),
        cost_estimate=pl.CostEstimate(
            flops=1000 * pairs, bytes_accessed=2 * 2**20, transcendentals=pairs
        ),
        name=f"wall_{stage}",
    )(raw, pos, layer)


def layer_sums(sources, own_ref, left_ref, feature_ref, target_ref, moment_ref):
    patches = own_ref.shape[1]
    x = [own_ref[d] for d in range(3)]
    target_raw(target_ref, 0, x, TARGET_ROWS)
    rows = [x[0] * x[0], x[1] * x[1], x[2] * x[2], x[0] * x[1], x[0] * x[2], x[1] * x[2]]
    rows += x + [jnp.ones_like(x[0])] + [jnp.zeros_like(x[0])] * 6
    for k, row in enumerate(rows):
        put_rows(target_ref, 8 + k, patches, TARGET_ROWS, row)

    def patch(p, carry):
        raw = get_rows(target_ref, pl.multiple_of(p * TARGET_ROWS, 8), TARGET_ROWS)
        near, form = target_rows(raw[0:8]), target_rows(raw[8:24])
        total = None
        for s in sources(p):
            square = product(near, left_ref[s, 0:64])
            scalar = product(form, left_ref[s, 64:192])
            root = lax.rsqrt(jnp.maximum(square, SOFT))
            double = root * root
            scalar = (scalar * (double * double * root)).astype(BF16)
            part = weighted(feature_ref[s], scalar)
            total = part if total is None else total + part
        moments = total[0:8] + total[8:16] + total[16:24]
        put_rows(moment_ref, p, 8, patches, moments)
        return carry

    lax.fori_loop(0, patches, patch, 0, unroll=True)
    moments = [get_rows(moment_ref, k * patches, patches) for k in range(4)]
    return [(-2.0 * LAYER_SCALE) * (x[d] * moments[3] - moments[d]) for d in range(3)]


def layer_prepare(blocks, left_ref, feature_ref, raw_ref):
    patches = blocks[0][0].shape[1]
    for block, (ref, _) in enumerate(blocks):
        y = [ref[d] for d in range(3)]
        n = [ref[3 + d] for d in range(3)]
        v = [ref[6 + d] * ref[9] for d in range(3)]
        square = y[0] * y[0] + y[1] * y[1] + y[2] * y[2]
        along_n = y[0] * n[0] + y[1] * n[1] + y[2] * n[2]
        along_v = y[0] * v[0] + y[1] * v[1] + y[2] * v[2]
        one, zero = jnp.ones_like(square), jnp.zeros_like(square)
        rows = [-2.0 * y[0], -2.0 * y[1], -2.0 * y[2], square, one, zero, zero, zero]
        rows += [v[d] * n[d] for d in range(3)]
        rows += [v[a] * n[b] + v[b] * n[a] for a, b in ((0, 1), (0, 2), (1, 2))]
        rows += [-(v[d] * along_n + n[d] * along_v) for d in range(3)]
        rows += [along_v * along_n] + [zero] * 6
        rows += [y[0], y[1], y[2], one, zero, zero, zero, zero]
        for k, row in enumerate(rows):
            put_rows(raw_ref, block * patches * LAYER_ROWS + k, patches, LAYER_ROWS, row)

    for block, (_, first) in enumerate(blocks):

        def prepare(i, carry, block=block, first=first):
            base = (block * patches + i) * LAYER_ROWS
            raw = get_rows(raw_ref, pl.multiple_of(base, 8), LAYER_ROWS)
            left_ref[first + i, 0:64] = source_rows(raw[0:8])
            left_ref[first + i, 64:192] = source_rows(raw[8:24])
            split = [p.astype(F32) for p in parts(raw[24:32])]
            split.append(jnp.zeros_like(split[0]))
            feature_ref[first + i] = jnp.concatenate(split, axis=0).astype(BF16)
            return carry

        lax.fori_loop(0, patches, prepare, 0, unroll=4)


def layer_first(own_ref, out_ref, left_ref, feature_ref, raw_ref, target_ref, moment_ref):
    layer_prepare([(own_ref, 0)], left_ref, feature_ref, raw_ref)
    sums = layer_sums(lambda p: [p], own_ref, left_ref, feature_ref, target_ref, moment_ref)
    for d in range(3):
        out_ref[d] = sums[d]


def layer_second(
    listed_ref,
    own_ref,
    before_ref,
    after_ref,
    own_left_ref,
    own_feature_ref,
    so_far_ref,
    out_ref,
    left_ref,
    feature_ref,
    raw_ref,
    target_ref,
    moment_ref,
):
    patches = own_ref.shape[1]
    left_ref[patches : 2 * patches] = own_left_ref[...]
    feature_ref[patches : 2 * patches] = own_feature_ref[...]
    blocks = [(before_ref, 0), (after_ref, 2 * patches)]
    layer_prepare(blocks, left_ref, feature_ref, raw_ref)
    count = listed_ref.shape[1]
    sums = layer_sums(
        lambda p: [listed_ref[p, k] for k in range(count)],
        own_ref,
        left_ref,
        feature_ref,
        target_ref,
        moment_ref,
    )
    for d in range(3):
        out_ref[d] = so_far_ref[d] + sums[d]


def layer_part(kernel, *arrays, listed=None):
    _, patches, points = arrays[0].shape
    tiles = points // LANES
    in_vmem = pl.BlockSpec(memory_space=pltpu.VMEM)
    in_smem = pl.BlockSpec(memory_space=pltpu.SMEM)
    out_shape = [jax.ShapeDtypeStruct((3, patches, points), F32)]
    blocks, sources = (2, listed.shape[1]) if listed is not None else (1, 1)
    scratch = [
        pltpu.VMEM((tiles, blocks * patches * LAYER_ROWS, LANES), F32),
        pltpu.VMEM((tiles, patches * TARGET_ROWS, LANES), F32),
        pltpu.VMEM((tiles, patches * 8, LANES), F32),
    ]
    if listed is None:
        sides = (patches, 192, points), (patches, 32, points)
        out_shape += [jax.ShapeDtypeStruct(side, BF16) for side in sides]
        scalars = ()
    else:
        sides = (3 * patches, 192, points), (3 * patches, 32, points)
        scratch = [pltpu.VMEM(side, BF16) for side in sides] + scratch
        scalars = (listed,)
    pairs = patches * points * sources * points
    return pl.pallas_call(
        kernel,
        in_specs=[in_smem] * len(scalars) + [in_vmem] * len(arrays),
        out_specs=[in_vmem] * len(out_shape),
        out_shape=out_shape,
        scratch_shapes=scratch,
        compiler_params=pltpu.CompilerParams(vmem_limit_bytes=24 * 2**20),
        cost_estimate=pl.CostEstimate(
            flops=1000 * pairs, bytes_accessed=2**20, transcendentals=pairs
        ),
        name=kernel.__name__,
    )(*scalars, *arrays)


def move_kernel(*refs):
    *tops, pos_ref, velocity_ref, out_ref = refs
    top = functools.reduce(jnp.maximum, [t[...] for t in tops])
    step = 1.0 / (top[0:1, 0:1] + 1e-06)
    rows, _, cols, _ = pos_ref.shape
    for r in range(rows):
        for d in range(3):
            out_ref[r, d] = pos_ref[r, d] + step * velocity_ref[r, d]


def move_part(tops, pos, velocity):
    in_vmem = pl.BlockSpec(memory_space=pltpu.VMEM)
    return pl.pallas_call(
        move_kernel,
        in_specs=[in_vmem] * (len(tops) + 2),
        out_specs=in_vmem,
        out_shape=jax.ShapeDtypeStruct(pos.shape, F32),
        compiler_params=pltpu.CompilerParams(vmem_limit_bytes=8 * 2**20),
        name="move",
    )(*tops, pos, velocity)


def neighbours(low, high, axis):
    size = lax.axis_size(axis)
    up = [(i, (i + 1) % size) for i in range(size)]
    down = [(b, a) for a, b in up]
    return lax.ppermute(high, axis, up), lax.ppermute(low, axis, down)


def rotations(outer, inner, along_outer):
    size = outer if along_outer else inner
    for turn in range(1, size):
        yield [
            (
                a * inner + b,
                (a + turn) % outer * inner + b if along_outer else a * inner + (b + turn) % inner,
            )
            for a in range(outer)
            for b in range(inner)
        ]


def over_all(value):
    values = [value]
    for axis, inner in (("cy", 2), ("cx", 4)):
        outer = lax.axis_size(axis) // inner
        for along_outer in (False, True):
            value = functools.reduce(jnp.maximum, values)
            values = [value] + [
                lax.ppermute(value, axis, pairs)
                for pairs in rotations(outer, inner, along_outer)
            ]
    return values


def body(
    cell_pos,
    cell_drag,
    cell_near,
    analysis,
    stiffness,
    synthesis,
    wall_pos,
    wall_normal,
    wall_weight,
    density,
    patch_near,
    cell_to_patch,
):
    rows, cols = cell_pos.shape[:2]
    all_rows = rows * lax.axis_size("cx")
    all_cols = cols * lax.axis_size("cy")
    first_row = lax.axis_index("cx") * rows
    first_col = lax.axis_index("cy") * cols

    pos = jnp.transpose(cell_pos, (0, 2, 1, 3))
    walls = [jnp.transpose(v, (1, 0, 2)) for v in (wall_pos, wall_normal, density)]
    packed = jnp.concatenate(walls + [wall_weight[None]], axis=0)

    below, above = neighbours(pos, pos, "cx")
    inner_left, inner_right = neighbours(pos[:, :, :HALO], pos[:, :, cols - HALO :], "cy")
    below, above, later = lax.optimization_barrier((below, above, packed))
    wall_below, wall_above = neighbours(later, later, AXES)
    outer = [
        jnp.concatenate([v[:, :, c : c + HALO] for v in (below[rows - HALO :], above[:HALO])])
        for c in (0, cols - HALO)
    ]
    outer_left, outer_right = neighbours(*outer, "cy")

    patches = wall_pos.shape[0]
    all_patches = patches * lax.axis_size(AXES)
    start = lax.axis_index(AXES) * patches
    listed = (patch_near - start + patches) % all_patches
    layer, lefts, features = layer_part(layer_first, later)

    def code(cell):
        row = (cell // all_cols - first_row + HALO) % all_rows
        col = (cell % all_cols - first_col + HALO) % all_cols
        return (row * 16 + col).reshape(-1)

    near_code, layer = lax.optimization_barrier((code(cell_near), layer))
    velocity, top, wall_raw = near_part(
        near_code,
        code(cell_to_patch),
        below,
        pos,
        above,
        (inner_left, outer_left),
        (inner_right, outer_right),
        cell_drag.reshape(-1, 1),
        (analysis, stiffness[None, :], synthesis),
    )
    top, listed = lax.optimization_barrier((top, listed))
    tops = over_all(top)
    [density_next] = layer_part(
        layer_second, packed, wall_below, wall_above, lefts, features, layer, listed=listed
    )
    per = cell_to_patch.shape[1]
    for stage in range(per):
        density_next = wall_part(stage, per, wall_raw, walls[0], density_next)
    moved = move_part(tops, pos, velocity)
    return jnp.transpose(moved, (0, 2, 1, 3)), jnp.transpose(density_next, (1, 0, 2))


def solution(mesh):
    patch = P(AXES, None, None)
    return jax.shard_map(
        body,
        mesh=mesh,
        in_specs=(
            P("cx", "cy", None, None),
            P("cx", "cy"),
            P("cx", "cy", None),
            P(),
            P(),
            P(),
            patch,
            patch,
            P(AXES, None),
            patch,
            P(AXES, None),
            P(AXES, None),
        ),
        out_specs=(P("cx", "cy", None, None), patch),
        check_vma=False,
    )
```

```python
import functools
import math

import jax
import jax.numpy as jnp
from jax import lax
from jax.experimental import pallas as pl
from jax.experimental.pallas import tpu as pltpu
from jax.sharding import PartitionSpec as P

HALO = 3
AXES = ("cx", "cy")
SOFT = 0.25
STOKES_SCALE = 1.0 / (8.0 * math.pi)
LAYER_SCALE = 3.0 / (4.0 * math.pi)
F32 = jnp.float32
BF16 = jnp.bfloat16
LANES = 128

GROUPS = ((0, 0), (0, 1), (1, 0), (0, 2), (2, 0), (1, 1), (1, 2), (2, 1))
STOKES_ROWS = 24
LAYER_ROWS = 32
TARGET_ROWS = 24


def parts(v):
    high = v.astype(BF16)
    rest = v - high.astype(F32)
    middle = rest.astype(BF16)
    low = (rest - middle.astype(F32)).astype(BF16)
    return high, middle, low


def target_rows(raw):
    split = [p.astype(F32) for p in parts(raw)]
    return jnp.concatenate([split[a] for a, _ in GROUPS], axis=0).astype(BF16)


def source_rows(raw):
    split = [p.astype(F32) for p in parts(raw)]
    return jnp.concatenate([split[b] for _, b in GROUPS], axis=0).astype(BF16)


def product(left, right):
    return lax.dot_general(left, right, (((0,), (0,)), ((), ())), preferred_element_type=F32)


def feature_rows(raw):
    return jnp.concatenate(parts(raw), axis=0)


def put_rows(ref, first, count, stride, value):
    for tile in range(ref.shape[0]):
        ref[tile, pl.ds(first, count, stride=stride), :] = value[
            :, tile * LANES : (tile + 1) * LANES
        ]


def get_rows(ref, first, count):
    return jnp.concatenate(
        [ref[tile, pl.ds(first, count), :] for tile in range(ref.shape[0])], axis=1
    )


def stokes_raw(ref, first, pos, force):
    square = pos[0] * pos[0] + pos[1] * pos[1] + pos[2] * pos[2]
    along = pos[0] * force[0] + pos[1] * force[1] + pos[2] * force[2]
    rows = [-2.0 * pos[0], -2.0 * pos[1], -2.0 * pos[2], square, jnp.ones_like(square)]
    rows += [jnp.zeros_like(square)] * 3
    rows += [force[0], force[1], force[2]]
    rows += [pos[j] * force[i] for j in range(3) for i in range(3)]
    rows += [square * force[i] + pos[i] * along for i in range(3)]
    rows += [jnp.zeros_like(square)]
    for k, row in enumerate(rows):
        put_rows(ref, first + k, 8, STOKES_ROWS, row)


def target_raw(ref, first, pos, stride=8):
    square = pos[0] * pos[0] + pos[1] * pos[1] + pos[2] * pos[2] + SOFT
    rows = [pos[0], pos[1], pos[2], jnp.ones_like(square), square]
    rows += [jnp.zeros_like(square)] * 3
    for k, row in enumerate(rows):
        put_rows(ref, first + k, 8, stride, row)


def weighted(features, factor):
    return lax.dot_general(
        features, factor, (((1,), (1,)), ((), ())), preferred_element_type=F32
    )


def stokes_moments(raw_ref, slots, target):
    total = None
    for slot in slots:
        base = pl.multiple_of(slot * STOKES_ROWS, 8)
        left = source_rows(get_rows(raw_ref, base, 8))
        targets_first = target.shape[1] < left.shape[1]
        square = product(target, left) if targets_first else product(left, target)
        root = lax.rsqrt(jnp.maximum(square, SOFT))
        factor = (root * root * root).astype(BF16)
        features = feature_rows(get_rows(raw_ref, base + 8, 16))
        if targets_first:
            part = weighted(features, factor)
        else:
            part = jnp.dot(features, factor, preferred_element_type=F32)
        total = part if total is None else total + part
    return total[0:16] + total[16:32] + total[32:48]


def stokes_finish(pos, moments):
    m0 = moments[0:3]
    m1 = [[moments[3 + 3 * j + i] for i in range(3)] for j in range(3)]
    m2 = moments[12:15]
    square = pos[0] * pos[0] + pos[1] * pos[1] + pos[2] * pos[2] + 2.0 * SOFT
    along = pos[0] * m0[0] + pos[1] * m0[1] + pos[2] * m0[2]
    along = along - (m1[0][0] + m1[1][1] + m1[2][2])
    out = []
    for i in range(3):
        cross = sum(pos[j] * (2.0 * m1[j][i] + m1[i][j]) for j in range(3))
        out.append(square * m0[i] + m2[i] + pos[i] * along - cross)
    return out


def near_kernel(
    near_ref,
    wall_ref,
    below_ref,
    own_ref,
    above_ref,
    left_ref,
    left_outer_ref,
    right_ref,
    right_outer_ref,
    drag_ref,
    analysis_ref,
    stiffness_ref,
    synthesis_ref,
    velocity_ref,
    top_ref,
    wall_raw_ref,
    ext_ref,
    pos_ref,
    raw_ref,
    target_ref,
    moment_ref,
    first_ref,
    second_ref,
    sems,
):
    tables = [
        pltpu.make_async_copy(a, b, sems.at[k])
        for k, (a, b) in enumerate(((analysis_ref, first_ref), (synthesis_ref, second_ref)))
    ]
    for table in tables:
        table.start()
    rows, _, cols, points = own_ref.shape
    own = rows * cols
    near = near_ref.shape[0]
    wall = wall_ref.shape[0]
    slots = own + near + wall
    columns = (
        (slice(0, HALO), left_outer_ref, 0, left_ref, left_outer_ref, HALO),
        (slice(HALO, HALO + cols), below_ref, rows - HALO, own_ref, above_ref, 0),
        (slice(HALO + cols, cols + 2 * HALO), right_outer_ref, 0, right_ref, right_outer_ref, HALO),
    )
    for where, before, low, beside, after, high in columns:
        ext_ref[0:HALO, :, where, :] = before[low : low + HALO]
        ext_ref[HALO : HALO + rows, :, where, :] = beside[...]
        ext_ref[HALO + rows :, :, where, :] = after[high : high + HALO]
    for r in range(rows):
        for d in range(3):
            pos_ref[d, r * cols : (r + 1) * cols, :] = own_ref[r, d]
    for i in range(near + wall):
        code = near_ref[i] if i < near else wall_ref[i - near]
        row = code // 16
        col = code % 16
        for d in range(3):
            pos_ref[d, own + i : own + i + 1, :] = ext_ref[row, d, pl.ds(col, 1), :]
    everything = [pos_ref[d] for d in range(3)]
    centred = [v - jnp.sum(v, axis=1, keepdims=True) * (1.0 / points) for v in everything]
    flat = jnp.concatenate(centred, axis=0).astype(BF16)
    tables[0].wait()
    coeff = jnp.dot(flat, first_ref[...], preferred_element_type=F32)
    scaled = (coeff * stiffness_ref[...]).astype(BF16)
    tables[1].wait()
    force = -jnp.dot(scaled, second_ref[...], preferred_element_type=F32)
    forces = [force[d * slots : (d + 1) * slots] for d in range(3)]
    for g in range((near + wall) // 8):
        a = own + 8 * g
        into, base = (raw_ref, 8 * g) if 8 * g < near else (wall_raw_ref, 8 * g - near)
        stokes_raw(
            into,
            base * STOKES_ROWS,
            [v[a : a + 8] for v in everything],
            [v[a : a + 8] for v in forces],
        )
    for g in range(own // 8):
        target_raw(target_ref, 64 * g, [v[8 * g : 8 * g + 8] for v in everything])

    def cell(c, carry):
        target = target_rows(get_rows(target_ref, pl.multiple_of(c * 8, 8), 8))
        per = near // own
        moments = stokes_moments(raw_ref, [c * per + k for k in range(per)], target)
        put_rows(moment_ref, c, 16, own, moments)
        return carry

    lax.fori_loop(0, own, cell, 0, unroll=4)
    moments = [get_rows(moment_ref, k * own, own) for k in range(15)]
    own_pos = [v[0:own] for v in everything]
    sums = stokes_finish(own_pos, moments)
    speed = jnp.zeros_like(sums[0])
    for d in range(3):
        velocity = drag_ref[...] * forces[d][0:own] + STOKES_SCALE * sums[d]
        speed = speed + velocity * velocity
        for r in range(rows):
            velocity_ref[r, d] = velocity[r * cols : (r + 1) * cols]
    top = jnp.sqrt(jnp.max(speed, axis=(0, 1), keepdims=True))
    top_ref[...] = jnp.broadcast_to(top, top_ref.shape)


def near_part(near_code, wall_code, below, pos, above, left, right, drag, tables):
    rows, _, cols, points = pos.shape
    own = rows * cols
    near, wall = near_code.shape[0], wall_code.shape[0]
    slots = own + near + wall
    tiles = points // LANES
    in_vmem = pl.BlockSpec(memory_space=pltpu.VMEM)
    in_smem = pl.BlockSpec(memory_space=pltpu.SMEM)
    in_hbm = pl.BlockSpec(memory_space=pl.ANY)
    pairs = own * points * (near // own) * points
    return pl.pallas_call(
        near_kernel,
        in_specs=[in_smem] * 2 + [in_vmem] * 8 + [in_hbm, in_vmem, in_hbm],
        out_specs=[in_vmem] * 3,
        out_shape=[
            jax.ShapeDtypeStruct((rows, 3, cols, points), F32),
            jax.ShapeDtypeStruct((8, LANES), F32),
            jax.ShapeDtypeStruct((tiles, wall * STOKES_ROWS, LANES), F32),
        ],
        scratch_shapes=[
            pltpu.VMEM((rows + 2 * HALO, 3, cols + 2 * HALO, points), F32),
            pltpu.VMEM((3, slots, points), F32),
            pltpu.VMEM((tiles, near * STOKES_ROWS, LANES), F32),
            pltpu.VMEM((tiles, own * 8, LANES), F32),
            pltpu.VMEM((tiles, own * 16, LANES), F32),
            pltpu.VMEM(tables[0].shape, BF16),
            pltpu.VMEM(tables[2].shape, BF16),
            pltpu.SemaphoreType.DMA((2,)),
        ],
        compiler_params=pltpu.CompilerParams(vmem_limit_bytes=50 * 2**20),
        cost_estimate=pl.CostEstimate(
            flops=1000 * pairs, bytes_accessed=8 * 2**20, transcendentals=pairs
        ),
        name="near",
    )(near_code, wall_code, below, pos, above, *left, *right, drag, *tables)


def wall_kernel(stage, per, raw_ref, pos_ref, layer_ref, out_ref, target_ref, moment_ref):
    patches = pos_ref.shape[1]
    pos = [pos_ref[d] for d in range(3)]
    target_raw(target_ref, 0, pos)

    def patch(p, carry):
        target = target_rows(get_rows(target_ref, pl.multiple_of(p * 8, 8), 8))
        moments = stokes_moments(raw_ref, [p * per + stage], target)
        put_rows(moment_ref, p, 16, patches, moments)
        return carry

    lax.fori_loop(0, patches, patch, 0, unroll=True)
    sums = stokes_finish(pos, [get_rows(moment_ref, k * patches, patches) for k in range(15)])
    for d in range(3):
        out_ref[d] = layer_ref[d] + (2.0 * STOKES_SCALE) * sums[d]


def wall_part(stage, per, raw, pos, layer):
    _, patches, points = pos.shape
    tiles = points // LANES
    in_vmem = pl.BlockSpec(memory_space=pltpu.VMEM)
    pairs = patches * raw.shape[0] * LANES * points
    return pl.pallas_call(
        functools.partial(wall_kernel, stage, per),
        in_specs=[in_vmem] * 3,
        out_specs=in_vmem,
        out_shape=jax.ShapeDtypeStruct(pos.shape, F32),
        scratch_shapes=[
            pltpu.VMEM((tiles, patches * 8, LANES), F32),
            pltpu.VMEM((tiles, patches * 16, LANES), F32),
        ],
        compiler_params=pltpu.CompilerParams(vmem_limit_bytes=24 * 2**20),
        cost_estimate=pl.CostEstimate(
            flops=1000 * pairs, bytes_accessed=2 * 2**20, transcendentals=pairs
        ),
        name=f"wall_{stage}",
    )(raw, pos, layer)


def layer_sums(sources, own_ref, left_ref, feature_ref, target_ref, moment_ref):
    patches = own_ref.shape[1]
    x = [own_ref[d] for d in range(3)]
    target_raw(target_ref, 0, x, TARGET_ROWS)
    rows = [x[0] * x[0], x[1] * x[1], x[2] * x[2], x[0] * x[1], x[0] * x[2], x[1] * x[2]]
    rows += x + [jnp.ones_like(x[0])] + [jnp.zeros_like(x[0])] * 6
    for k, row in enumerate(rows):
        put_rows(target_ref, 8 + k, patches, TARGET_ROWS, row)

    def patch(p, carry):
        raw = get_rows(target_ref, pl.multiple_of(p * TARGET_ROWS, 8), TARGET_ROWS)
        near, form = target_rows(raw[0:8]), target_rows(raw[8:24])
        total = None
        for s in sources(p):
            square = product(near, left_ref[s, 0:64])
            scalar = product(form, left_ref[s, 64:192])
            root = lax.rsqrt(jnp.maximum(square, SOFT))
            double = root * root
            scalar = (scalar * (double * double * root)).astype(BF16)
            part = weighted(feature_ref[s], scalar)
            total = part if total is None else total + part
        moments = total[0:8] + total[8:16] + total[16:24]
        put_rows(moment_ref, p, 8, patches, moments)
        return carry

    lax.fori_loop(0, patches, patch, 0, unroll=True)
    moments = [get_rows(moment_ref, k * patches, patches) for k in range(4)]
    return [(-2.0 * LAYER_SCALE) * (x[d] * moments[3] - moments[d]) for d in range(3)]


def layer_prepare(blocks, left_ref, feature_ref, raw_ref):
    patches = blocks[0][0].shape[1]
    for block, (ref, _) in enumerate(blocks):
        y = [ref[d] for d in range(3)]
        n = [ref[3 + d] for d in range(3)]
        v = [ref[6 + d] * ref[9] for d in range(3)]
        square = y[0] * y[0] + y[1] * y[1] + y[2] * y[2]
        along_n = y[0] * n[0] + y[1] * n[1] + y[2] * n[2]
        along_v = y[0] * v[0] + y[1] * v[1] + y[2] * v[2]
        one, zero = jnp.ones_like(square), jnp.zeros_like(square)
        rows = [-2.0 * y[0], -2.0 * y[1], -2.0 * y[2], square, one, zero, zero, zero]
        rows += [v[d] * n[d] for d in range(3)]
        rows += [v[a] * n[b] + v[b] * n[a] for a, b in ((0, 1), (0, 2), (1, 2))]
        rows += [-(v[d] * along_n + n[d] * along_v) for d in range(3)]
        rows += [along_v * along_n] + [zero] * 6
        rows += [y[0], y[1], y[2], one, zero, zero, zero, zero]
        for k, row in enumerate(rows):
            put_rows(raw_ref, block * patches * LAYER_ROWS + k, patches, LAYER_ROWS, row)

    for block, (_, first) in enumerate(blocks):

        def prepare(i, carry, block=block, first=first):
            base = (block * patches + i) * LAYER_ROWS
            raw = get_rows(raw_ref, pl.multiple_of(base, 8), LAYER_ROWS)
            left_ref[first + i, 0:64] = source_rows(raw[0:8])
            left_ref[first + i, 64:192] = source_rows(raw[8:24])
            split = [p.astype(F32) for p in parts(raw[24:32])]
            split.append(jnp.zeros_like(split[0]))
            feature_ref[first + i] = jnp.concatenate(split, axis=0).astype(BF16)
            return carry

        lax.fori_loop(0, patches, prepare, 0, unroll=True)


def layer_first(own_ref, out_ref, left_ref, feature_ref, raw_ref, target_ref, moment_ref):
    layer_prepare([(own_ref, 0)], left_ref, feature_ref, raw_ref)
    sums = layer_sums(lambda p: [p], own_ref, left_ref, feature_ref, target_ref, moment_ref)
    for d in range(3):
        out_ref[d] = sums[d]


def layer_second(
    listed_ref,
    own_ref,
    before_ref,
    after_ref,
    own_left_ref,
    own_feature_ref,
    so_far_ref,
    out_ref,
    left_ref,
    feature_ref,
    raw_ref,
    target_ref,
    moment_ref,
):
    patches = own_ref.shape[1]
    left_ref[patches : 2 * patches] = own_left_ref[...]
    feature_ref[patches : 2 * patches] = own_feature_ref[...]
    blocks = [(before_ref, 0), (after_ref, 2 * patches)]
    layer_prepare(blocks, left_ref, feature_ref, raw_ref)
    count = listed_ref.shape[1]
    sums = layer_sums(
        lambda p: [listed_ref[p, k] for k in range(count)],
        own_ref,
        left_ref,
        feature_ref,
        target_ref,
        moment_ref,
    )
    for d in range(3):
        out_ref[d] = so_far_ref[d] + sums[d]


def layer_part(kernel, *arrays, listed=None):
    _, patches, points = arrays[0].shape
    tiles = points // LANES
    in_vmem = pl.BlockSpec(memory_space=pltpu.VMEM)
    in_smem = pl.BlockSpec(memory_space=pltpu.SMEM)
    out_shape = [jax.ShapeDtypeStruct((3, patches, points), F32)]
    blocks, sources = (2, listed.shape[1]) if listed is not None else (1, 1)
    scratch = [
        pltpu.VMEM((tiles, blocks * patches * LAYER_ROWS, LANES), F32),
        pltpu.VMEM((tiles, patches * TARGET_ROWS, LANES), F32),
        pltpu.VMEM((tiles, patches * 8, LANES), F32),
    ]
    if listed is None:
        sides = (patches, 192, points), (patches, 32, points)
        out_shape += [jax.ShapeDtypeStruct(side, BF16) for side in sides]
        scalars = ()
    else:
        sides = (3 * patches, 192, points), (3 * patches, 32, points)
        scratch = [pltpu.VMEM(side, BF16) for side in sides] + scratch
        scalars = (listed,)
    pairs = patches * points * sources * points
    return pl.pallas_call(
        kernel,
        in_specs=[in_smem] * len(scalars) + [in_vmem] * len(arrays),
        out_specs=[in_vmem] * len(out_shape),
        out_shape=out_shape,
        scratch_shapes=scratch,
        compiler_params=pltpu.CompilerParams(vmem_limit_bytes=24 * 2**20),
        cost_estimate=pl.CostEstimate(
            flops=1000 * pairs, bytes_accessed=2**20, transcendentals=pairs
        ),
        name=kernel.__name__,
    )(*scalars, *arrays)


def move_kernel(*refs):
    *tops, pos_ref, velocity_ref, out_ref = refs
    top = functools.reduce(jnp.maximum, [t[...] for t in tops])
    step = 1.0 / (top[0:1, 0:1] + 1e-06)
    rows, _, cols, _ = pos_ref.shape
    for r in range(rows):
        for d in range(3):
            out_ref[r, d] = pos_ref[r, d] + step * velocity_ref[r, d]


def move_part(tops, pos, velocity):
    in_vmem = pl.BlockSpec(memory_space=pltpu.VMEM)
    return pl.pallas_call(
        move_kernel,
        in_specs=[in_vmem] * (len(tops) + 2),
        out_specs=in_vmem,
        out_shape=jax.ShapeDtypeStruct(pos.shape, F32),
        compiler_params=pltpu.CompilerParams(vmem_limit_bytes=8 * 2**20),
        name="move",
    )(*tops, pos, velocity)


def neighbours(low, high, axis):
    size = lax.axis_size(axis)
    up = [(i, (i + 1) % size) for i in range(size)]
    down = [(b, a) for a, b in up]
    return lax.ppermute(high, axis, up), lax.ppermute(low, axis, down)


def rotations(outer, inner, along_outer):
    size = outer if along_outer else inner
    for turn in range(1, size):
        yield [
            (
                a * inner + b,
                (a + turn) % outer * inner + b if along_outer else a * inner + (b + turn) % inner,
            )
            for a in range(outer)
            for b in range(inner)
        ]


def over_all(value):
    values = [value]
    for axis, inner in (("cy", 2), ("cx", 4)):
        outer = lax.axis_size(axis) // inner
        for along_outer in (False, True):
            value = functools.reduce(jnp.maximum, values)
            values = [value] + [
                lax.ppermute(value, axis, pairs)
                for pairs in rotations(outer, inner, along_outer)
            ]
    return values


def body(
    cell_pos,
    cell_drag,
    cell_near,
    analysis,
    stiffness,
    synthesis,
    wall_pos,
    wall_normal,
    wall_weight,
    density,
    patch_near,
    cell_to_patch,
):
    rows, cols = cell_pos.shape[:2]
    all_rows = rows * lax.axis_size("cx")
    all_cols = cols * lax.axis_size("cy")
    first_row = lax.axis_index("cx") * rows
    first_col = lax.axis_index("cy") * cols

    pos = jnp.transpose(cell_pos, (0, 2, 1, 3))
    walls = [jnp.transpose(v, (1, 0, 2)) for v in (wall_pos, wall_normal, density)]
    packed = jnp.concatenate(walls + [wall_weight[None]], axis=0)

    below, above = neighbours(pos, pos, "cx")
    inner_left, inner_right = neighbours(pos[:, :, :HALO], pos[:, :, cols - HALO :], "cy")
    below, above, later = lax.optimization_barrier((below, above, packed))
    wall_below, wall_above = neighbours(later, later, AXES)
    outer = [
        jnp.concatenate([v[:, :, c : c + HALO] for v in (below[rows - HALO :], above[:HALO])])
        for c in (0, cols - HALO)
    ]
    outer_left, outer_right = neighbours(*outer, "cy")

    patches = wall_pos.shape[0]
    all_patches = patches * lax.axis_size(AXES)
    start = lax.axis_index(AXES) * patches
    listed = (patch_near - start + patches) % all_patches
    layer, lefts, features = layer_part(layer_first, later)

    def code(cell):
        row = (cell // all_cols - first_row + HALO) % all_rows
        col = (cell % all_cols - first_col + HALO) % all_cols
        return (row * 16 + col).reshape(-1)

    near_code, layer = lax.optimization_barrier((code(cell_near), layer))
    velocity, top, wall_raw = near_part(
        near_code,
        code(cell_to_patch),
        below,
        pos,
        above,
        (inner_left, outer_left),
        (inner_right, outer_right),
        cell_drag.reshape(-1, 1),
        (analysis, stiffness[None, :], synthesis),
    )
    top, listed = lax.optimization_barrier((top, listed))
    tops = over_all(top)
    [density_next] = layer_part(
        layer_second, packed, wall_below, wall_above, lefts, features, layer, listed=listed
    )
    per = cell_to_patch.shape[1]
    for stage in range(per):
        density_next = wall_part(stage, per, wall_raw, walls[0], density_next)
    moved = move_part(tops, pos, velocity)
    return jnp.transpose(moved, (0, 2, 1, 3)), jnp.transpose(density_next, (1, 0, 2))


def solution(mesh):
    patch = P(AXES, None, None)
    return jax.shard_map(
        body,
        mesh=mesh,
        in_specs=(
            P("cx", "cy", None, None),
            P("cx", "cy"),
            P("cx", "cy", None),
            P(),
            P(),
            P(),
            patch,
            patch,
            P(AXES, None),
            patch,
            P(AXES, None),
            P(AXES, None),
        ),
        out_specs=(P("cx", "cy", None, None), patch),
        check_vma=False,
    )
```
